512 devices in a mesh: row: 8 (over y_lo, x), channel: 8 (over y_hi, core), sample: 8 (over z).
Axes of the slice: x: 4, y: 8 (y_hi: 4, y_lo: 2; y = y_hi * 2 + y_lo), z: 8, core: 2. Of those that a mesh axis runs over, the one named last changes fastest.
Arguments:
- features: bfloat16 [8, 48, 72, 2048], P('sample', 'row', None, 'channel'), may hold values from -6 to 6
- weights: bfloat16 [256, 3, 9, 2048], P('sample', None, None, 'channel'), may hold values from -0.046875 to 0.046875
- proj: bfloat16 [768, 256], replicated, may hold values from -0.21875 to 0.21875
- classify: bfloat16 [256, 3], replicated, may hold values from -0.375 to 0.375
- labels: int32 [8, 48, 72], P('sample', 'row'), may hold values from 0 to 2
Outputs:
- weight_grad: bfloat16 [256, 3, 9, 2048], P('sample', None, None, 'channel')
The draws below stay inside these ranges and needn't reach their ends.
All inputs are finite; a program needn't handle non-finite values.
Results may differ from the reference program's by a relative error of at most 0.03.
Values may be sent and summed in bfloat16 or wider, within the bound.
No kernel may reach another device: no remote copies, remote signals or barrier semaphores. Data moves between devices by JAX's collectives and lax.ppermute only.
A program may use at most 64 MiB of HBM per device.

```python
import jax
import jax.numpy as jnp
from jax import lax

C = 2048
O = 256
E = 256
CLASSES = 3
B_DEV = 1
ROWS_DEV = 6
WD = 72
RATE = 12
H = 48
SAMPLES = 8
N_ROW = 8
N_SAMPLE = 8


def plant(array, rng, low, high):
    spot = [jax.random.randint(jax.random.fold_in(rng, axis), (), 0, length) for axis, length in enumerate(array.shape)]
    main_axis = array.shape.index(max(array.shape))
    neighbour = spot[:main_axis] + [(spot[main_axis] + 1) % array.shape[main_axis]] + spot[main_axis + 1:]
    return array.at[tuple(spot)].set(low).at[tuple(neighbour)].set(high)


def level_of(key, shape, shards, least, high):
    gain = 1.0
    for position, parts in shards:
        steps = jax.random.uniform(jax.random.fold_in(jax.random.fold_in(key, 6), position), (parts,), jnp.float32, least / len(shards), high / len(shards))
        gain = gain * jnp.repeat(jnp.exp(steps), shape[position] // parts).reshape((-1,) + (1,) * (len(shape) - 1 - position))
    return gain


def bell_draw(rng, extent, scale, most, shards=(), held_as=jnp.bfloat16):
    drawn = scale * jax.random.normal(rng, extent, jnp.float32)
    if shards:
        drawn = drawn * level_of(rng, extent, shards, -0.22, 0.18)
    return jnp.clip(drawn, -most, most).astype(held_as)


def setup_inputs(seed: int = 0) -> dict:
    key_list = jax.random.split(jax.random.key(seed), 6)
    features = bell_draw(key_list[0], (SAMPLES, H, WD, C), 1.0, 6.0, ((0, 8), (1, 8), (3, 8)))
    weights = bell_draw(key_list[1], (O, 3, 9, C), (9 * C) ** -0.5, 0.046875, ((0, 8), (3, 8)))
    proj = bell_draw(key_list[2], (3 * O, E), (3 * O) ** -0.5, 0.21875)
    classify = bell_draw(key_list[3], (E, CLASSES), E ** -0.5, 0.375)
    labels = plant(jax.random.randint(key_list[4], (SAMPLES, H, WD), 0, CLASSES), jax.random.fold_in(key_list[4], 1), 0, CLASSES - 1).astype(jnp.int32)
    return dict(features=features, weights=weights, proj=proj, classify=classify, labels=labels)


def swish_grad(values):
    gate_value = jax.nn.sigmoid(values)
    return gate_value * (1.0 + values * (1.0 - gate_value))

def tail_grad(preact, proj, classify, flat_labels):
    pixel_count = preact.shape[0]
    activated = jax.nn.silu(preact).astype(jnp.bfloat16).reshape(pixel_count, -1)
    mixed_pre = jnp.dot(activated, proj, preferred_element_type=jnp.float32)
    hidden = jax.nn.silu(mixed_pre).astype(jnp.bfloat16)
    logits = jnp.dot(hidden, classify, preferred_element_type=jnp.float32)
    exp_logits = jnp.exp(logits)
    probabilities = exp_logits / lax.optimization_barrier(jnp.sum(exp_logits, axis=1, keepdims=True))
    classes_row = jnp.arange(classify.shape[1], dtype=jnp.int32)
    onehot = (flat_labels[:, None] == classes_row[None, :]).astype(jnp.float32)
    dlogits = (probabilities - onehot).astype(jnp.bfloat16)
    grad_hidden = lax.dot_general(dlogits, classify, (((1,), (1,)), ((), ())), preferred_element_type=jnp.float32)
    grad_mixed = (grad_hidden * swish_grad(mixed_pre)).astype(jnp.bfloat16)
    grad_act = lax.dot_general(grad_mixed, proj, (((1,), (1,)), ((), ())), preferred_element_type=jnp.float32)
    return (grad_act.reshape(preact.shape) * swish_grad(preact)).astype(jnp.bfloat16)

def reference(features, weights, proj, classify, labels):
    margin = 3 * RATE

    def sample_step(sample_block, accumulated):
        first_sample = (sample_block * B_DEV).astype(jnp.int32)
        padded_slab = lax.dynamic_slice_in_dim(features, first_sample, B_DEV, 0)
        padded_slab = jnp.pad(padded_slab, ((0, 0), (margin, margin), (margin, margin), (0, 0)))
        label_slab = lax.dynamic_slice_in_dim(labels, first_sample, B_DEV, 0)

        def row_step(row_block, accumulated):
            first_row = (row_block * ROWS_DEV).astype(jnp.int32)
            tap_list = []
            for branch in range(3):
                dilation = (branch + 1) * RATE
                for tap_row in range(3):
                    row_slice = lax.dynamic_slice_in_dim(padded_slab, (first_row + margin + dilation * (tap_row - 1)).astype(jnp.int32), ROWS_DEV, 1)
                    for tap_col in range(3):
                        left = margin + dilation * (tap_col - 1)
                        tap_list.append(row_slice[:, :, left:left + WD, :].reshape(-1, C))
            branch_outs = []
            for branch in range(3):
                running = jnp.zeros((tap_list[0].shape[0], O), jnp.float32)
                for tap_index in range(9):
                    running = running + lax.dot_general(tap_list[9 * branch + tap_index], weights[:, branch, tap_index, :], (((1,), (1,)), ((), ())), preferred_element_type=jnp.float32)
                branch_outs.append(running)
            preact = jnp.stack(branch_outs, axis=1)
            flat_labels = lax.dynamic_slice_in_dim(label_slab, first_row, ROWS_DEV, 1).reshape(-1)
            grad_pre = tail_grad(preact, proj, classify, flat_labels)
            grad_blocks = []
            for branch in range(3):
                for tap_index in range(9):
                    grad_blocks.append(lax.dot_general(grad_pre[:, branch, :], tap_list[9 * branch + tap_index], (((0,), (0,)), ((), ())), preferred_element_type=jnp.float32))
            partial_value = jnp.stack(grad_blocks, axis=1).reshape(O, 3, 9, C).astype(jnp.bfloat16)
            return accumulated + partial_value.astype(jnp.float32)
        return lax.fori_loop(0, N_ROW, row_step, accumulated)
    accumulated = lax.fori_loop(0, N_SAMPLE, sample_step, jnp.zeros((O, 3, 9, C), jnp.float32))
    return accumulated.astype(jnp.bfloat16)
```

```python
import jax
import jax.numpy as jnp
from jax import lax
from jax.experimental import pallas as pl
from jax.experimental.pallas import tpu as pltpu
from jax.sharding import Mesh, PartitionSpec as P

BF16 = jnp.bfloat16
F32 = jnp.float32

ROWS = 8
GRID_J = 4
GRID_Q = 6
UNIT = 72
UNITS = GRID_J * GRID_Q
HALF = UNITS * UNIT
PARTS = 32
SHARE = 56
PADDED = PARTS * SHARE
LANES = 128
CHAN = 256
OUTS = 32
TAPS = 27
ROW_AXES = ("row",)
VMEM_LIMIT = 48 * 1024 * 1024


def block_taps(j, q):
    found = []
    for branch in range(3):
        rate = branch + 1
        for tap_row in range(3):
            out_j = j - rate * (tap_row - 1)
            if not 0 <= out_j < GRID_J:
                continue
            for tap_col in range(3):
                out_q = q - rate * (tap_col - 1)
                if not 0 <= out_q < GRID_Q:
                    continue
                found.append((9 * branch + 3 * tap_row + tap_col, branch, out_j * GRID_Q + out_q))
    return found


def compiler_params():
    return pltpu.CompilerParams(vmem_limit_bytes=VMEM_LIMIT)


def prepare_kernel(features_ref, out_ref, rows_ref, units_ref):
    rows_ref[...] = features_ref[...].astype(F32)
    for row in range(6):
        for q in range(GRID_Q):
            units_ref[q * UNIT + row * 12 : q * UNIT + row * 12 + 12, :] = rows_ref[
                row * 72 + q * 12 : row * 72 + q * 12 + 12, :
            ]
    for q in range(GRID_Q):
        unit = units_ref[q * UNIT : (q + 1) * UNIT, :].astype(BF16)
        for device in range(ROWS):
            out_ref[device, q] = unit


def prepare(features):
    return pl.pallas_call(
        prepare_kernel,
        out_shape=jax.ShapeDtypeStruct((ROWS, GRID_Q, UNIT, CHAN), BF16),
        scratch_shapes=[pltpu.VMEM((432, CHAN), F32), pltpu.VMEM((432, CHAN), F32)],
        compiler_params=compiler_params(),
        cost_estimate=pl.CostEstimate(flops=0, bytes_accessed=2 * 9 * 432 * CHAN, transcendentals=0),
        name="prepare_features",
    )(features)


def forward_kernel(parity_ref, features_ref, weights_ref, out_ref, acc_ref, flat_ref):
    del parity_ref
    acc_ref[...] = jnp.zeros(acc_ref.shape, F32)
    for j in range(GRID_J):
        for q in range(GRID_Q):
            taps = block_taps(j, q)
            kernels = jnp.concatenate(
                [weights_ref[tap * OUTS : (tap + 1) * OUTS, :] for tap, _, _ in taps], axis=0
            )
            product = lax.dot_general(
                kernels, features_ref[j, 0, q], (((1,), (1,)), ((), ())), preferred_element_type=F32
            )
            for place, (_, branch, block) in enumerate(taps):
                acc_ref[block, branch * OUTS : (branch + 1) * OUTS, :UNIT] += product[
                    place * OUTS : (place + 1) * OUTS, :
                ]
    for block in range(UNITS):
        flat_ref[block * UNIT : (block + 1) * UNIT, :] = jnp.transpose(acc_ref[block])[:UNIT, :]
    flat_ref[HALF:, :] = jnp.zeros((PADDED - HALF, LANES), F32)
    out_ref[...] = flat_ref[...].astype(BF16)


def forward(parity, features, weights):
    return pl.pallas_call(
        forward_kernel,
        grid_spec=pltpu.PrefetchScalarGridSpec(
            num_scalar_prefetch=1,
            grid=(1,),
            in_specs=[
                pl.BlockSpec((GRID_J, 1, GRID_Q, UNIT, CHAN), lambda i, p: (0, p[0], 0, 0, 0)),
                pl.BlockSpec((TAPS * OUTS, CHAN), lambda i, p: (0, 0)),
            ],
            out_specs=pl.BlockSpec((PADDED, LANES), lambda i, p: (0, 0)),
            scratch_shapes=[
                pltpu.VMEM((UNITS, LANES, LANES), F32),
                pltpu.VMEM((PADDED, LANES), F32),
            ],
        ),
        out_shape=jax.ShapeDtypeStruct((PADDED, LANES), BF16),
        compiler_params=compiler_params(),
        cost_estimate=pl.CostEstimate(
            flops=2 * HALF * CHAN * TAPS * OUTS, bytes_accessed=2000000, transcendentals=0
        ),
        name="forward_taps",
    )(parity, features, weights)


def sigmoid(values):
    return 1.0 / (1.0 + jnp.exp(-values))


def swish_grad(values, gate_value):
    return gate_value * (1.0 + values * (1.0 - gate_value))


def tail_kernel(parts_ref, proj_ref, classify_ref, classify_t_ref, onehot_ref, out_ref):
    pre = []
    for row in range(ROWS):
        total = parts_ref[row].astype(F32)
        for part in range(1, PARTS // ROWS):
            total = total + parts_ref[part * ROWS + row].astype(F32)
        pre.append(total)
    preact = jnp.concatenate(pre, axis=1)
    gate = sigmoid(preact)
    activated = (preact * gate).astype(BF16)
    mixed_pre = jnp.dot(activated, proj_ref[...], preferred_element_type=F32)
    mixed_gate = sigmoid(mixed_pre)
    hidden = (mixed_pre * mixed_gate).astype(BF16)
    logits = jnp.dot(hidden, classify_ref[...], preferred_element_type=F32)
    lane = lax.broadcasted_iota(jnp.int32, logits.shape, 1)
    exp_logits = jnp.where(lane < 3, jnp.exp(logits), 0.0)
    probabilities = exp_logits / jnp.sum(exp_logits, axis=1, keepdims=True)
    dlogits = (probabilities - onehot_ref[...]).astype(BF16)
    grad_hidden = jnp.dot(dlogits, classify_t_ref[...], preferred_element_type=F32)
    grad_mixed = (grad_hidden * swish_grad(mixed_pre, mixed_gate)).astype(BF16)
    grad_act = lax.dot_general(
        grad_mixed, proj_ref[...], (((1,), (1,)), ((), ())), preferred_element_type=F32
    )
    grad_pre = (grad_act * swish_grad(preact, gate)).astype(BF16)
    for row in range(ROWS):
        block = grad_pre[:, row * LANES : (row + 1) * LANES]
        for part in range(PARTS // ROWS):
            out_ref[part * ROWS + row] = block


def tail(parts, proj, classify, classify_t, onehot):
    return pl.pallas_call(
        tail_kernel,
        out_shape=jax.ShapeDtypeStruct((PARTS, SHARE, LANES), BF16),
        compiler_params=compiler_params(),
        cost_estimate=pl.CostEstimate(
            flops=4 * SHARE * 1024 * CHAN, bytes_accessed=1500000, transcendentals=SHARE * 2000
        ),
        name="tail",
    )(parts, proj, classify, classify_t, onehot)


def gradient_kernel(parity_ref, own_ref, other_ref, features_ref, out_ref, flat_ref, turned_ref, acc_ref):
    own = parity_ref[0]
    for half, grads in enumerate((own_ref, other_ref)):
        flat_ref[...] = grads[...].astype(F32)
        for block in range(UNITS):
            turned = jnp.transpose(flat_ref[block * UNIT : block * UNIT + LANES, :])
            turned_ref[block, :, half * LANES : (half + 1) * LANES] = turned[: 3 * OUTS, :].astype(BF16)
    acc_ref[...] = jnp.zeros(acc_ref.shape, F32)
    gap = jnp.zeros((LANES - UNIT, CHAN), BF16)
    for j in range(GRID_J):
        for q in range(GRID_Q):
            taps = block_taps(j, q)
            grads = jnp.concatenate(
                [turned_ref[block, branch * OUTS : (branch + 1) * OUTS, :] for _, branch, block in taps],
                axis=0,
            )
            pixels = jnp.concatenate(
                [features_ref[j, own, q], gap, features_ref[j, 1 - own, q], gap], axis=0
            )
            product = jnp.dot(grads, pixels, preferred_element_type=F32)
            for place, (tap, _, _) in enumerate(taps):
                for lanes in range(2):
                    acc_ref[lanes, tap * OUTS : (tap + 1) * OUTS, :] += product[
                        place * OUTS : (place + 1) * OUTS, lanes * LANES : (lanes + 1) * LANES
                    ]
    for slot in range(OUTS):
        for lanes in range(2):
            start = slot % 4 * CHAN + lanes * LANES
            out_ref[slot // 4, :, start : start + LANES] = acc_ref[
                lanes, pl.ds(slot, 32, stride=OUTS), :
            ].astype(BF16)


def gradient(parity, own, other, features):
    whole = pl.BlockSpec(memory_space=pltpu.VMEM)
    return pl.pallas_call(
        gradient_kernel,
        in_specs=[pl.BlockSpec(memory_space=pltpu.SMEM), whole, whole, whole],
        out_specs=whole,
        out_shape=jax.ShapeDtypeStruct((8, 32, 4 * CHAN), BF16),
        scratch_shapes=[
            pltpu.VMEM((PADDED, LANES), F32),
            pltpu.VMEM((UNITS, 3 * OUTS, 2 * LANES), BF16),
            pltpu.VMEM((2, 32 * OUTS, LANES), F32),
        ],
        compiler_params=compiler_params(),
        cost_estimate=pl.CostEstimate(
            flops=4 * HALF * CHAN * TAPS * OUTS, bytes_accessed=4000000, transcendentals=0
        ),
        name="gradient_taps",
    )(parity, own, other, features)


def unshuffle_kernel(parts_ref, out_ref, rows_ref):
    for slot in range(OUTS):
        for lanes in range(2):
            start = slot % 4 * CHAN + lanes * LANES
            rows_ref[lanes, pl.ds(slot, 32, stride=OUTS), :] = parts_ref[
                slot // 4, :, start : start + LANES
            ].astype(F32)
    for lanes in range(2):
        out_ref[:, lanes * LANES : (lanes + 1) * LANES] = rows_ref[lanes, : TAPS * OUTS, :].astype(BF16)


def unshuffle(parts):
    return pl.pallas_call(
        unshuffle_kernel,
        out_shape=jax.ShapeDtypeStruct((TAPS * OUTS, CHAN), BF16),
        scratch_shapes=[pltpu.VMEM((2, 32 * OUTS, LANES), F32)],
        compiler_params=compiler_params(),
        cost_estimate=pl.CostEstimate(flops=0, bytes_accessed=1000000, transcendentals=0),
        name="unshuffle",
    )(parts)


def shards(features, weights, proj, classify, labels):
    row = lax.axis_index("row")
    core = lax.axis_index("core")
    part = lax.axis_index("yhi") * ROWS + row
    swap = [(0, 1), (1, 0)]

    sent = prepare(features.reshape(432, CHAN))
    gathered = lax.all_to_all(sent, "row", 0, 0).reshape(GRID_J, 2, GRID_Q, UNIT, CHAN)

    by_tap = weights.transpose(1, 2, 0, 3).reshape(TAPS, 32, CHAN)
    mine = lax.dynamic_slice_in_dim(by_tap, 4 * row, 4, 1).reshape(TAPS, 4 * CHAN)
    mine = jnp.pad(mine, ((0, 32 - TAPS), (0, 0)))
    kernels = unshuffle(lax.all_to_all(jnp.broadcast_to(mine[None], (8, 32, 4 * CHAN)), "sample", 0, 0))

    marks = labels.reshape(6, GRID_Q, 12).transpose(1, 0, 2).reshape(1, 432)
    marks = lax.all_to_all(jnp.broadcast_to(marks, (ROWS, 432)), "row", 0, 0).reshape(GRID_J, 2, 432)
    marks = lax.dynamic_index_in_dim(marks, core, 1, keepdims=False).reshape(HALF)
    marks = jnp.pad(marks, (0, PADDED - HALF)).reshape(PARTS, SHARE)
    marks = lax.dynamic_index_in_dim(marks, part, 0, keepdims=False)
    onehot = (marks[:, None] == jnp.arange(LANES, dtype=jnp.int32)[None, :]).astype(F32)

    mixing = proj.reshape(3, 8, ROWS, 4, CHAN).transpose(2, 0, 1, 3, 4).reshape(ROWS, 3 * OUTS, CHAN)
    mixing = jnp.pad(mixing, ((0, 0), (0, LANES - 3 * OUTS), (0, 0))).reshape(ROWS * LANES, CHAN)
    heads = jnp.pad(classify, ((0, 0), (0, LANES - 3)))
    heads_t = jnp.pad(classify.T, ((0, LANES - 3), (0, 0)))

    parity = core.astype(jnp.int32).reshape(1)
    other = forward(1 - parity, gathered, kernels)
    received = lax.ppermute(other, "core", swap)
    own = forward(parity, gathered, kernels)
    pair = (own.astype(F32) + received.astype(F32)).astype(BF16).reshape(PARTS, SHARE, LANES)
    parts = lax.all_to_all(pair, ("yhi", "row"), 0, 0)
    grads = tail(parts, mixing, heads, heads_t, onehot)
    grads_own = lax.all_to_all(grads, ("yhi", "row"), 0, 0).reshape(PADDED, LANES)
    grads_other = lax.ppermute(grads_own, "core", swap)
    partial = gradient(parity, grads_own, grads_other, gathered)
    over_samples = lax.all_to_all(partial, "sample", 0, 0)
    summed = jnp.sum(over_samples.astype(F32), axis=0).astype(BF16)
    final = lax.all_to_all(jnp.broadcast_to(summed[None], (ROWS, 32, 4 * CHAN)), "row", 0, 0)
    return unshuffle(final).reshape(3, 9, 32, CHAN).transpose(2, 0, 1, 3)


def solution(mesh):
    split = Mesh(mesh.devices.reshape(8, 4, 2, 8), ("row", "yhi", "core", "sample"))
    in_specs = (
        P("sample", "row", None, ("yhi", "core")),
        P("sample", None, None, ("yhi", "core")),
        P(),
        P(),
        P("sample", "row", None),
    )
    out_specs = P("sample", None, None, ("yhi", "core"))
    return jax.shard_map(shards, mesh=split, in_specs=in_specs, out_specs=out_specs, check_vma=False)
```

```python
import jax
import jax.numpy as jnp
from jax import lax
from jax.experimental import pallas as pl
from jax.experimental.pallas import tpu as pltpu
from jax.sharding import Mesh, PartitionSpec as P

BF16 = jnp.bfloat16
F32 = jnp.float32

ROWS = 8
GRID_J = 4
GRID_Q = 6
UNIT = 72
UNITS = GRID_J * GRID_Q
HALF = UNITS * UNIT
SHARD = 432
SENT = 440
PARTS = 32
USED = 27
SHARE = 48
BLOCK = 216
LANES = 128
CHAN = 256
OUTS = 32
TAPS = 27
ROW_AXES = ("row",)
VMEM_LIMIT = 48 * 1024 * 1024


def block_taps(j, q):
    found = []
    for branch in range(3):
        rate = branch + 1
        for tap_row in range(3):
            out_j = j - rate * (tap_row - 1)
            if not 0 <= out_j < GRID_J:
                continue
            for tap_col in range(3):
                out_q = q - rate * (tap_col - 1)
                if not 0 <= out_q < GRID_Q:
                    continue
                found.append((9 * branch + 3 * tap_row + tap_col, branch, out_j * GRID_Q + out_q))
    return found


def compiler_params():
    return pltpu.CompilerParams(vmem_limit_bytes=VMEM_LIMIT)


def prepare_kernel(features_ref, marks_ref, out_ref, rows_ref, units_ref):
    rows_ref[...] = features_ref[...].astype(F32)
    for row in range(6):
        for q in range(GRID_Q):
            units_ref[q * UNIT + row * 12 : q * UNIT + row * 12 + 12, :] = rows_ref[
                row * 72 + q * 12 : row * 72 + q * 12 + 12, :
            ]
    units_ref[SHARD:, :] = marks_ref[...]
    block = units_ref[...].astype(BF16)
    for device in range(ROWS):
        out_ref[device] = block


def prepare(features, marks):
    return pl.pallas_call(
        prepare_kernel,
        out_shape=jax.ShapeDtypeStruct((ROWS, SENT, CHAN), BF16),
        scratch_shapes=[pltpu.VMEM((SHARD, CHAN), F32), pltpu.VMEM((SENT, CHAN), F32)],
        compiler_params=compiler_params(),
        cost_estimate=pl.CostEstimate(flops=0, bytes_accessed=2 * 9 * SHARD * CHAN, transcendentals=0),
        name="prepare_features",
    )(features, marks)


def unit_rows(q):
    return slice(q * UNIT, (q + 1) * UNIT)


def forward_kernel(parity_ref, features_ref, weights_ref, out_ref, acc_ref, flat_ref):
    del parity_ref
    acc_ref[...] = jnp.zeros(acc_ref.shape, F32)
    for j in range(GRID_J):
        for q in range(GRID_Q):
            taps = block_taps(j, q)
            kernels = jnp.concatenate(
                [weights_ref[tap * OUTS : (tap + 1) * OUTS, :] for tap, _, _ in taps], axis=0
            )
            product = lax.dot_general(
                kernels,
                features_ref[j, 0, unit_rows(q), :],
                (((1,), (1,)), ((), ())),
                preferred_element_type=F32,
            )
            for place, (_, branch, block) in enumerate(taps):
                lane = block % 4 * OUTS
                acc_ref[block // 4, branch, lane : lane + OUTS, :UNIT] += product[
                    place * OUTS : (place + 1) * OUTS, :
                ]
    for group in range(UNITS // 4):
        for branch in range(3):
            flat_ref[branch, group * UNIT : (group + 1) * UNIT, :] = jnp.transpose(
                acc_ref[group, branch]
            )[:UNIT, :]
    for part in range(USED):
        for branch in range(3):
            out_ref[part, branch * 16 : (branch + 1) * 16, :] = flat_ref[
                branch, part * 16 : (part + 1) * 16, :
            ].astype(BF16)
    out_ref[USED:] = jnp.zeros((PARTS - USED, SHARE, LANES), BF16)


def forward(parity, features, weights):
    return pl.pallas_call(
        forward_kernel,
        grid_spec=pltpu.PrefetchScalarGridSpec(
            num_scalar_prefetch=1,
            grid=(1,),
            in_specs=[
                pl.BlockSpec((GRID_J, 1, SENT, CHAN), lambda i, p: (0, p[0], 0, 0)),
                pl.BlockSpec((TAPS * OUTS, CHAN), lambda i, p: (0, 0)),
            ],
            out_specs=pl.BlockSpec((PARTS, SHARE, LANES), lambda i, p: (0, 0, 0)),
            scratch_shapes=[
                pltpu.VMEM((UNITS // 4, 3, LANES, LANES), F32),
                pltpu.VMEM((3, HALF // 4, LANES), F32),
            ],
        ),
        out_shape=jax.ShapeDtypeStruct((PARTS, SHARE, LANES), BF16),
        compiler_params=compiler_params(),
        cost_estimate=pl.CostEstimate(
            flops=2 * HALF * CHAN * TAPS * OUTS, bytes_accessed=2000000, transcendentals=0
        ),
        name="forward_taps",
    )(parity, features, weights)


def sigmoid(values):
    return 1.0 / (1.0 + jnp.exp(-values))


def swish_grad(values, gate_value):
    return gate_value * (1.0 + values * (1.0 - gate_value))


def tail_kernel(parts_ref, proj_ref, classify_ref, classify_t_ref, onehot_ref, out_ref, act_ref, packed_ref):
    pieces = [(row, branch, place) for row in range(ROWS) for branch in range(3) for place in range(4)]

    def packed_at(branch, place):
        return slice(branch * 16, (branch + 1) * 16), slice(place * OUTS, (place + 1) * OUTS)

    def flat_at(row, branch, place):
        start = (row * 3 + branch) * OUTS
        return slice(place * 16, (place + 1) * 16), slice(start, start + OUTS)

    preact, gate = [], []
    for row in range(ROWS):
        total = parts_ref[row].astype(F32)
        for part in range(1, PARTS // ROWS):
            total = total + parts_ref[part * ROWS + row].astype(F32)
        preact.append(total)
        gate.append(sigmoid(total))
        packed_ref[row] = total * gate[row]
    for row, branch, place in pieces:
        at, lanes = packed_at(branch, place)
        act_ref[flat_at(row, branch, place)] = packed_ref[row, at, lanes]
    mixed_pre = jnp.dot(act_ref[...].astype(BF16), proj_ref[...], preferred_element_type=F32)
    mixed_gate = sigmoid(mixed_pre)
    hidden = (mixed_pre * mixed_gate).astype(BF16)
    logits = jnp.dot(hidden, classify_ref[...], preferred_element_type=F32)
    lane = lax.broadcasted_iota(jnp.int32, logits.shape, 1)
    exp_logits = jnp.where(lane < 3, jnp.exp(logits), 0.0)
    probabilities = exp_logits / jnp.sum(exp_logits, axis=1, keepdims=True)
    dlogits = (probabilities - onehot_ref[...]).astype(BF16)
    grad_hidden = jnp.dot(dlogits, classify_t_ref[...], preferred_element_type=F32)
    grad_mixed = (grad_hidden * swish_grad(mixed_pre, mixed_gate)).astype(BF16)
    act_ref[...] = lax.dot_general(
        grad_mixed, proj_ref[...], (((1,), (1,)), ((), ())), preferred_element_type=F32
    )
    for row, branch, place in pieces:
        at, lanes = packed_at(branch, place)
        packed_ref[row, at, lanes] = act_ref[flat_at(row, branch, place)]
    for row in range(ROWS):
        block = (packed_ref[row] * swish_grad(preact[row], gate[row])).astype(BF16)
        for part in range(PARTS // ROWS):
            out_ref[part * ROWS + row] = block


def tail(parts, proj, classify, classify_t, onehot):
    return pl.pallas_call(
        tail_kernel,
        out_shape=jax.ShapeDtypeStruct((PARTS, SHARE, LANES), BF16),
        scratch_shapes=[
            pltpu.VMEM((64, ROWS * 3 * OUTS), F32),
            pltpu.VMEM((ROWS, SHARE, LANES), F32),
        ],
        compiler_params=compiler_params(),
        cost_estimate=pl.CostEstimate(
            flops=4 * 64 * 768 * CHAN, bytes_accessed=1500000, transcendentals=64 * 2000
        ),
        name="tail",
    )(parts, proj, classify, classify_t, onehot)


def gradient_kernel(
    parity_ref, own_ref, other_ref, features_ref, out_ref, flat_ref, turned_ref, acc_ref, rows_ref
):
    own = parity_ref[0]
    flat_ref[:, HALF // 4 :, :] = jnp.zeros((3, LANES - UNIT, LANES), F32)
    for half, grads in enumerate((own_ref, other_ref)):
        for part in range(USED):
            for branch in range(3):
                flat_ref[branch, part * 16 : (part + 1) * 16, :] = grads[
                    part, branch * 16 : (branch + 1) * 16, :
                ].astype(F32)
        for group in range(UNITS // 4):
            for branch in range(3):
                turned = jnp.transpose(flat_ref[branch, group * UNIT : group * UNIT + LANES, :]).astype(BF16)
                for place in range(4):
                    turned_ref[
                        group * 4 + place,
                        branch * OUTS : (branch + 1) * OUTS,
                        half * LANES : (half + 1) * LANES,
                    ] = turned[place * OUTS : (place + 1) * OUTS, :]
    acc_ref[...] = jnp.zeros(acc_ref.shape, F32)
    gap = jnp.zeros((LANES - UNIT, CHAN), BF16)
    for j in range(GRID_J):
        for q in range(GRID_Q):
            taps = block_taps(j, q)
            grads = jnp.concatenate(
                [turned_ref[block, branch * OUTS : (branch + 1) * OUTS, :] for _, branch, block in taps],
                axis=0,
            )
            pixels = jnp.concatenate(
                [features_ref[j, own, unit_rows(q), :], gap, features_ref[j, 1 - own, unit_rows(q), :], gap],
                axis=0,
            )
            product = jnp.dot(grads, pixels, preferred_element_type=F32)
            for place, (tap, _, _) in enumerate(taps):
                for lanes in range(2):
                    acc_ref[lanes, tap * OUTS : (tap + 1) * OUTS, :] += product[
                        place * OUTS : (place + 1) * OUTS, lanes * LANES : (lanes + 1) * LANES
                    ]
    for slot in range(OUTS):
        for lanes in range(2):
            rows_ref[pl.ds(slot // 4 * BLOCK + slot % 4 * 2 + lanes, TAPS, stride=8), :] = acc_ref[
                lanes, pl.ds(slot, TAPS, stride=OUTS), :
            ]
    for sample in range(8):
        out_ref[sample] = rows_ref[sample * BLOCK : (sample + 1) * BLOCK, :].astype(BF16)


def gradient(parity, own, other, features):
    whole = pl.BlockSpec(memory_space=pltpu.VMEM)
    return pl.pallas_call(
        gradient_kernel,
        in_specs=[pl.BlockSpec(memory_space=pltpu.SMEM), whole, whole, whole],
        out_specs=whole,
        out_shape=jax.ShapeDtypeStruct((8, BLOCK, LANES), BF16),
        scratch_shapes=[
            pltpu.VMEM((3, HALF // 4 + LANES - UNIT, LANES), F32),
            pltpu.VMEM((UNITS, 3 * OUTS, 2 * LANES), BF16),
            pltpu.VMEM((2, TAPS * OUTS, LANES), F32),
            pltpu.VMEM((8 * BLOCK, LANES), F32),
        ],
        compiler_params=compiler_params(),
        cost_estimate=pl.CostEstimate(
            flops=4 * HALF * CHAN * TAPS * OUTS, bytes_accessed=4000000, transcendentals=0
        ),
        name="gradient_taps",
    )(parity, own, other, features)


def unshuffle_kernel(parts_ref, out_ref, packed_ref, rows_ref):
    for block in range(8):
        packed_ref[block * BLOCK : (block + 1) * BLOCK, :] = parts_ref[block].astype(F32)
    for slot in range(OUTS):
        for lanes in range(2):
            rows_ref[lanes, pl.ds(slot, TAPS, stride=OUTS), :] = packed_ref[
                pl.ds(slot // 4 * BLOCK + slot % 4 * 2 + lanes, TAPS, stride=8), :
            ]
    for lanes in range(2):
        out_ref[:, lanes * LANES : (lanes + 1) * LANES] = rows_ref[lanes].astype(BF16)


def unshuffle(parts):
    return pl.pallas_call(
        unshuffle_kernel,
        out_shape=jax.ShapeDtypeStruct((TAPS * OUTS, CHAN), BF16),
        scratch_shapes=[
            pltpu.VMEM((8 * BLOCK, LANES), F32),
            pltpu.VMEM((2, TAPS * OUTS, LANES), F32),
        ],
        compiler_params=compiler_params(),
        cost_estimate=pl.CostEstimate(flops=0, bytes_accessed=1000000, transcendentals=0),
        name="unshuffle",
    )(parts)


def shards(features, weights, proj, classify, labels):
    row = lax.axis_index("row")
    core = lax.axis_index("core")
    part = lax.axis_index("yhi") * ROWS + row
    swap = [(0, 1), (1, 0)]

    marks = labels.reshape(6, GRID_Q, 12).transpose(1, 0, 2).reshape(SHARD).astype(F32)
    marks = jnp.pad(marks, (0, (SENT - SHARD) * CHAN - SHARD)).reshape(SENT - SHARD, CHAN)
    sent = prepare(features.reshape(SHARD, CHAN), marks)
    by_tap = weights.transpose(1, 2, 0, 3).reshape(TAPS, 32, CHAN)
    mine = lax.dynamic_slice_in_dim(by_tap, 4 * row, 4, 1).reshape(BLOCK, LANES)
    sent, mine = lax.optimization_barrier((sent, mine))
    gathered = lax.all_to_all(sent, "row", 0, 0).reshape(GRID_J, 2, SENT, CHAN)
    kernels = unshuffle(lax.all_gather(mine, "sample"))

    mixing = proj.reshape(3, 8, ROWS, 4, CHAN).transpose(2, 0, 1, 3, 4).reshape(ROWS * 3 * OUTS, CHAN)
    heads = jnp.pad(classify, ((0, 0), (0, LANES - 3)))
    heads_t = jnp.pad(classify.T, ((0, LANES - 3), (0, 0)))
    kernels, mixing, heads, heads_t = lax.optimization_barrier((kernels, mixing, heads, heads_t))

    parity = core.astype(jnp.int32).reshape(1)
    other = forward(1 - parity, gathered, kernels)
    received = lax.ppermute(other, "core", swap)
    own = forward(parity, gathered, kernels)
    pair = (own.astype(F32) + received.astype(F32)).astype(BF16)

    marks = lax.dynamic_index_in_dim(gathered[:, :, SHARD : SHARD + 2, :], core, 1, keepdims=False)
    marks = marks.reshape(GRID_J, 2 * CHAN)[:, :SHARD].reshape(UNITS // 4, 4, UNIT)
    marks = marks.transpose(1, 0, 2).reshape(4, HALF // 4)
    marks = lax.dynamic_slice_in_dim(jnp.pad(marks, ((0, 0), (0, (PARTS - USED) * 16))), part * 16, 16, 1)
    onehot = (marks.reshape(64, 1) == jnp.arange(LANES, dtype=BF16)[None, :]).astype(F32)
    pair, onehot = lax.optimization_barrier((pair, onehot))

    parts = lax.all_to_all(pair, ("yhi", "row"), 0, 0)
    grads = tail(parts, mixing, heads, heads_t, onehot)
    grads_own = lax.all_to_all(grads, ("yhi", "row"), 0, 0)
    grads_other = lax.ppermute(grads_own, "core", swap)
    partial = gradient(parity, grads_own, grads_other, gathered)
    over_samples = lax.all_to_all(partial, "sample", 0, 0)
    summed = jnp.sum(over_samples.astype(F32), axis=0).astype(BF16)
    final = lax.all_to_all(jnp.broadcast_to(summed[None], (ROWS, BLOCK, LANES)), "row", 0, 0)
    return unshuffle(final).reshape(3, 9, 32, CHAN).transpose(2, 0, 1, 3)


def solution(mesh):
    split = Mesh(mesh.devices.reshape(8, 4, 2, 8), ("row", "yhi", "core", "sample"))
    in_specs = (
        P("sample", "row", None, ("yhi", "core")),
        P("sample", None, None, ("yhi", "core")),
        P(),
        P(),
        P("sample", "row", None),
    )
    out_specs = P("sample", None, None, ("yhi", "core"))
    return jax.shard_map(shards, mesh=split, in_specs=in_specs, out_specs=out_specs, check_vma=False)
```

```python
import jax
import jax.numpy as jnp
from jax import lax
from jax.experimental import pallas as pl
from jax.experimental.pallas import tpu as pltpu
from jax.sharding import Mesh, PartitionSpec as P

BF16 = jnp.bfloat16
F32 = jnp.float32

ROWS = 8
GRID_J = 4
GRID_Q = 6
UNIT = 72
UNITS = GRID_J * GRID_Q
HALF = UNITS * UNIT
SHARD = 432
SENT = 440
PARTS = 32
USED = 27
SHARE = 48
BLOCK = 216
LANES = 128
CHAN = 256
OUTS = 32
TAPS = 27
ROW_AXES = ("row",)
VMEM_LIMIT = 16 * 1024 * 1024


def block_taps(j, q):
    found = []
    for branch in range(3):
        rate = branch + 1
        for tap_row in range(3):
            out_j = j - rate * (tap_row - 1)
            if not 0 <= out_j < GRID_J:
                continue
            for tap_col in range(3):
                out_q = q - rate * (tap_col - 1)
                if not 0 <= out_q < GRID_Q:
                    continue
                found.append((9 * branch + 3 * tap_row + tap_col, branch, out_j * GRID_Q + out_q))
    return found


def compiler_params(limit=VMEM_LIMIT):
    return pltpu.CompilerParams(vmem_limit_bytes=limit)


def prepare_kernel(
    row_ref,
    features_ref,
    labels_ref,
    weights_ref,
    out_ref,
    mine_ref,
    local_ref,
    marks_ref,
    taps_ref,
    rows_ref,
    units_ref,
    wide_ref,
    packed_ref,
    block_ref,
    sems,
):
    copies = [
        pltpu.make_async_copy(source, target, sems.at[place])
        for place, (source, target) in enumerate(
            ((features_ref, local_ref), (labels_ref, marks_ref), (weights_ref, taps_ref))
        )
    ]
    for copy in copies:
        copy.start()
    units_ref[SHARD:, :] = jnp.zeros((SENT - SHARD, CHAN), F32)
    copies[1].wait()
    for row in range(6):
        for q in range(GRID_Q):
            units_ref[SHARD + q : SHARD + q + 1, row * 12 : row * 12 + 12] = marks_ref[
                row, :, q * 12 : q * 12 + 12
            ].astype(F32)
    copies[0].wait()
    rows_ref[...] = local_ref[...].astype(F32)
    for row in range(6):
        for q in range(GRID_Q):
            units_ref[q * UNIT + row * 12 : q * UNIT + row * 12 + 12, :] = rows_ref[
                row * 72 + q * 12 : row * 72 + q * 12 + 12, :
            ]
    block_ref[...] = units_ref[...].astype(BF16)
    sends = [
        pltpu.make_async_copy(block_ref, out_ref.at[device], sems.at[3 + device]) for device in range(ROWS)
    ]
    for send in sends:
        send.start()
    copies[2].wait()
    for lanes in range(2):
        wide_ref[lanes] = taps_ref[:, lanes * LANES : (lanes + 1) * LANES].astype(F32)
    first = row_ref[0] * 4
    for slot in range(4):
        for lanes in range(2):
            packed_ref[pl.ds(slot * 2 + lanes, TAPS, stride=8), :] = wide_ref[
                lanes, pl.ds(first + slot, TAPS, stride=OUTS), :
            ]
    mine_ref[...] = packed_ref[...].astype(BF16)
    for send in sends:
        send.wait()


def prepare(row, features, labels, weights):
    hbm = pl.BlockSpec(memory_space=pl.ANY)
    vmem = pl.BlockSpec(memory_space=pltpu.VMEM)
    return pl.pallas_call(
        prepare_kernel,
        in_specs=[pl.BlockSpec(memory_space=pltpu.SMEM), hbm, hbm, hbm],
        out_specs=[hbm, vmem],
        out_shape=[
            jax.ShapeDtypeStruct((ROWS, SENT, CHAN), BF16),
            jax.ShapeDtypeStruct((BLOCK, LANES), BF16),
        ],
        scratch_shapes=[
            pltpu.VMEM((SHARD, CHAN), BF16),
            pltpu.VMEM((6, 1, 72), jnp.int32),
            pltpu.VMEM((TAPS * OUTS, CHAN), BF16),
            pltpu.VMEM((SHARD, CHAN), F32),
            pltpu.VMEM((SENT, CHAN), F32),
            pltpu.VMEM((2, TAPS * OUTS, LANES), F32),
            pltpu.VMEM((BLOCK, LANES), F32),
            pltpu.VMEM((SENT, CHAN), BF16),
            pltpu.SemaphoreType.DMA((3 + ROWS,)),
        ],
        compiler_params=compiler_params(60 * 1024 * 1024),
        cost_estimate=pl.CostEstimate(flops=0, bytes_accessed=2 * 9 * SHARD * CHAN, transcendentals=0),
        name="prepare_blocks",
    )(row, features, labels, weights)


def unit_rows(q):
    return slice(q * UNIT, (q + 1) * UNIT)


def forward_kernel(core_ref, features_ref, weights_ref, own_ref, other_ref, acc_ref, flat_ref):
    acc_ref[...] = jnp.zeros(acc_ref.shape, F32)
    for j in range(GRID_J):
        for q in range(GRID_Q):
            taps = block_taps(j, q)
            kernels = jnp.concatenate(
                [weights_ref[tap * OUTS : (tap + 1) * OUTS, :] for tap, _, _ in taps], axis=0
            )
            pixels = jnp.concatenate(
                [features_ref[j, 0, unit_rows(q), :], features_ref[j, 1, unit_rows(q), :]], axis=0
            )
            product = lax.dot_general(
                kernels, pixels, (((1,), (1,)), ((), ())), preferred_element_type=F32
            )
            for place, (_, branch, block) in enumerate(taps):
                lane = block % 4 * OUTS
                acc_ref[block // 4, branch, lane : lane + OUTS, : 2 * UNIT] += product[
                    place * OUTS : (place + 1) * OUTS, :
                ]
    for group in range(UNITS // 4):
        for branch in range(3):
            turned = jnp.transpose(acc_ref[group, branch])
            for half in range(2):
                flat_ref[half, branch, group * UNIT : (group + 1) * UNIT, :] = turned[
                    half * UNIT : (half + 1) * UNIT, :
                ]
    own = core_ref[0]
    for half, out_ref in ((own, own_ref), (1 - own, other_ref)):
        for part in range(USED):
            for branch in range(3):
                out_ref[part, branch * 16 : (branch + 1) * 16, :] = flat_ref[
                    half, branch, part * 16 : (part + 1) * 16, :
                ].astype(BF16)
        out_ref[USED:] = jnp.zeros((PARTS - USED, SHARE, LANES), BF16)


def forward(core, features, weights):
    whole = pl.BlockSpec(memory_space=pltpu.VMEM)
    return pl.pallas_call(
        forward_kernel,
        in_specs=[pl.BlockSpec(memory_space=pltpu.SMEM), whole, whole],
        out_specs=[whole, whole],
        out_shape=[jax.ShapeDtypeStruct((PARTS, SHARE, LANES), BF16)] * 2,
        scratch_shapes=[
            pltpu.VMEM((UNITS // 4, 3, LANES, 2 * LANES), F32),
            pltpu.VMEM((2, 3, HALF // 4, LANES), F32),
        ],
        compiler_params=compiler_params(),
        cost_estimate=pl.CostEstimate(
            flops=4 * HALF * CHAN * TAPS * OUTS, bytes_accessed=4000000, transcendentals=0
        ),
        name="forward_taps",
    )(core, features, weights)


def sigmoid(values):
    return 1.0 / (1.0 + jnp.exp(-values))


def swish_grad(values, gate_value):
    return gate_value * (1.0 + values * (1.0 - gate_value))


def tail_kernel(parts_ref, proj_ref, classify_ref, classify_t_ref, onehot_ref, out_ref, act_ref, packed_ref):
    pieces = [(row, branch, place) for row in range(ROWS) for branch in range(3) for place in range(4)]

    def packed_at(branch, place):
        return slice(branch * 16, (branch + 1) * 16), slice(place * OUTS, (place + 1) * OUTS)

    def flat_at(row, branch, place):
        start = (row * 3 + branch) * OUTS
        return slice(place * 16, (place + 1) * 16), slice(start, start + OUTS)

    preact, gate = [], []
    for row in range(ROWS):
        total = parts_ref[row].astype(F32)
        for part in range(1, PARTS // ROWS):
            total = total + parts_ref[part * ROWS + row].astype(F32)
        preact.append(total)
        gate.append(sigmoid(total))
        packed_ref[row] = total * gate[row]
    for row, branch, place in pieces:
        at, lanes = packed_at(branch, place)
        act_ref[flat_at(row, branch, place)] = packed_ref[row, at, lanes]
    mixed_pre = jnp.dot(act_ref[...].astype(BF16), proj_ref[...], preferred_element_type=F32)
    mixed_gate = sigmoid(mixed_pre)
    hidden = (mixed_pre * mixed_gate).astype(BF16)
    logits = jnp.dot(hidden, classify_ref[...], preferred_element_type=F32)
    lane = lax.broadcasted_iota(jnp.int32, logits.shape, 1)
    exp_logits = jnp.where(lane < 3, jnp.exp(logits), 0.0)
    probabilities = exp_logits / jnp.sum(exp_logits, axis=1, keepdims=True)
    dlogits = (probabilities - onehot_ref[...]).astype(BF16)
    grad_hidden = jnp.dot(dlogits, classify_t_ref[...], preferred_element_type=F32)
    grad_mixed = (grad_hidden * swish_grad(mixed_pre, mixed_gate)).astype(BF16)
    act_ref[...] = lax.dot_general(
        grad_mixed, proj_ref[...], (((1,), (1,)), ((), ())), preferred_element_type=F32
    )
    for row, branch, place in pieces:
        at, lanes = packed_at(branch, place)
        packed_ref[row, at, lanes] = act_ref[flat_at(row, branch, place)]
    for row in range(ROWS):
        block = (packed_ref[row] * swish_grad(preact[row], gate[row])).astype(BF16)
        for part in range(PARTS // ROWS):
            out_ref[part * ROWS + row] = block


def tail(parts, proj, classify, classify_t, onehot):
    return pl.pallas_call(
        tail_kernel,
        out_shape=jax.ShapeDtypeStruct((PARTS, SHARE, LANES), BF16),
        scratch_shapes=[
            pltpu.VMEM((64, ROWS * 3 * OUTS), F32),
            pltpu.VMEM((ROWS, SHARE, LANES), F32),
        ],
        compiler_params=compiler_params(),
        cost_estimate=pl.CostEstimate(
            flops=4 * 64 * 768 * CHAN, bytes_accessed=1500000, transcendentals=64 * 2000
        ),
        name="tail",
    )(parts, proj, classify, classify_t, onehot)


def gradient_kernel(
    parity_ref, own_ref, other_ref, features_ref, out_ref, flat_ref, turned_ref, acc_ref, rows_ref
):
    own = parity_ref[0]
    flat_ref[:, HALF // 4 :, :] = jnp.zeros((3, LANES - UNIT, LANES), F32)
    for half, grads in enumerate((own_ref, other_ref)):
        for part in range(USED):
            for branch in range(3):
                flat_ref[branch, part * 16 : (part + 1) * 16, :] = grads[
                    part, branch * 16 : (branch + 1) * 16, :
                ].astype(F32)
        for group in range(UNITS // 4):
            for branch in range(3):
                turned = jnp.transpose(flat_ref[branch, group * UNIT : group * UNIT + LANES, :]).astype(BF16)
                for place in range(4):
                    turned_ref[
                        group * 4 + place,
                        branch * OUTS : (branch + 1) * OUTS,
                        half * LANES : (half + 1) * LANES,
                    ] = turned[place * OUTS : (place + 1) * OUTS, :]
    acc_ref[...] = jnp.zeros(acc_ref.shape, F32)
    gap = jnp.zeros((LANES - UNIT, CHAN), BF16)
    for j in range(GRID_J):
        for q in range(GRID_Q):
            taps = block_taps(j, q)
            grads = jnp.concatenate(
                [turned_ref[block, branch * OUTS : (branch + 1) * OUTS, :] for _, branch, block in taps],
                axis=0,
            )
            pixels = jnp.concatenate(
                [features_ref[j, own, unit_rows(q), :], gap, features_ref[j, 1 - own, unit_rows(q), :], gap],
                axis=0,
            )
            product = jnp.dot(grads, pixels, preferred_element_type=F32)
            for place, (tap, _, _) in enumerate(taps):
                for lanes in range(2):
                    acc_ref[lanes, tap * OUTS : (tap + 1) * OUTS, :] += product[
                        place * OUTS : (place + 1) * OUTS, lanes * LANES : (lanes + 1) * LANES
                    ]
    for slot in range(OUTS):
        for lanes in range(2):
            rows_ref[pl.ds(slot // 4 * BLOCK + slot % 4 * 2 + lanes, TAPS, stride=8), :] = acc_ref[
                lanes, pl.ds(slot, TAPS, stride=OUTS), :
            ]
    for sample in range(8):
        out_ref[sample] = rows_ref[sample * BLOCK : (sample + 1) * BLOCK, :].astype(BF16)


def gradient(parity, own, other, features):
    whole = pl.BlockSpec(memory_space=pltpu.VMEM)
    return pl.pallas_call(
        gradient_kernel,
        in_specs=[pl.BlockSpec(memory_space=pltpu.SMEM), whole, whole, whole],
        out_specs=whole,
        out_shape=jax.ShapeDtypeStruct((8, BLOCK, LANES), BF16),
        scratch_shapes=[
            pltpu.VMEM((3, HALF // 4 + LANES - UNIT, LANES), F32),
            pltpu.VMEM((UNITS, 3 * OUTS, 2 * LANES), BF16),
            pltpu.VMEM((2, TAPS * OUTS, LANES), F32),
            pltpu.VMEM((8 * BLOCK, LANES), F32),
        ],
        compiler_params=compiler_params(),
        cost_estimate=pl.CostEstimate(
            flops=4 * HALF * CHAN * TAPS * OUTS, bytes_accessed=4000000, transcendentals=0
        ),
        name="gradient_taps",
    )(parity, own, other, features)


def unshuffle_kernel(parts_ref, out_ref, packed_ref, rows_ref):
    for block in range(8):
        packed_ref[block * BLOCK : (block + 1) * BLOCK, :] = parts_ref[block].astype(F32)
    for slot in range(OUTS):
        for lanes in range(2):
            rows_ref[lanes, pl.ds(slot, TAPS, stride=OUTS), :] = packed_ref[
                pl.ds(slot // 4 * BLOCK + slot % 4 * 2 + lanes, TAPS, stride=8), :
            ]
    for lanes in range(2):
        out_ref[:, lanes * LANES : (lanes + 1) * LANES] = rows_ref[lanes].astype(BF16)


def unshuffle(parts):
    return pl.pallas_call(
        unshuffle_kernel,
        out_shape=jax.ShapeDtypeStruct((TAPS * OUTS, CHAN), BF16),
        scratch_shapes=[
            pltpu.VMEM((8 * BLOCK, LANES), F32),
            pltpu.VMEM((2, TAPS * OUTS, LANES), F32),
        ],
        compiler_params=compiler_params(),
        cost_estimate=pl.CostEstimate(flops=0, bytes_accessed=1000000, transcendentals=0),
        name="unshuffle",
    )(parts)


def shards(features, weights, proj, classify, labels):
    row = lax.axis_index("row")
    core = lax.axis_index("core")
    part = lax.axis_index("yhi") * ROWS + row
    swap = [(0, 1), (1, 0)]

    sent, mine = prepare(
        row.astype(jnp.int32).reshape(1),
        features.reshape(SHARD, CHAN),
        labels.transpose(1, 0, 2),
        weights.transpose(1, 2, 0, 3).reshape(TAPS * OUTS, CHAN),
    )
    gathered = lax.all_to_all(sent, "row", 0, 0).reshape(GRID_J, 2, SENT, CHAN)
    kernels = unshuffle(lax.all_gather(mine, "sample"))

    mixing = proj.reshape(3, 8, ROWS, 4, CHAN).transpose(2, 0, 1, 3, 4).reshape(ROWS * 3 * OUTS, CHAN)
    heads = jnp.pad(classify, ((0, 0), (0, LANES - 3)))
    heads_t = jnp.pad(classify.T, ((0, LANES - 3), (0, 0)))
    marks = lax.dynamic_index_in_dim(gathered[:, :, SHARD : SHARD + GRID_Q, :UNIT], core, 1, keepdims=False)
    marks = marks.reshape(UNITS // 4, 4, UNIT).transpose(1, 0, 2).reshape(4, HALF // 4)
    marks = lax.dynamic_slice_in_dim(jnp.pad(marks, ((0, 0), (0, (PARTS - USED) * 16))), part * 16, 16, 1)
    onehot = (marks.reshape(64, 1) == jnp.arange(LANES, dtype=BF16)[None, :]).astype(F32)
    kernels, mixing, heads, heads_t, onehot = lax.optimization_barrier(
        (kernels, mixing, heads, heads_t, onehot)
    )

    parity = core.astype(jnp.int32).reshape(1)
    own, other = forward(parity, gathered, kernels)
    received = lax.ppermute(other, "core", swap)
    pair = (own.astype(F32) + received.astype(F32)).astype(BF16)

    parts = lax.all_to_all(pair, ("yhi", "row"), 0, 0)
    grads = tail(parts, mixing, heads, heads_t, onehot)
    grads_own = lax.all_to_all(grads, ("yhi", "row"), 0, 0)
    grads_other = lax.ppermute(grads_own, "core", swap)
    partial = gradient(parity, grads_own, grads_other, gathered)
    over_samples = lax.all_to_all(partial, "sample", 0, 0)
    summed = jnp.sum(over_samples.astype(F32), axis=0).astype(BF16)
    final = lax.all_to_all(jnp.broadcast_to(summed[None], (ROWS, BLOCK, LANES)), "row", 0, 0)
    return unshuffle(final).reshape(3, 9, 32, CHAN).transpose(2, 0, 1, 3)


def solution(mesh):
    split = Mesh(mesh.devices.reshape(8, 4, 2, 8), ("row", "yhi", "core", "sample"))
    in_specs = (
        P("sample", "row", None, ("yhi", "core")),
        P("sample", None, None, ("yhi", "core")),
        P(),
        P(),
        P("sample", "row", None),
    )
    out_specs = P("sample", None, None, ("yhi", "core"))
    return jax.shard_map(shards, mesh=split, in_specs=in_specs, out_specs=out_specs, check_vma=False)
```

```python
import jax
import jax.numpy as jnp
from jax import lax
from jax.experimental import pallas as pl
from jax.experimental.pallas import tpu as pltpu
from jax.sharding import Mesh, PartitionSpec as P

BF16 = jnp.bfloat16
F32 = jnp.float32

ROWS = 8
GRID_J = 4
GRID_Q = 6
UNIT = 72
UNITS = GRID_J * GRID_Q
HALF = UNITS * UNIT
SHARD = 432
SENT = 440
PARTS = 32
USED = 27
SHARE = 48
BLOCK = 216
LANES = 128
CHAN = 256
OUTS = 32
TAPS = 27
ROW_AXES = ("row",)
VMEM_LIMIT = 16 * 1024 * 1024


def block_taps(j, q):
    found = []
    for branch in range(3):
        rate = branch + 1
        for tap_row in range(3):
            out_j = j - rate * (tap_row - 1)
            if not 0 <= out_j < GRID_J:
                continue
            for tap_col in range(3):
                out_q = q - rate * (tap_col - 1)
                if not 0 <= out_q < GRID_Q:
                    continue
                found.append((9 * branch + 3 * tap_row + tap_col, branch, out_j * GRID_Q + out_q))
    return found


def compiler_params(limit=VMEM_LIMIT):
    return pltpu.CompilerParams(vmem_limit_bytes=limit)


def prepare_kernel(
    row_ref,
    features_ref,
    labels_ref,
    weights_ref,
    out_ref,
    mine_ref,
    local_ref,
    marks_ref,
    taps_ref,
    rows_ref,
    units_ref,
    wide_ref,
    packed_ref,
    block_ref,
    sems,
):
    near = weights_ref.at[:, pl.ds(row_ref[0] // 4 * 16, 16), :]
    copies = [
        pltpu.make_async_copy(source, target, sems.at[place])
        for place, (source, target) in enumerate(
            ((features_ref, local_ref), (labels_ref, marks_ref), (near, taps_ref))
        )
    ]
    for copy in copies:
        copy.start()
    units_ref[SHARD:, :] = jnp.zeros((SENT - SHARD, CHAN), F32)
    copies[1].wait()
    for row in range(6):
        for q in range(GRID_Q):
            units_ref[SHARD + q : SHARD + q + 1, row * 12 : row * 12 + 12] = marks_ref[
                row, :, q * 12 : q * 12 + 12
            ].astype(F32)
    copies[0].wait()
    rows_ref[...] = local_ref[...].astype(F32)
    for row in range(6):
        for q in range(GRID_Q):
            units_ref[q * UNIT + row * 12 : q * UNIT + row * 12 + 12, :] = rows_ref[
                row * 72 + q * 12 : row * 72 + q * 12 + 12, :
            ]
    block_ref[...] = units_ref[...].astype(BF16)
    sends = [
        pltpu.make_async_copy(block_ref, out_ref.at[device], sems.at[3 + device]) for device in range(ROWS)
    ]
    for send in sends:
        send.start()
    copies[2].wait()
    for tap in range(TAPS):
        for lanes in range(2):
            wide_ref[lanes, tap * 16 : (tap + 1) * 16, :] = taps_ref[
                tap, :, lanes * LANES : (lanes + 1) * LANES
            ].astype(F32)
    first = row_ref[0] % 4 * 4
    for slot in range(4):
        for lanes in range(2):
            packed_ref[pl.ds(slot * 2 + lanes, TAPS, stride=8), :] = wide_ref[
                lanes, pl.ds(first + slot, TAPS, stride=16), :
            ]
    mine_ref[...] = packed_ref[...].astype(BF16)
    for send in sends:
        send.wait()


def prepare(row, features, labels, weights):
    hbm = pl.BlockSpec(memory_space=pl.ANY)
    vmem = pl.BlockSpec(memory_space=pltpu.VMEM)
    return pl.pallas_call(
        prepare_kernel,
        in_specs=[pl.BlockSpec(memory_space=pltpu.SMEM), hbm, hbm, hbm],
        out_specs=[hbm, vmem],
        out_shape=[
            jax.ShapeDtypeStruct((ROWS, SENT, CHAN), BF16),
            jax.ShapeDtypeStruct((BLOCK, LANES), BF16),
        ],
        scratch_shapes=[
            pltpu.VMEM((SHARD, CHAN), BF16),
            pltpu.VMEM((6, 1, 72), jnp.int32),
            pltpu.VMEM((TAPS, 16, CHAN), BF16),
            pltpu.VMEM((SHARD, CHAN), F32),
            pltpu.VMEM((SENT, CHAN), F32),
            pltpu.VMEM((2, TAPS * 16, LANES), F32),
            pltpu.VMEM((BLOCK, LANES), F32),
            pltpu.VMEM((SENT, CHAN), BF16),
            pltpu.SemaphoreType.DMA((3 + ROWS,)),
        ],
        compiler_params=compiler_params(60 * 1024 * 1024),
        cost_estimate=pl.CostEstimate(flops=0, bytes_accessed=2 * 9 * SHARD * CHAN, transcendentals=0),
        name="prepare_blocks",
    )(row, features, labels, weights)


def unit_rows(q):
    return slice(q * UNIT, (q + 1) * UNIT)


def spread_rows(packed_ref, rows_ref, out_ref):
    for slot in range(OUTS):
        for lanes in range(2):
            rows_ref[lanes, pl.ds(slot, TAPS, stride=OUTS), :] = packed_ref[
                pl.ds(slot // 4 * BLOCK + slot % 4 * 2 + lanes, TAPS, stride=8), :
            ]
    for lanes in range(2):
        out_ref[:, lanes * LANES : (lanes + 1) * LANES] = rows_ref[lanes].astype(BF16)


def forward_kernel(
    core_ref, zlo_ref, features_ref, parts_ref, own_ref, other_ref, acc_ref, flat_ref, packed_ref, rows_ref, weights_ref
):
    acc_ref[...] = jnp.zeros(acc_ref.shape, F32)
    for sample in range(8):
        packed_ref[sample * BLOCK : (sample + 1) * BLOCK, :] = parts_ref[
            sample // 2, sample % 2 ^ zlo_ref[0]
        ].astype(F32)
    spread_rows(packed_ref, rows_ref, weights_ref)
    for j in range(GRID_J):
        for q in range(GRID_Q):
            taps = block_taps(j, q)
            kernels = jnp.concatenate(
                [weights_ref[tap * OUTS : (tap + 1) * OUTS, :] for tap, _, _ in taps], axis=0
            )
            pixels = jnp.concatenate(
                [features_ref[j, 0, unit_rows(q), :], features_ref[j, 1, unit_rows(q), :]], axis=0
            )
            product = lax.dot_general(
                kernels, pixels, (((1,), (1,)), ((), ())), preferred_element_type=F32
            )
            for place, (_, branch, block) in enumerate(taps):
                lane = block % 4 * OUTS
                acc_ref[block // 4, branch, lane : lane + OUTS, : 2 * UNIT] += product[
                    place * OUTS : (place + 1) * OUTS, :
                ]
    for group in range(UNITS // 4):
        for branch in range(3):
            turned = jnp.transpose(acc_ref[group, branch])
            for half in range(2):
                flat_ref[half, branch, group * UNIT : (group + 1) * UNIT, :] = turned[
                    half * UNIT : (half + 1) * UNIT, :
                ]
    own = core_ref[0]
    for half, out_ref in ((own, own_ref), (1 - own, other_ref)):
        for part in range(USED):
            for branch in range(3):
                out_ref[part, branch * 16 : (branch + 1) * 16, :] = flat_ref[
                    half, branch, part * 16 : (part + 1) * 16, :
                ].astype(BF16)
        out_ref[USED:] = jnp.zeros((PARTS - USED, SHARE, LANES), BF16)


def forward(core, zlo, features, parts):
    whole = pl.BlockSpec(memory_space=pltpu.VMEM)
    return pl.pallas_call(
        forward_kernel,
        in_specs=[pl.BlockSpec(memory_space=pltpu.SMEM)] * 2 + [whole, whole],
        out_specs=[whole, whole],
        out_shape=[jax.ShapeDtypeStruct((PARTS, SHARE, LANES), BF16)] * 2,
        scratch_shapes=[
            pltpu.VMEM((UNITS // 4, 3, LANES, 2 * LANES), F32),
            pltpu.VMEM((2, 3, HALF // 4, LANES), F32),
            pltpu.VMEM((8 * BLOCK, LANES), F32),
            pltpu.VMEM((2, TAPS * OUTS, LANES), F32),
            pltpu.VMEM((TAPS * OUTS, CHAN), BF16),
        ],
        compiler_params=compiler_params(),
        cost_estimate=pl.CostEstimate(
            flops=4 * HALF * CHAN * TAPS * OUTS, bytes_accessed=4000000, transcendentals=0
        ),
        name="forward_taps",
    )(core, zlo, features, parts)


def sigmoid(values):
    return 1.0 / (1.0 + jnp.exp(-values))


def swish_grad(values, gate_value):
    return gate_value * (1.0 + values * (1.0 - gate_value))


def tail_kernel(parts_ref, proj_ref, classify_ref, classify_t_ref, onehot_ref, out_ref, act_ref, packed_ref):
    pieces = [(row, branch, place) for row in range(ROWS) for branch in range(3) for place in range(4)]

    def packed_at(branch, place):
        return slice(branch * 16, (branch + 1) * 16), slice(place * OUTS, (place + 1) * OUTS)

    def flat_at(row, branch, place):
        start = (row * 3 + branch) * OUTS
        return slice(place * 16, (place + 1) * 16), slice(start, start + OUTS)

    preact, gate = [], []
    for row in range(ROWS):
        total = parts_ref[row].astype(F32)
        for part in range(1, PARTS // ROWS):
            total = total + parts_ref[part * ROWS + row].astype(F32)
        preact.append(total)
        gate.append(sigmoid(total))
        packed_ref[row] = total * gate[row]
    for row, branch, place in pieces:
        at, lanes = packed_at(branch, place)
        act_ref[flat_at(row, branch, place)] = packed_ref[row, at, lanes]
    mixed_pre = jnp.dot(act_ref[...].astype(BF16), proj_ref[...], preferred_element_type=F32)
    mixed_gate = sigmoid(mixed_pre)
    hidden = (mixed_pre * mixed_gate).astype(BF16)
    logits = jnp.dot(hidden, classify_ref[...], preferred_element_type=F32)
    lane = lax.broadcasted_iota(jnp.int32, logits.shape, 1)
    exp_logits = jnp.where(lane < 3, jnp.exp(logits), 0.0)
    probabilities = exp_logits / jnp.sum(exp_logits, axis=1, keepdims=True)
    dlogits = (probabilities - onehot_ref[...]).astype(BF16)
    grad_hidden = jnp.dot(dlogits, classify_t_ref[...], preferred_element_type=F32)
    grad_mixed = (grad_hidden * swish_grad(mixed_pre, mixed_gate)).astype(BF16)
    act_ref[...] = lax.dot_general(
        grad_mixed, proj_ref[...], (((1,), (1,)), ((), ())), preferred_element_type=F32
    )
    for row, branch, place in pieces:
        at, lanes = packed_at(branch, place)
        packed_ref[row, at, lanes] = act_ref[flat_at(row, branch, place)]
    for row in range(ROWS):
        block = (packed_ref[row] * swish_grad(preact[row], gate[row])).astype(BF16)
        for part in range(PARTS // ROWS):
            out_ref[part * ROWS + row] = block


def tail(parts, proj, classify, classify_t, onehot):
    return pl.pallas_call(
        tail_kernel,
        out_shape=jax.ShapeDtypeStruct((PARTS, SHARE, LANES), BF16),
        scratch_shapes=[
            pltpu.VMEM((64, ROWS * 3 * OUTS), F32),
            pltpu.VMEM((ROWS, SHARE, LANES), F32),
        ],
        compiler_params=compiler_params(),
        cost_estimate=pl.CostEstimate(
            flops=4 * 64 * 768 * CHAN, bytes_accessed=1500000, transcendentals=64 * 2000
        ),
        name="tail",
    )(parts, proj, classify, classify_t, onehot)


def gradient_kernel(
    parity_ref, own_ref, other_ref, features_ref, out_ref, flat_ref, turned_ref, acc_ref, rows_ref
):
    own = parity_ref[0]
    flat_ref[:, HALF // 4 :, :] = jnp.zeros((3, LANES - UNIT, LANES), F32)
    for half, grads in enumerate((own_ref, other_ref)):
        for part in range(USED):
            for branch in range(3):
                flat_ref[branch, part * 16 : (part + 1) * 16, :] = grads[
                    part, branch * 16 : (branch + 1) * 16, :
                ].astype(F32)
        for group in range(UNITS // 4):
            for branch in range(3):
                turned = jnp.transpose(flat_ref[branch, group * UNIT : group * UNIT + LANES, :]).astype(BF16)
                for place in range(4):
                    turned_ref[
                        group * 4 + place,
                        branch * OUTS : (branch + 1) * OUTS,
                        half * LANES : (half + 1) * LANES,
                    ] = turned[place * OUTS : (place + 1) * OUTS, :]
    acc_ref[...] = jnp.zeros(acc_ref.shape, F32)
    gap = jnp.zeros((LANES - UNIT, CHAN), BF16)
    for j in range(GRID_J):
        for q in range(GRID_Q):
            taps = block_taps(j, q)
            grads = jnp.concatenate(
                [turned_ref[block, branch * OUTS : (branch + 1) * OUTS, :] for _, branch, block in taps],
                axis=0,
            )
            pixels = jnp.concatenate(
                [features_ref[j, own, unit_rows(q), :], gap, features_ref[j, 1 - own, unit_rows(q), :], gap],
                axis=0,
            )
            product = jnp.dot(grads, pixels, preferred_element_type=F32)
            for place, (tap, _, _) in enumerate(taps):
                for lanes in range(2):
                    acc_ref[lanes, tap * OUTS : (tap + 1) * OUTS, :] += product[
                        place * OUTS : (place + 1) * OUTS, lanes * LANES : (lanes + 1) * LANES
                    ]
    for slot in range(OUTS):
        for lanes in range(2):
            rows_ref[pl.ds(slot // 4 * BLOCK + slot % 4 * 2 + lanes, TAPS, stride=8), :] = acc_ref[
                lanes, pl.ds(slot, TAPS, stride=OUTS), :
            ]
    for sample in range(8):
        out_ref[sample] = rows_ref[sample * BLOCK : (sample + 1) * BLOCK, :].astype(BF16)


def gradient(parity, own, other, features):
    whole = pl.BlockSpec(memory_space=pltpu.VMEM)
    return pl.pallas_call(
        gradient_kernel,
        in_specs=[pl.BlockSpec(memory_space=pltpu.SMEM), whole, whole, whole],
        out_specs=whole,
        out_shape=jax.ShapeDtypeStruct((8, BLOCK, LANES), BF16),
        scratch_shapes=[
            pltpu.VMEM((3, HALF // 4 + LANES - UNIT, LANES), F32),
            pltpu.VMEM((UNITS, 3 * OUTS, 2 * LANES), BF16),
            pltpu.VMEM((2, TAPS * OUTS, LANES), F32),
            pltpu.VMEM((8 * BLOCK, LANES), F32),
        ],
        compiler_params=compiler_params(),
        cost_estimate=pl.CostEstimate(
            flops=4 * HALF * CHAN * TAPS * OUTS, bytes_accessed=4000000, transcendentals=0
        ),
        name="gradient_taps",
    )(parity, own, other, features)


def finish_kernel(parts_ref, out_ref, packed_ref, rows_ref, done_ref, sems):
    for block in range(8):
        packed_ref[block * BLOCK : (block + 1) * BLOCK, :] = parts_ref[block].astype(F32)
    sends = []
    for place, first in enumerate(range(0, TAPS, 9)):
        at = slice(first * OUTS, (first + 9) * OUTS)
        for slot in range(OUTS):
            for lanes in range(2):
                source = slot // 4 * BLOCK + slot % 4 * 2 + lanes + first * 8
                rows_ref[lanes, pl.ds(first * OUTS + slot, 9, stride=OUTS), :] = packed_ref[
                    pl.ds(source, 9, stride=8), :
                ]
        for lanes in range(2):
            done_ref[at, lanes * LANES : (lanes + 1) * LANES] = rows_ref[lanes, at, :].astype(BF16)
        sends.append(pltpu.make_async_copy(done_ref.at[at], out_ref.at[at], sems.at[place]))
        sends[-1].start()
    for send in sends:
        send.wait()


def finish(parts):
    return pl.pallas_call(
        finish_kernel,
        in_specs=[pl.BlockSpec(memory_space=pltpu.VMEM)],
        out_specs=pl.BlockSpec(memory_space=pl.ANY),
        out_shape=jax.ShapeDtypeStruct((TAPS * OUTS, CHAN), BF16),
        scratch_shapes=[
            pltpu.VMEM((8 * BLOCK, LANES), F32),
            pltpu.VMEM((2, TAPS * OUTS, LANES), F32),
            pltpu.VMEM((TAPS * OUTS, CHAN), BF16),
            pltpu.SemaphoreType.DMA((3,)),
        ],
        compiler_params=compiler_params(),
        cost_estimate=pl.CostEstimate(flops=0, bytes_accessed=1000000, transcendentals=0),
        name="finish",
    )(parts)


def shards(features, weights, proj, classify, labels):
    row = lax.axis_index("row")
    core = lax.axis_index("core")
    part = lax.axis_index("yhi") * ROWS + row
    swap = [(0, 1), (1, 0)]

    sent, mine = prepare(
        row.astype(jnp.int32).reshape(1),
        features.reshape(SHARD, CHAN),
        labels.transpose(1, 0, 2),
        weights.transpose(1, 2, 0, 3).reshape(TAPS, OUTS, CHAN),
    )
    gathered = lax.all_to_all(sent, "row", 0, 0).reshape(GRID_J, 2, SENT, CHAN)
    pairs = jnp.stack([mine, lax.ppermute(mine, "zlo", swap)])
    kernels = lax.all_gather(pairs, "zhi")

    mixing = proj.reshape(3, 8, ROWS, 4, CHAN).transpose(2, 0, 1, 3, 4).reshape(ROWS * 3 * OUTS, CHAN)
    heads = jnp.pad(classify, ((0, 0), (0, LANES - 3)))
    heads_t = jnp.pad(classify.T, ((0, LANES - 3), (0, 0)))
    marks = lax.dynamic_index_in_dim(gathered[:, :, SHARD : SHARD + GRID_Q, :UNIT], core, 1, keepdims=False)
    marks = marks.reshape(UNITS // 4, 4, UNIT).transpose(1, 0, 2).reshape(4, HALF // 4)
    marks = lax.dynamic_slice_in_dim(jnp.pad(marks, ((0, 0), (0, (PARTS - USED) * 16))), part * 16, 16, 1)
    onehot = (marks.reshape(64, 1) == jnp.arange(LANES, dtype=BF16)[None, :]).astype(F32)
    kernels, mixing, heads, heads_t, onehot = lax.optimization_barrier(
        (kernels, mixing, heads, heads_t, onehot)
    )

    parity = core.astype(jnp.int32).reshape(1)
    zlo = lax.axis_index("zlo").astype(jnp.int32).reshape(1)
    own, other = forward(parity, zlo, gathered, kernels)
    received = lax.ppermute(other, "core", swap)
    pair = (own.astype(F32) + received.astype(F32)).astype(BF16)

    parts = lax.all_to_all(pair, ("yhi", "row"), 0, 0)
    grads = tail(parts, mixing, heads, heads_t, onehot)
    grads_own = lax.all_to_all(grads, ("yhi", "row"), 0, 0)
    grads_other = lax.ppermute(grads_own, "core", swap)
    partial = gradient(parity, grads_own, grads_other, gathered)
    over_samples = lax.all_to_all(partial, ("zhi", "zlo"), 0, 0)
    summed = jnp.sum(over_samples.astype(F32), axis=0).astype(BF16)
    final = lax.all_to_all(jnp.broadcast_to(summed[None], (ROWS, BLOCK, LANES)), "row", 0, 0)
    return finish(final).reshape(3, 9, 32, CHAN).transpose(2, 0, 1, 3)


def solution(mesh):
    split = Mesh(mesh.devices.reshape(8, 4, 2, 4, 2), ("row", "yhi", "core", "zhi", "zlo"))
    sample, channel = ("zhi", "zlo"), ("yhi", "core")
    in_specs = (
        P(sample, "row", None, channel),
        P(sample, None, None, channel),
        P(),
        P(),
        P(sample, "row", None),
    )
    out_specs = P(sample, None, None, channel)
    return jax.shard_map(shards, mesh=split, in_specs=in_specs, out_specs=out_specs, check_vma=False)
```

```python
import jax
import jax.numpy as jnp
from jax import lax
from jax.experimental import pallas as pl
from jax.experimental.pallas import tpu as pltpu
from jax.sharding import Mesh, PartitionSpec as P

BF16 = jnp.bfloat16
F32 = jnp.float32

ROWS = 8
GRID_J = 4
GRID_Q = 6
UNIT = 72
UNITS = GRID_J * GRID_Q
HALF = UNITS * UNIT
SHARD = 432
SENT = 440
PARTS = 32
USED = 27
SHARE = 48
LANES = 128
CHAN = 256
OUTS = 32
TAPS = 27
ROW_AXES = ("row",)
VMEM_LIMIT = 16 * 1024 * 1024


def block_taps(j, q):
    found = []
    for branch in range(3):
        rate = branch + 1
        for tap_row in range(3):
            out_j = j - rate * (tap_row - 1)
            if not 0 <= out_j < GRID_J:
                continue
            for tap_col in range(3):
                out_q = q - rate * (tap_col - 1)
                if not 0 <= out_q < GRID_Q:
                    continue
                found.append((9 * branch + 3 * tap_row + tap_col, branch, out_j * GRID_Q + out_q))
    return found


def compiler_params(limit=VMEM_LIMIT):
    return pltpu.CompilerParams(vmem_limit_bytes=limit)


def prepare_kernel(
    row_ref,
    features_ref,
    labels_ref,
    weights_ref,
    out_ref,
    mine_ref,
    local_ref,
    marks_ref,
    taps_ref,
    rows_ref,
    units_ref,
    wide_ref,
    packed_ref,
    block_ref,
    sems,
):
    near = weights_ref.at[:, pl.ds(row_ref[0] // 4 * 16, 16), :]
    copies = [
        pltpu.make_async_copy(source, target, sems.at[place])
        for place, (source, target) in enumerate(
            ((features_ref, local_ref), (labels_ref, marks_ref), (near, taps_ref))
        )
    ]
    for copy in copies:
        copy.start()
    units_ref[SHARD:, :] = jnp.zeros((SENT - SHARD, CHAN), F32)
    copies[1].wait()
    for row in range(6):
        for q in range(GRID_Q):
            units_ref[SHARD + q : SHARD + q + 1, row * 12 : row * 12 + 12] = marks_ref[
                row, :, q * 12 : q * 12 + 12
            ].astype(F32)
    copies[0].wait()
    rows_ref[...] = local_ref[...].astype(F32)
    for row in range(6):
        for q in range(GRID_Q):
            units_ref[q * UNIT + row * 12 : q * UNIT + row * 12 + 12, :] = rows_ref[
                row * 72 + q * 12 : row * 72 + q * 12 + 12, :
            ]
    block_ref[...] = units_ref[...].astype(BF16)
    sends = [
        pltpu.make_async_copy(block_ref, out_ref.at[device], sems.at[3 + device]) for device in range(ROWS)
    ]
    for send in sends:
        send.start()
    copies[2].wait()
    for tap in range(TAPS):
        for lanes in range(2):
            wide_ref[lanes, tap * 16 : (tap + 1) * 16, :] = taps_ref[
                tap, :, lanes * LANES : (lanes + 1) * LANES
            ].astype(F32)
    first = row_ref[0] % 4 * 4
    for slot in range(4):
        for lanes in range(2):
            packed_ref[lanes, pl.ds(slot, TAPS, stride=4), :] = wide_ref[
                lanes, pl.ds(first + slot, TAPS, stride=16), :
            ]
    for lanes in range(2):
        mine_ref[:, lanes * LANES : (lanes + 1) * LANES] = packed_ref[lanes].astype(BF16)
    for send in sends:
        send.wait()


def prepare(row, features, labels, weights):
    hbm = pl.BlockSpec(memory_space=pl.ANY)
    vmem = pl.BlockSpec(memory_space=pltpu.VMEM)
    return pl.pallas_call(
        prepare_kernel,
        in_specs=[pl.BlockSpec(memory_space=pltpu.SMEM), hbm, hbm, hbm],
        out_specs=[hbm, vmem],
        out_shape=[
            jax.ShapeDtypeStruct((ROWS, SENT, CHAN), BF16),
            jax.ShapeDtypeStruct((4 * TAPS, CHAN), BF16),
        ],
        scratch_shapes=[
            pltpu.VMEM((SHARD, CHAN), BF16),
            pltpu.VMEM((6, 1, 72), jnp.int32),
            pltpu.VMEM((TAPS, 16, CHAN), BF16),
            pltpu.VMEM((SHARD, CHAN), F32),
            pltpu.VMEM((SENT, CHAN), F32),
            pltpu.VMEM((2, TAPS * 16, LANES), F32),
            pltpu.VMEM((2, 4 * TAPS, LANES), F32),
            pltpu.VMEM((SENT, CHAN), BF16),
            pltpu.SemaphoreType.DMA((3 + ROWS,)),
        ],
        compiler_params=compiler_params(60 * 1024 * 1024),
        cost_estimate=pl.CostEstimate(flops=0, bytes_accessed=2 * 9 * SHARD * CHAN, transcendentals=0),
        name="prepare_blocks",
    )(row, features, labels, weights)


def unit_rows(q):
    return slice(q * UNIT, (q + 1) * UNIT)


def forward_kernel(core_ref, features_ref, weights_ref, own_ref, other_ref, acc_ref, flat_ref):
    acc_ref[...] = jnp.zeros(acc_ref.shape, F32)
    for j in range(GRID_J):
        for q in range(GRID_Q):
            taps = block_taps(j, q)
            kernels = jnp.concatenate(
                [weights_ref[tap * OUTS : (tap + 1) * OUTS, :] for tap, _, _ in taps], axis=0
            )
            pixels = jnp.concatenate(
                [features_ref[j, 0, unit_rows(q), :], features_ref[j, 1, unit_rows(q), :]], axis=0
            )
            product = lax.dot_general(
                kernels, pixels, (((1,), (1,)), ((), ())), preferred_element_type=F32
            )
            for place, (_, branch, block) in enumerate(taps):
                lane = block % 4 * OUTS
                acc_ref[block // 4, branch, lane : lane + OUTS, : 2 * UNIT] += product[
                    place * OUTS : (place + 1) * OUTS, :
                ]
    for group in range(UNITS // 4):
        for branch in range(3):
            turned = jnp.transpose(acc_ref[group, branch])
            for half in range(2):
                flat_ref[half, branch, group * UNIT : (group + 1) * UNIT, :] = turned[
                    half * UNIT : (half + 1) * UNIT, :
                ]
    own = core_ref[0]
    for half, out_ref in ((own, own_ref), (1 - own, other_ref)):
        for part in range(USED):
            for branch in range(3):
                out_ref[part, branch * 16 : (branch + 1) * 16, :] = flat_ref[
                    half, branch, part * 16 : (part + 1) * 16, :
                ].astype(BF16)
        out_ref[USED:] = jnp.zeros((PARTS - USED, SHARE, LANES), BF16)


def forward(core, features, weights):
    whole = pl.BlockSpec(memory_space=pltpu.VMEM)
    return pl.pallas_call(
        forward_kernel,
        in_specs=[pl.BlockSpec(memory_space=pltpu.SMEM), whole, whole],
        out_specs=[whole, whole],
        out_shape=[jax.ShapeDtypeStruct((PARTS, SHARE, LANES), BF16)] * 2,
        scratch_shapes=[
            pltpu.VMEM((UNITS // 4, 3, LANES, 2 * LANES), F32),
            pltpu.VMEM((2, 3, HALF // 4, LANES), F32),
        ],
        compiler_params=compiler_params(),
        cost_estimate=pl.CostEstimate(
            flops=4 * HALF * CHAN * TAPS * OUTS, bytes_accessed=4000000, transcendentals=0
        ),
        name="forward_taps",
    )(core, features, weights)


def sigmoid(values):
    return 1.0 / (1.0 + jnp.exp(-values))


def swish_grad(values, gate_value):
    return gate_value * (1.0 + values * (1.0 - gate_value))


def tail_kernel(parts_ref, proj_ref, classify_ref, classify_t_ref, onehot_ref, out_ref, act_ref, packed_ref):
    pieces = [(row, branch, place) for row in range(ROWS) for branch in range(3) for place in range(4)]

    def packed_at(branch, place):
        return slice(branch * 16, (branch + 1) * 16), slice(place * OUTS, (place + 1) * OUTS)

    def flat_at(row, branch, place):
        start = (row * 3 + branch) * OUTS
        return slice(place * 16, (place + 1) * 16), slice(start, start + OUTS)

    preact, gate = [], []
    for row in range(ROWS):
        total = parts_ref[row].astype(F32)
        for part in range(1, PARTS // ROWS):
            total = total + parts_ref[part * ROWS + row].astype(F32)
        preact.append(total)
        gate.append(sigmoid(total))
        packed_ref[row] = total * gate[row]
    for row, branch, place in pieces:
        at, lanes = packed_at(branch, place)
        act_ref[flat_at(row, branch, place)] = packed_ref[row, at, lanes]
    mixed_pre = jnp.dot(act_ref[...].astype(BF16), proj_ref[...], preferred_element_type=F32)
    mixed_gate = sigmoid(mixed_pre)
    hidden = (mixed_pre * mixed_gate).astype(BF16)
    logits = jnp.dot(hidden, classify_ref[...], preferred_element_type=F32)
    lane = lax.broadcasted_iota(jnp.int32, logits.shape, 1)
    exp_logits = jnp.where(lane < 3, jnp.exp(logits), 0.0)
    probabilities = exp_logits / jnp.sum(exp_logits, axis=1, keepdims=True)
    dlogits = (probabilities - onehot_ref[...]).astype(BF16)
    grad_hidden = jnp.dot(dlogits, classify_t_ref[...], preferred_element_type=F32)
    grad_mixed = (grad_hidden * swish_grad(mixed_pre, mixed_gate)).astype(BF16)
    act_ref[...] = lax.dot_general(
        grad_mixed, proj_ref[...], (((1,), (1,)), ((), ())), preferred_element_type=F32
    )
    for row, branch, place in pieces:
        at, lanes = packed_at(branch, place)
        packed_ref[row, at, lanes] = act_ref[flat_at(row, branch, place)]
    for row in range(ROWS):
        block = (packed_ref[row] * swish_grad(preact[row], gate[row])).astype(BF16)
        for part in range(PARTS // ROWS):
            out_ref[part * ROWS + row] = block


def tail(parts, proj, classify, classify_t, onehot):
    return pl.pallas_call(
        tail_kernel,
        out_shape=jax.ShapeDtypeStruct((PARTS, SHARE, LANES), BF16),
        scratch_shapes=[
            pltpu.VMEM((64, ROWS * 3 * OUTS), F32),
            pltpu.VMEM((ROWS, SHARE, LANES), F32),
        ],
        compiler_params=compiler_params(),
        cost_estimate=pl.CostEstimate(
            flops=4 * 64 * 768 * CHAN, bytes_accessed=1500000, transcendentals=64 * 2000
        ),
        name="tail",
    )(parts, proj, classify, classify_t, onehot)


def gradient_kernel(
    parity_ref, own_ref, other_ref, features_ref, out_ref, flat_ref, turned_ref, acc_ref
):
    own = parity_ref[0]
    flat_ref[:, HALF // 4 :, :] = jnp.zeros((3, LANES - UNIT, LANES), F32)
    for half, grads in enumerate((own_ref, other_ref)):
        for part in range(USED):
            for branch in range(3):
                flat_ref[branch, part * 16 : (part + 1) * 16, :] = grads[
                    part, branch * 16 : (branch + 1) * 16, :
                ].astype(F32)
        for group in range(UNITS // 4):
            for branch in range(3):
                turned = jnp.transpose(flat_ref[branch, group * UNIT : group * UNIT + LANES, :]).astype(BF16)
                for place in range(4):
                    turned_ref[
                        group * 4 + place,
                        branch * OUTS : (branch + 1) * OUTS,
                        half * LANES : (half + 1) * LANES,
                    ] = turned[place * OUTS : (place + 1) * OUTS, :]
    acc_ref[...] = jnp.zeros(acc_ref.shape, F32)
    gap = jnp.zeros((LANES - UNIT, CHAN), BF16)
    for j in range(GRID_J):
        for q in range(GRID_Q):
            taps = block_taps(j, q)
            grads = jnp.concatenate(
                [turned_ref[block, branch * OUTS : (branch + 1) * OUTS, :] for _, branch, block in taps],
                axis=0,
            )
            pixels = jnp.concatenate(
                [features_ref[j, own, unit_rows(q), :], gap, features_ref[j, 1 - own, unit_rows(q), :], gap],
                axis=0,
            )
            product = jnp.dot(grads, pixels, preferred_element_type=F32)
            for place, (tap, _, _) in enumerate(taps):
                acc_ref[tap * OUTS : (tap + 1) * OUTS, :] += product[place * OUTS : (place + 1) * OUTS, :]
    out_ref[...] = acc_ref[...].astype(BF16)


def gradient(parity, own, other, features):
    whole = pl.BlockSpec(memory_space=pltpu.VMEM)
    return pl.pallas_call(
        gradient_kernel,
        in_specs=[pl.BlockSpec(memory_space=pltpu.SMEM), whole, whole, whole],
        out_specs=whole,
        out_shape=jax.ShapeDtypeStruct((TAPS * OUTS, CHAN), BF16),
        scratch_shapes=[
            pltpu.VMEM((3, HALF // 4 + LANES - UNIT, LANES), F32),
            pltpu.VMEM((UNITS, 3 * OUTS, 2 * LANES), BF16),
            pltpu.VMEM((TAPS * OUTS, CHAN), F32),
        ],
        compiler_params=compiler_params(),
        cost_estimate=pl.CostEstimate(
            flops=4 * HALF * CHAN * TAPS * OUTS, bytes_accessed=4000000, transcendentals=0
        ),
        name="gradient_taps",
    )(parity, own, other, features)


def shards(features, weights, proj, classify, labels):
    row = lax.axis_index("row")
    core = lax.axis_index("core")
    part = lax.axis_index("yhi") * ROWS + row
    swap = [(0, 1), (1, 0)]

    sent, mine = prepare(
        row.astype(jnp.int32).reshape(1),
        features.reshape(SHARD, CHAN),
        labels.transpose(1, 0, 2),
        weights.transpose(1, 2, 0, 3).reshape(TAPS, OUTS, CHAN),
    )
    gathered = lax.all_to_all(sent, "row", 0, 0).reshape(GRID_J, 2, SENT, CHAN)
    mine = mine.reshape(TAPS, 4, CHAN)
    theirs = lax.ppermute(mine, "zlo", swap)
    even = lax.axis_index("zlo") == 0
    pairs = jnp.stack([jnp.where(even, mine, theirs), jnp.where(even, theirs, mine)])
    kernels = lax.all_gather(pairs, "zhi").reshape(8, TAPS, 4, CHAN)
    kernels = kernels.transpose(1, 0, 2, 3).reshape(TAPS * OUTS, CHAN)

    mixing = proj.reshape(3, 8, ROWS, 4, CHAN).transpose(2, 0, 1, 3, 4).reshape(ROWS * 3 * OUTS, CHAN)
    heads = jnp.pad(classify, ((0, 0), (0, LANES - 3)))
    heads_t = jnp.pad(classify.T, ((0, LANES - 3), (0, 0)))
    marks = lax.dynamic_index_in_dim(gathered[:, :, SHARD : SHARD + GRID_Q, :UNIT], core, 1, keepdims=False)
    marks = marks.reshape(UNITS // 4, 4, UNIT).transpose(1, 0, 2).reshape(4, HALF // 4)
    marks = lax.dynamic_slice_in_dim(jnp.pad(marks, ((0, 0), (0, (PARTS - USED) * 16))), part * 16, 16, 1)
    onehot = (marks.reshape(64, 1) == jnp.arange(LANES, dtype=BF16)[None, :]).astype(F32)
    kernels, mixing, heads, heads_t, onehot = lax.optimization_barrier(
        (kernels, mixing, heads, heads_t, onehot)
    )

    parity = core.astype(jnp.int32).reshape(1)
    own, other = forward(parity, gathered, kernels)
    received = lax.ppermute(other, "core", swap)
    pair = (own.astype(F32) + received.astype(F32)).astype(BF16)

    parts = lax.all_to_all(pair, ("yhi", "row"), 0, 0)
    grads = tail(parts, mixing, heads, heads_t, onehot)
    grads_own = lax.all_to_all(grads, ("yhi", "row"), 0, 0)
    grads_other = lax.ppermute(grads_own, "core", swap)
    partial = gradient(parity, grads_own, grads_other, gathered)
    partial = partial.reshape(TAPS, 8, 4, CHAN).transpose(1, 0, 2, 3)
    over_samples = lax.all_to_all(partial, ("zhi", "zlo"), 0, 0)
    summed = jnp.sum(over_samples.astype(F32), axis=0).astype(BF16)
    final = lax.all_to_all(jnp.broadcast_to(summed[None], (ROWS, TAPS, 4, CHAN)), "row", 0, 0)
    return final.transpose(0, 2, 1, 3).reshape(OUTS, 3, 9, CHAN)


def solution(mesh):
    split = Mesh(mesh.devices.reshape(8, 4, 2, 4, 2), ("row", "yhi", "core", "zhi", "zlo"))
    sample, channel = ("zhi", "zlo"), ("yhi", "core")
    in_specs = (
        P(sample, "row", None, channel),
        P(sample, None, None, channel),
        P(),
        P(),
        P(sample, "row", None),
    )
    out_specs = P(sample, None, None, channel)
    return jax.shard_map(shards, mesh=split, in_specs=in_specs, out_specs=out_specs, check_vma=False)
```

```python
import jax
import jax.numpy as jnp
from jax import lax
from jax.experimental import pallas as pl
from jax.experimental.pallas import tpu as pltpu
from jax.sharding import Mesh, PartitionSpec as P

BF16 = jnp.bfloat16
F32 = jnp.float32

ROWS = 8
GRID_J = 4
GRID_Q = 6
UNIT = 72
UNITS = GRID_J * GRID_Q
HALF = UNITS * UNIT
SHARD = 432
SENT = 448
PARTS = 32
USED = 27
SHARE = 48
LANES = 128
CHAN = 256
OUTS = 32
TAPS = 27
ROW_AXES = ("row",)
VMEM_LIMIT = 16 * 1024 * 1024


def block_taps(j, q):
    found = []
    for branch in range(3):
        rate = branch + 1
        for tap_row in range(3):
            out_j = j - rate * (tap_row - 1)
            if not 0 <= out_j < GRID_J:
                continue
            for tap_col in range(3):
                out_q = q - rate * (tap_col - 1)
                if not 0 <= out_q < GRID_Q:
                    continue
                found.append((9 * branch + 3 * tap_row + tap_col, branch, out_j * GRID_Q + out_q))
    return found


def compiler_params(limit=VMEM_LIMIT):
    return pltpu.CompilerParams(vmem_limit_bytes=limit)


def prepare_kernel(
    row_ref,
    features_ref,
    labels_ref,
    weights_ref,
    out_ref,
    mine_ref,
    local_ref,
    marks_ref,
    taps_ref,
    rows_ref,
    units_ref,
    wide_ref,
    packed_ref,
    block_ref,
    sems,
):
    near = weights_ref.at[:, pl.ds(row_ref[0] // 4 * 16, 16), :]
    copies = [
        pltpu.make_async_copy(source, target, sems.at[place])
        for place, (source, target) in enumerate(
            ((features_ref, local_ref), (labels_ref, marks_ref), (near, taps_ref))
        )
    ]
    for copy in copies:
        copy.start()
    units_ref[SHARD:, :] = jnp.zeros((SENT - SHARD, CHAN), F32)
    copies[1].wait()
    for row in range(6):
        for q in range(GRID_Q):
            units_ref[SHARD + q : SHARD + q + 1, row * 12 : row * 12 + 12] = marks_ref[
                row, :, q * 12 : q * 12 + 12
            ].astype(F32)
    copies[0].wait()
    rows_ref[...] = local_ref[...].astype(F32)
    for row in range(6):
        for q in range(GRID_Q):
            units_ref[q * UNIT + row * 12 : q * UNIT + row * 12 + 12, :] = rows_ref[
                row * 72 + q * 12 : row * 72 + q * 12 + 12, :
            ]
    block_ref[...] = units_ref[...].astype(BF16)
    sends = [
        pltpu.make_async_copy(block_ref, out_ref.at[device], sems.at[3 + device]) for device in range(ROWS)
    ]
    for send in sends:
        send.start()
    copies[2].wait()
    for tap in range(TAPS):
        for lanes in range(2):
            wide_ref[lanes, tap * 16 : (tap + 1) * 16, :] = taps_ref[
                tap, :, lanes * LANES : (lanes + 1) * LANES
            ].astype(F32)
    first = row_ref[0] % 4 * 4
    for slot in range(4):
        for lanes in range(2):
            packed_ref[lanes, pl.ds(slot, TAPS, stride=4), :] = wide_ref[
                lanes, pl.ds(first + slot, TAPS, stride=16), :
            ]
    for lanes in range(2):
        mine_ref[:, lanes * LANES : (lanes + 1) * LANES] = packed_ref[lanes].astype(BF16)
    for send in sends:
        send.wait()


def prepare(row, features, labels, weights):
    hbm = pl.BlockSpec(memory_space=pl.ANY)
    vmem = pl.BlockSpec(memory_space=pltpu.VMEM)
    return pl.pallas_call(
        prepare_kernel,
        in_specs=[pl.BlockSpec(memory_space=pltpu.SMEM), hbm, hbm, hbm],
        out_specs=[hbm, vmem],
        out_shape=[
            jax.ShapeDtypeStruct((ROWS, SENT, CHAN), BF16),
            jax.ShapeDtypeStruct((4 * TAPS, CHAN), BF16),
        ],
        scratch_shapes=[
            pltpu.VMEM((SHARD, CHAN), BF16),
            pltpu.VMEM((6, 1, 72), jnp.int32),
            pltpu.VMEM((TAPS, 16, CHAN), BF16),
            pltpu.VMEM((SHARD, CHAN), F32),
            pltpu.VMEM((SENT, CHAN), F32),
            pltpu.VMEM((2, TAPS * 16, LANES), F32),
            pltpu.VMEM((2, 4 * TAPS, LANES), F32),
            pltpu.VMEM((SENT, CHAN), BF16),
            pltpu.SemaphoreType.DMA((3 + ROWS,)),
        ],
        compiler_params=compiler_params(60 * 1024 * 1024),
        cost_estimate=pl.CostEstimate(flops=0, bytes_accessed=2 * 9 * SHARD * CHAN, transcendentals=0),
        name="prepare_blocks",
    )(row, features, labels, weights)


def unit(features_ref, j, parity, q):
    pair = features_ref[j, parity, q // 2 * 2 * UNIT : (q // 2 + 1) * 2 * UNIT, :]
    return pair[q % 2 * UNIT : (q % 2 + 1) * UNIT, :]


def forward_kernel(core_ref, features_ref, weights_ref, own_ref, other_ref, acc_ref, flat_ref):
    written = set()
    for j in range(GRID_J):
        for q in range(GRID_Q):
            taps = block_taps(j, q)
            kernels = jnp.concatenate(
                [weights_ref[tap * OUTS : (tap + 1) * OUTS, :] for tap, _, _ in taps], axis=0
            )
            pixels = jnp.concatenate(
                [unit(features_ref, j, 0, q), unit(features_ref, j, 1, q)], axis=0
            )
            product = lax.dot_general(
                kernels, pixels, (((1,), (1,)), ((), ())), preferred_element_type=F32
            )
            for place, (_, branch, block) in enumerate(taps):
                at = (block // 4, branch, slice(block % 4 * OUTS, (block % 4 + 1) * OUTS), slice(2 * UNIT))
                term = product[place * OUTS : (place + 1) * OUTS, :]
                acc_ref[at] = acc_ref[at] + term if (branch, block) in written else term
                written.add((branch, block))
    for group in range(UNITS // 4):
        for branch in range(3):
            turned = jnp.transpose(acc_ref[group, branch])
            for half in range(2):
                flat_ref[half, branch, group * UNIT : (group + 1) * UNIT, :] = turned[
                    half * UNIT : (half + 1) * UNIT, :
                ]
    own = core_ref[0]
    for half, out_ref in ((own, own_ref), (1 - own, other_ref)):
        for part in range(USED):
            for branch in range(3):
                out_ref[part, branch * 16 : (branch + 1) * 16, :] = flat_ref[
                    half, branch, part * 16 : (part + 1) * 16, :
                ].astype(BF16)
        out_ref[USED:] = jnp.zeros((PARTS - USED, SHARE, LANES), BF16)


def forward(core, features, weights):
    whole = pl.BlockSpec(memory_space=pltpu.VMEM)
    return pl.pallas_call(
        forward_kernel,
        in_specs=[pl.BlockSpec(memory_space=pltpu.SMEM), whole, whole],
        out_specs=[whole, whole],
        out_shape=[jax.ShapeDtypeStruct((PARTS, SHARE, LANES), BF16)] * 2,
        scratch_shapes=[
            pltpu.VMEM((UNITS // 4, 3, LANES, 2 * LANES), F32),
            pltpu.VMEM((2, 3, HALF // 4, LANES), F32),
        ],
        compiler_params=compiler_params(),
        cost_estimate=pl.CostEstimate(
            flops=4 * HALF * CHAN * TAPS * OUTS, bytes_accessed=4000000, transcendentals=0
        ),
        name="forward_taps",
    )(core, features, weights)


def sigmoid(values):
    return 1.0 / (1.0 + jnp.exp(-values))


def swish_grad(values, gate_value):
    return gate_value * (1.0 + values * (1.0 - gate_value))


def tail_kernel(parts_ref, proj_ref, classify_ref, classify_t_ref, onehot_ref, out_ref, act_ref, packed_ref):
    pieces = [(row, branch, place) for row in range(ROWS) for branch in range(3) for place in range(4)]

    def packed_at(branch, place):
        return slice(branch * 16, (branch + 1) * 16), slice(place * OUTS, (place + 1) * OUTS)

    def flat_at(row, branch, place):
        start = (row * 3 + branch) * OUTS
        return slice(place * 16, (place + 1) * 16), slice(start, start + OUTS)

    preact, gate = [], []
    for row in range(ROWS):
        total = parts_ref[row].astype(F32)
        for part in range(1, PARTS // ROWS):
            total = total + parts_ref[part * ROWS + row].astype(F32)
        preact.append(total)
        gate.append(sigmoid(total))
        packed_ref[row] = total * gate[row]
    for row, branch, place in pieces:
        at, lanes = packed_at(branch, place)
        act_ref[flat_at(row, branch, place)] = packed_ref[row, at, lanes]
    mixed_pre = jnp.dot(act_ref[...].astype(BF16), proj_ref[...], preferred_element_type=F32)
    mixed_gate = sigmoid(mixed_pre)
    hidden = (mixed_pre * mixed_gate).astype(BF16)
    logits = jnp.dot(hidden, classify_ref[...], preferred_element_type=F32)
    lane = lax.broadcasted_iota(jnp.int32, logits.shape, 1)
    exp_logits = jnp.where(lane < 3, jnp.exp(logits), 0.0)
    probabilities = exp_logits / jnp.sum(exp_logits, axis=1, keepdims=True)
    dlogits = (probabilities - onehot_ref[...]).astype(BF16)
    grad_hidden = jnp.dot(dlogits, classify_t_ref[...], preferred_element_type=F32)
    grad_mixed = (grad_hidden * swish_grad(mixed_pre, mixed_gate)).astype(BF16)
    act_ref[...] = lax.dot_general(
        grad_mixed, proj_ref[...], (((1,), (1,)), ((), ())), preferred_element_type=F32
    )
    for row, branch, place in pieces:
        at, lanes = packed_at(branch, place)
        packed_ref[row, at, lanes] = act_ref[flat_at(row, branch, place)]
    for row in range(ROWS):
        block = (packed_ref[row] * swish_grad(preact[row], gate[row])).astype(BF16)
        for part in range(PARTS // ROWS):
            out_ref[part * ROWS + row] = block


def tail(parts, proj, classify, classify_t, onehot):
    return pl.pallas_call(
        tail_kernel,
        out_shape=jax.ShapeDtypeStruct((PARTS, SHARE, LANES), BF16),
        scratch_shapes=[
            pltpu.VMEM((64, ROWS * 3 * OUTS), F32),
            pltpu.VMEM((ROWS, SHARE, LANES), F32),
        ],
        compiler_params=compiler_params(),
        cost_estimate=pl.CostEstimate(
            flops=4 * 64 * 768 * CHAN, bytes_accessed=1500000, transcendentals=64 * 2000
        ),
        name="tail",
    )(parts, proj, classify, classify_t, onehot)


def gradient_kernel(
    parity_ref, own_ref, other_ref, features_ref, out_ref, flat_ref, turned_ref, acc_ref
):
    own = parity_ref[0]
    flat_ref[:, HALF // 4 :, :] = jnp.zeros((3, LANES - UNIT, LANES), F32)
    for half, grads in enumerate((own_ref, other_ref)):
        for part in range(USED):
            for branch in range(3):
                flat_ref[branch, part * 16 : (part + 1) * 16, :] = grads[
                    part, branch * 16 : (branch + 1) * 16, :
                ].astype(F32)
        for group in range(UNITS // 4):
            for branch in range(3):
                turned = jnp.transpose(flat_ref[branch, group * UNIT : group * UNIT + LANES, :]).astype(BF16)
                for place in range(4):
                    turned_ref[
                        group * 4 + place,
                        branch * OUTS : (branch + 1) * OUTS,
                        half * LANES : (half + 1) * LANES,
                    ] = turned[place * OUTS : (place + 1) * OUTS, :]
    written = set()
    gap = jnp.zeros((LANES - UNIT, CHAN), BF16)
    for j in range(GRID_J):
        for q in range(GRID_Q):
            taps = block_taps(j, q)
            grads = jnp.concatenate(
                [turned_ref[block, branch * OUTS : (branch + 1) * OUTS, :] for _, branch, block in taps],
                axis=0,
            )
            pixels = jnp.concatenate(
                [unit(features_ref, j, own, q), gap, unit(features_ref, j, 1 - own, q), gap], axis=0
            )
            product = jnp.dot(grads, pixels, preferred_element_type=F32)
            for place, (tap, _, _) in enumerate(taps):
                at = slice(tap * OUTS, (tap + 1) * OUTS)
                term = product[place * OUTS : (place + 1) * OUTS, :]
                acc_ref[at, :] = acc_ref[at, :] + term if tap in written else term
                written.add(tap)
    out_ref[...] = acc_ref[...].astype(BF16)


def gradient(parity, own, other, features):
    whole = pl.BlockSpec(memory_space=pltpu.VMEM)
    return pl.pallas_call(
        gradient_kernel,
        in_specs=[pl.BlockSpec(memory_space=pltpu.SMEM), whole, whole, whole],
        out_specs=whole,
        out_shape=jax.ShapeDtypeStruct((TAPS * OUTS, CHAN), BF16),
        scratch_shapes=[
            pltpu.VMEM((3, HALF // 4 + LANES - UNIT, LANES), F32),
            pltpu.VMEM((UNITS, 3 * OUTS, 2 * LANES), BF16),
            pltpu.VMEM((TAPS * OUTS, CHAN), F32),
        ],
        compiler_params=compiler_params(),
        cost_estimate=pl.CostEstimate(
            flops=4 * HALF * CHAN * TAPS * OUTS, bytes_accessed=4000000, transcendentals=0
        ),
        name="gradient_taps",
    )(parity, own, other, features)


def shards(features, weights, proj, classify, labels):
    row = lax.axis_index("row")
    core = lax.axis_index("core")
    part = lax.axis_index("yhi") * ROWS + row
    swap = [(0, 1), (1, 0)]

    sent, mine = prepare(
        row.astype(jnp.int32).reshape(1),
        features.reshape(SHARD, CHAN),
        labels.transpose(1, 0, 2),
        weights.transpose(1, 2, 0, 3).reshape(TAPS, OUTS, CHAN),
    )
    gathered = lax.all_to_all(sent, "row", 0, 0).reshape(GRID_J, 2, SENT, CHAN)
    mine = mine.reshape(TAPS, 4, CHAN)
    theirs = lax.ppermute(mine, "zlo", swap)
    even = lax.axis_index("zlo") == 0
    pairs = jnp.stack([jnp.where(even, mine, theirs), jnp.where(even, theirs, mine)])
    kernels = lax.all_gather(pairs, "zhi").reshape(8, TAPS, 4, CHAN)
    kernels = kernels.transpose(1, 0, 2, 3).reshape(TAPS * OUTS, CHAN)

    mixing = proj.reshape(3, 8, ROWS, 4, CHAN).transpose(2, 0, 1, 3, 4).reshape(ROWS * 3 * OUTS, CHAN)
    heads = jnp.pad(classify, ((0, 0), (0, LANES - 3)))
    heads_t = jnp.pad(classify.T, ((0, LANES - 3), (0, 0)))
    marks = lax.dynamic_index_in_dim(gathered[:, :, SHARD : SHARD + GRID_Q, :UNIT], core, 1, keepdims=False)
    marks = marks.reshape(UNITS // 4, 4, UNIT).transpose(1, 0, 2).reshape(4, HALF // 4)
    marks = lax.dynamic_slice_in_dim(jnp.pad(marks, ((0, 0), (0, (PARTS - USED) * 16))), part * 16, 16, 1)
    onehot = (marks.reshape(64, 1) == jnp.arange(LANES, dtype=BF16)[None, :]).astype(F32)
    kernels, mixing, heads, heads_t, onehot = lax.optimization_barrier(
        (kernels, mixing, heads, heads_t, onehot)
    )

    parity = core.astype(jnp.int32).reshape(1)
    own, other = forward(parity, gathered, kernels)
    received = lax.ppermute(other, "core", swap)
    pair = (own.astype(F32) + received.astype(F32)).astype(BF16)

    parts = lax.all_to_all(pair, ("yhi", "row"), 0, 0)
    grads = tail(parts, mixing, heads, heads_t, onehot)
    grads_own = lax.all_to_all(grads, ("yhi", "row"), 0, 0)
    grads_other = lax.ppermute(grads_own, "core", swap)
    partial = gradient(parity, grads_own, grads_other, gathered)
    partial = partial.reshape(TAPS, 8, 4, CHAN).transpose(1, 0, 2, 3)
    over_samples = lax.all_to_all(partial, ("zhi", "zlo"), 0, 0)
    summed = jnp.sum(over_samples.astype(F32), axis=0).astype(BF16)
    final = lax.all_to_all(jnp.broadcast_to(summed[None], (ROWS, TAPS, 4, CHAN)), "row", 0, 0)
    return final.transpose(0, 2, 1, 3).reshape(OUTS, 3, 9, CHAN)


def solution(mesh):
    split = Mesh(mesh.devices.reshape(8, 4, 2, 4, 2), ("row", "yhi", "core", "zhi", "zlo"))
    sample, channel = ("zhi", "zlo"), ("yhi", "core")
    in_specs = (
        P(sample, "row", None, channel),
        P(sample, None, None, channel),
        P(),
        P(),
        P(sample, "row", None),
    )
    out_specs = P(sample, None, None, channel)
    return jax.shard_map(shards, mesh=split, in_specs=in_specs, out_specs=out_specs, check_vma=False)
```

```python
import jax
import jax.numpy as jnp
from jax import lax
from jax.experimental import pallas as pl
from jax.experimental.pallas import tpu as pltpu
from jax.sharding import Mesh, PartitionSpec as P

BF16 = jnp.bfloat16
F32 = jnp.float32

ROWS = 8
GRID_J = 4
GRID_Q = 6
UNIT = 72
UNITS = GRID_J * GRID_Q
HALF = UNITS * UNIT
SHARD = 432
SENT = 448
PARTS = 32
USED = 27
SHARE = 48
LANES = 128
CHAN = 256
OUTS = 32
TAPS = 27
KEPT = 112
ROW_AXES = ("row",)
VMEM_LIMIT = 16 * 1024 * 1024


def block_taps(j, q):
    found = []
    for branch in range(3):
        rate = branch + 1
        for tap_row in range(3):
            out_j = j - rate * (tap_row - 1)
            if not 0 <= out_j < GRID_J:
                continue
            for tap_col in range(3):
                out_q = q - rate * (tap_col - 1)
                if not 0 <= out_q < GRID_Q:
                    continue
                found.append((9 * branch + 3 * tap_row + tap_col, branch, out_j * GRID_Q + out_q))
    return found


def compiler_params(limit=VMEM_LIMIT):
    return pltpu.CompilerParams(vmem_limit_bytes=limit)


def prepare_kernel(
    row_ref,
    features_ref,
    labels_ref,
    weights_ref,
    out_ref,
    mine_ref,
    local_ref,
    marks_ref,
    taps_ref,
    rows_ref,
    units_ref,
    block_ref,
    kept_ref,
    sems,
):
    near = weights_ref.at[:, pl.ds(row_ref[0] // 4 * 16, 16), :]
    copies = [
        pltpu.make_async_copy(source, target, sems.at[place])
        for place, (source, target) in enumerate(
            ((features_ref, local_ref), (labels_ref, marks_ref), (near, taps_ref))
        )
    ]
    for copy in (copies[2], copies[0], copies[1]):
        copy.start()
    units_ref[SHARD:, :] = jnp.zeros((SENT - SHARD, CHAN), F32)
    copies[1].wait()
    for row in range(6):
        for q in range(GRID_Q):
            units_ref[SHARD + q : SHARD + q + 1, row * 12 : row * 12 + 12] = marks_ref[
                row, :, q * 12 : q * 12 + 12
            ].astype(F32)
    copies[0].wait()
    rows_ref[...] = local_ref[...].astype(F32)
    for row in range(6):
        for q in range(GRID_Q):
            units_ref[q * UNIT + row * 12 : q * UNIT + row * 12 + 12, :] = rows_ref[
                row * 72 + q * 12 : row * 72 + q * 12 + 12, :
            ]
    block_ref[...] = units_ref[...].astype(BF16)
    sends = [
        pltpu.make_async_copy(block_ref, out_ref.at[device], sems.at[3 + device]) for device in range(ROWS)
    ]
    for send in sends:
        send.start()
    copies[2].wait()
    picked = lax.broadcasted_iota(jnp.int32, (KEPT, 16 * TAPS), 0)
    column = lax.broadcasted_iota(jnp.int32, (KEPT, 16 * TAPS), 1)
    wanted = picked // 4 * 16 + picked % 4 + row_ref[0] % 4 * 4
    picks = jnp.where(column == wanted, 1.0, 0.0).astype(BF16)
    near_rows = taps_ref[...].reshape(16 * TAPS, CHAN)
    kept_ref[...] = jnp.dot(picks, near_rows, preferred_element_type=F32).astype(BF16)
    sends.append(pltpu.make_async_copy(kept_ref, mine_ref, sems.at[3 + ROWS]))
    sends[-1].start()
    for send in sends:
        send.wait()


def prepare(row, features, labels, weights):
    hbm = pl.BlockSpec(memory_space=pl.ANY)
    return pl.pallas_call(
        prepare_kernel,
        in_specs=[pl.BlockSpec(memory_space=pltpu.SMEM), hbm, hbm, hbm],
        out_specs=[hbm, hbm],
        out_shape=[
            jax.ShapeDtypeStruct((ROWS, SENT, CHAN), BF16),
            jax.ShapeDtypeStruct((KEPT, CHAN), BF16),
        ],
        scratch_shapes=[
            pltpu.VMEM((SHARD, CHAN), BF16),
            pltpu.VMEM((6, 1, 72), jnp.int32),
            pltpu.VMEM((TAPS, 16, CHAN), BF16),
            pltpu.VMEM((SHARD, CHAN), F32),
            pltpu.VMEM((SENT, CHAN), F32),
            pltpu.VMEM((SENT, CHAN), BF16),
            pltpu.VMEM((KEPT, CHAN), BF16),
            pltpu.SemaphoreType.DMA((4 + ROWS,)),
        ],
        compiler_params=compiler_params(60 * 1024 * 1024),
        cost_estimate=pl.CostEstimate(flops=0, bytes_accessed=2 * 9 * SHARD * CHAN, transcendentals=0),
        name="prepare_blocks",
    )(row, features, labels, weights)


def unit(features_ref, j, parity, q):
    pair = features_ref[j, parity, q // 2 * 2 * UNIT : (q // 2 + 1) * 2 * UNIT, :]
    return pair[q % 2 * UNIT : (q % 2 + 1) * UNIT, :]


def forward_kernel(core_ref, features_ref, weights_ref, own_ref, other_ref, acc_ref, flat_ref):
    written = set()
    for j in range(GRID_J):
        for q in range(GRID_Q):
            taps = block_taps(j, q)
            kernels = jnp.concatenate(
                [weights_ref[tap * OUTS : (tap + 1) * OUTS, :] for tap, _, _ in taps], axis=0
            )
            pixels = jnp.concatenate(
                [unit(features_ref, j, 0, q), unit(features_ref, j, 1, q)], axis=0
            )
            product = lax.dot_general(
                kernels, pixels, (((1,), (1,)), ((), ())), preferred_element_type=F32
            )
            for place, (_, branch, block) in enumerate(taps):
                at = (block // 4, branch, slice(block % 4 * OUTS, (block % 4 + 1) * OUTS), slice(2 * UNIT))
                term = product[place * OUTS : (place + 1) * OUTS, :]
                acc_ref[at] = acc_ref[at] + term if (branch, block) in written else term
                written.add((branch, block))
    for group in range(UNITS // 4):
        for branch in range(3):
            turned = jnp.transpose(acc_ref[group, branch])
            for half in range(2):
                flat_ref[half, branch, group * UNIT : (group + 1) * UNIT, :] = turned[
                    half * UNIT : (half + 1) * UNIT, :
                ]
    own = core_ref[0]
    for half, out_ref in ((own, own_ref), (1 - own, other_ref)):
        for part in range(USED):
            for branch in range(3):
                out_ref[part, branch * 16 : (branch + 1) * 16, :] = flat_ref[
                    half, branch, part * 16 : (part + 1) * 16, :
                ].astype(BF16)
        out_ref[USED:] = jnp.zeros((PARTS - USED, SHARE, LANES), BF16)


def forward(core, features, weights):
    whole = pl.BlockSpec(memory_space=pltpu.VMEM)
    return pl.pallas_call(
        forward_kernel,
        in_specs=[pl.BlockSpec(memory_space=pltpu.SMEM), whole, whole],
        out_specs=[whole, whole],
        out_shape=[jax.ShapeDtypeStruct((PARTS, SHARE, LANES), BF16)] * 2,
        scratch_shapes=[
            pltpu.VMEM((UNITS // 4, 3, LANES, 2 * LANES), F32),
            pltpu.VMEM((2, 3, HALF // 4, LANES), F32),
        ],
        compiler_params=compiler_params(),
        cost_estimate=pl.CostEstimate(
            flops=4 * HALF * CHAN * TAPS * OUTS, bytes_accessed=4000000, transcendentals=0
        ),
        name="forward_taps",
    )(core, features, weights)


def sigmoid(values):
    return 1.0 / (1.0 + jnp.exp(-values))


def swish_grad(values, gate_value):
    return gate_value * (1.0 + values * (1.0 - gate_value))


def own_labels(part, marks):
    first = part * 16
    group = first // UNIT
    pixel = lax.broadcasted_iota(jnp.int32, (64, UNITS), 0)
    spot = first - group * UNIT + pixel % 16
    units = (group + jnp.where(spot >= UNIT, 1, 0)) * 4 + pixel // 16
    chosen = (units == lax.broadcasted_iota(jnp.int32, (64, UNITS), 1)).astype(BF16)
    rows = jnp.dot(chosen, marks, preferred_element_type=F32)
    pixel = lax.broadcasted_iota(jnp.int32, (64, UNIT), 0)
    spot = first - group * UNIT + pixel % 16
    spot = jnp.where(spot >= UNIT, spot - UNIT, spot)
    here = lax.broadcasted_iota(jnp.int32, (64, UNIT), 1) == spot
    return jnp.sum(jnp.where(here, rows, 0.0), axis=1, keepdims=True)


def tail_kernel(
    part_ref, parts_ref, proj_ref, classify_ref, classify_t_ref, marks_ref, out_ref, act_ref, packed_ref
):
    pieces = [(row, branch, place) for row in range(ROWS) for branch in range(3) for place in range(4)]

    def packed_at(branch, place):
        return slice(branch * 16, (branch + 1) * 16), slice(place * OUTS, (place + 1) * OUTS)

    def flat_at(row, branch, place):
        start = (row * 3 + branch) * OUTS
        return slice(place * 16, (place + 1) * 16), slice(start, start + OUTS)

    preact, gate = [], []
    for row in range(ROWS):
        total = parts_ref[row].astype(F32)
        for part in range(1, PARTS // ROWS):
            total = total + parts_ref[part * ROWS + row].astype(F32)
        preact.append(total)
        gate.append(sigmoid(total))
        packed_ref[row] = total * gate[row]
    for row, branch, place in pieces:
        at, lanes = packed_at(branch, place)
        act_ref[flat_at(row, branch, place)] = packed_ref[row, at, lanes]
    mixed_pre = jnp.dot(act_ref[...].astype(BF16), proj_ref[...], preferred_element_type=F32)
    mixed_gate = sigmoid(mixed_pre)
    hidden = (mixed_pre * mixed_gate).astype(BF16)
    logits = jnp.dot(hidden, classify_ref[...], preferred_element_type=F32)
    lane = lax.broadcasted_iota(jnp.int32, logits.shape, 1)
    exp_logits = jnp.where(lane < 3, jnp.exp(logits), 0.0)
    probabilities = exp_logits / jnp.sum(exp_logits, axis=1, keepdims=True)
    onehot = jnp.where(lane.astype(F32) == own_labels(part_ref[0], marks_ref[...]), 1.0, 0.0)
    dlogits = (probabilities - onehot).astype(BF16)
    grad_hidden = jnp.dot(dlogits, classify_t_ref[...], preferred_element_type=F32)
    grad_mixed = (grad_hidden * swish_grad(mixed_pre, mixed_gate)).astype(BF16)
    act_ref[...] = lax.dot_general(
        grad_mixed, proj_ref[...], (((1,), (1,)), ((), ())), preferred_element_type=F32
    )
    for row, branch, place in pieces:
        at, lanes = packed_at(branch, place)
        packed_ref[row, at, lanes] = act_ref[flat_at(row, branch, place)]
    for row in range(ROWS):
        block = (packed_ref[row] * swish_grad(preact[row], gate[row])).astype(BF16)
        for part in range(PARTS // ROWS):
            out_ref[part * ROWS + row] = block


def tail(part, parts, proj, classify, classify_t, marks):
    whole = pl.BlockSpec(memory_space=pltpu.VMEM)
    return pl.pallas_call(
        tail_kernel,
        in_specs=[pl.BlockSpec(memory_space=pltpu.SMEM)] + [whole] * 5,
        out_specs=whole,
        out_shape=jax.ShapeDtypeStruct((PARTS, SHARE, LANES), BF16),
        scratch_shapes=[
            pltpu.VMEM((64, ROWS * 3 * OUTS), F32),
            pltpu.VMEM((ROWS, SHARE, LANES), F32),
        ],
        compiler_params=compiler_params(),
        cost_estimate=pl.CostEstimate(
            flops=4 * 64 * 768 * CHAN, bytes_accessed=1500000, transcendentals=64 * 2000
        ),
        name="tail",
    )(part, parts, proj, classify, classify_t, marks)


def gradient_kernel(
    parity_ref, own_ref, other_ref, features_ref, out_ref, flat_ref, turned_ref, acc_ref
):
    own = parity_ref[0]
    flat_ref[:, HALF // 4 :, :] = jnp.zeros((3, LANES - UNIT, LANES), F32)
    for half, grads in enumerate((own_ref, other_ref)):
        for part in range(USED):
            for branch in range(3):
                flat_ref[branch, part * 16 : (part + 1) * 16, :] = grads[
                    part, branch * 16 : (branch + 1) * 16, :
                ].astype(F32)
        for group in range(UNITS // 4):
            for branch in range(3):
                turned = jnp.transpose(flat_ref[branch, group * UNIT : group * UNIT + LANES, :]).astype(BF16)
                for place in range(4):
                    turned_ref[
                        group * 4 + place,
                        branch * OUTS : (branch + 1) * OUTS,
                        half * LANES : (half + 1) * LANES,
                    ] = turned[place * OUTS : (place + 1) * OUTS, :]
    written = set()
    gap = jnp.zeros((LANES - UNIT, CHAN), BF16)
    for j in range(GRID_J):
        for q in range(GRID_Q):
            taps = block_taps(j, q)
            grads = jnp.concatenate(
                [turned_ref[block, branch * OUTS : (branch + 1) * OUTS, :] for _, branch, block in taps],
                axis=0,
            )
            pixels = jnp.concatenate(
                [unit(features_ref, j, own, q), gap, unit(features_ref, j, 1 - own, q), gap], axis=0
            )
            product = jnp.dot(grads, pixels, preferred_element_type=F32)
            for place, (tap, _, _) in enumerate(taps):
                at = slice(tap * OUTS, (tap + 1) * OUTS)
                term = product[place * OUTS : (place + 1) * OUTS, :]
                acc_ref[at, :] = acc_ref[at, :] + term if tap in written else term
                written.add(tap)
    out_ref[...] = acc_ref[...].astype(BF16)


def gradient(parity, own, other, features):
    whole = pl.BlockSpec(memory_space=pltpu.VMEM)
    return pl.pallas_call(
        gradient_kernel,
        in_specs=[pl.BlockSpec(memory_space=pltpu.SMEM), whole, whole, whole],
        out_specs=whole,
        out_shape=jax.ShapeDtypeStruct((TAPS * OUTS, CHAN), BF16),
        scratch_shapes=[
            pltpu.VMEM((3, HALF // 4 + LANES - UNIT, LANES), F32),
            pltpu.VMEM((UNITS, 3 * OUTS, 2 * LANES), BF16),
            pltpu.VMEM((TAPS * OUTS, CHAN), F32),
        ],
        compiler_params=compiler_params(),
        cost_estimate=pl.CostEstimate(
            flops=4 * HALF * CHAN * TAPS * OUTS, bytes_accessed=4000000, transcendentals=0
        ),
        name="gradient_taps",
    )(parity, own, other, features)


def shards(features, weights, proj, classify, labels):
    row = lax.axis_index("row")
    core = lax.axis_index("core")
    part = lax.axis_index("yhi") * ROWS + row
    swap = [(0, 1), (1, 0)]

    sent, mine = prepare(
        row.astype(jnp.int32).reshape(1),
        features.reshape(SHARD, CHAN),
        labels.transpose(1, 0, 2),
        weights.transpose(1, 2, 0, 3).reshape(TAPS, OUTS, CHAN),
    )
    gathered = lax.all_to_all(sent, "row", 0, 0).reshape(GRID_J, 2, SENT, CHAN)
    mine = mine[: 4 * TAPS].reshape(TAPS, 4, CHAN)
    theirs = lax.ppermute(mine, "zlo", swap)
    even = lax.axis_index("zlo") == 0
    pairs = jnp.stack([jnp.where(even, mine, theirs), jnp.where(even, theirs, mine)])
    kernels = lax.all_gather(pairs, "zhi").reshape(8, TAPS, 4, CHAN)
    kernels = kernels.transpose(1, 0, 2, 3).reshape(TAPS * OUTS, CHAN)

    mixing = proj.reshape(3, 8, ROWS, 4, CHAN).transpose(2, 0, 1, 3, 4).reshape(ROWS * 3 * OUTS, CHAN)
    heads = jnp.pad(classify, ((0, 0), (0, LANES - 3)))
    heads_t = jnp.pad(classify.T, ((0, LANES - 3), (0, 0)))
    marks = lax.dynamic_index_in_dim(gathered[:, :, SHARD : SHARD + GRID_Q, :UNIT], core, 1, keepdims=False)
    marks = marks.reshape(UNITS, UNIT)
    part = part.astype(jnp.int32).reshape(1)
    kernels, mixing, heads, heads_t, marks, part = lax.optimization_barrier(
        (kernels, mixing, heads, heads_t, marks, part)
    )

    parity = core.astype(jnp.int32).reshape(1)
    own, other = forward(parity, gathered, kernels)
    received = lax.ppermute(other, "core", swap)
    pair = (own.astype(F32) + received.astype(F32)).astype(BF16)

    parts = lax.all_to_all(pair, ("yhi", "row"), 0, 0)
    grads = tail(part, parts, mixing, heads, heads_t, marks)
    grads_own = lax.all_to_all(grads, ("yhi", "row"), 0, 0)
    grads_other = lax.ppermute(grads_own, "core", swap)
    partial = gradient(parity, grads_own, grads_other, gathered)
    partial = partial.reshape(TAPS, 8, 4, CHAN).transpose(1, 0, 2, 3)
    over_samples = lax.all_to_all(partial, ("zhi", "zlo"), 0, 0)
    summed = jnp.sum(over_samples.astype(F32), axis=0).astype(BF16)
    final = lax.all_to_all(jnp.broadcast_to(summed[None], (ROWS, TAPS, 4, CHAN)), "row", 0, 0)
    return final.transpose(0, 2, 1, 3).reshape(OUTS, 3, 9, CHAN)


def solution(mesh):
    split = Mesh(mesh.devices.reshape(8, 4, 2, 4, 2), ("row", "yhi", "core", "zhi", "zlo"))
    sample, channel = ("zhi", "zlo"), ("yhi", "core")
    in_specs = (
        P(sample, "row", None, channel),
        P(sample, None, None, channel),
        P(),
        P(),
        P(sample, "row", None),
    )
    out_specs = P(sample, None, None, channel)
    return jax.shard_map(shards, mesh=split, in_specs=in_specs, out_specs=out_specs, check_vma=False)
```

```python
import jax
import jax.numpy as jnp
from jax import lax
from jax.experimental import pallas as pl
from jax.experimental.pallas import tpu as pltpu
from jax.sharding import Mesh, PartitionSpec as P

BF16 = jnp.bfloat16
F32 = jnp.float32

ROWS = 8
GRID_J = 4
GRID_Q = 6
UNIT = 72
UNITS = GRID_J * GRID_Q
HALF = UNITS * UNIT
SHARD = 432
SENT = 440
PARTS = 32
USED = 27
SHARE = 48
LANES = 128
CHAN = 256
OUTS = 32
TAPS = 27
KEPT = 112
ROW_AXES = ("row",)
VMEM_LIMIT = 16 * 1024 * 1024


def block_taps(j, q):
    found = []
    for branch in range(3):
        rate = branch + 1
        for tap_row in range(3):
            out_j = j - rate * (tap_row - 1)
            if not 0 <= out_j < GRID_J:
                continue
            for tap_col in range(3):
                out_q = q - rate * (tap_col - 1)
                if not 0 <= out_q < GRID_Q:
                    continue
                found.append((9 * branch + 3 * tap_row + tap_col, branch, out_j * GRID_Q + out_q))
    return found


def compiler_params(limit=VMEM_LIMIT):
    return pltpu.CompilerParams(vmem_limit_bytes=limit)


def prepare_kernel(
    row_ref,
    features_ref,
    labels_ref,
    weights_ref,
    out_ref,
    mine_ref,
    local_ref,
    marks_ref,
    taps_ref,
    rows_ref,
    units_ref,
    block_ref,
    kept_ref,
    sems,
):
    near = weights_ref.at[:, pl.ds(row_ref[0] // 4 * 16, 16), :]
    copies = [
        pltpu.make_async_copy(source, target, sems.at[place])
        for place, (source, target) in enumerate(
            ((features_ref, local_ref), (labels_ref, marks_ref), (near, taps_ref))
        )
    ]
    for copy in (copies[2], copies[0], copies[1]):
        copy.start()
    units_ref[SHARD:, :] = jnp.zeros((SENT - SHARD, CHAN), F32)
    copies[1].wait()
    for row in range(6):
        for q in range(GRID_Q):
            units_ref[SHARD + q : SHARD + q + 1, row * 12 : row * 12 + 12] = marks_ref[
                row, :, q * 12 : q * 12 + 12
            ].astype(F32)
    copies[0].wait()
    rows_ref[...] = local_ref[...].astype(F32)
    for row in range(6):
        for q in range(GRID_Q):
            units_ref[q * UNIT + row * 12 : q * UNIT + row * 12 + 12, :] = rows_ref[
                row * 72 + q * 12 : row * 72 + q * 12 + 12, :
            ]
    block_ref[...] = units_ref[...].astype(BF16)
    sends = [
        pltpu.make_async_copy(block_ref, out_ref.at[device], sems.at[3 + device]) for device in range(ROWS)
    ]
    for send in sends:
        send.start()
    copies[2].wait()
    picked = lax.broadcasted_iota(jnp.int32, (KEPT, 16 * TAPS), 0)
    column = lax.broadcasted_iota(jnp.int32, (KEPT, 16 * TAPS), 1)
    wanted = picked // 4 * 16 + picked % 4 + row_ref[0] % 4 * 4
    picks = jnp.where(column == wanted, 1.0, 0.0).astype(BF16)
    near_rows = taps_ref[...].reshape(16 * TAPS, CHAN)
    kept_ref[...] = jnp.dot(picks, near_rows, preferred_element_type=F32).astype(BF16)
    sends.append(pltpu.make_async_copy(kept_ref, mine_ref, sems.at[3 + ROWS]))
    sends[-1].start()
    for send in sends:
        send.wait()


def prepare(row, features, labels, weights):
    hbm = pl.BlockSpec(memory_space=pl.ANY)
    return pl.pallas_call(
        prepare_kernel,
        in_specs=[pl.BlockSpec(memory_space=pltpu.SMEM), hbm, hbm, hbm],
        out_specs=[hbm, hbm],
        out_shape=[
            jax.ShapeDtypeStruct((ROWS, SENT, CHAN), BF16),
            jax.ShapeDtypeStruct((KEPT, CHAN), BF16),
        ],
        scratch_shapes=[
            pltpu.VMEM((SHARD, CHAN), BF16),
            pltpu.VMEM((6, 1, 72), jnp.int32),
            pltpu.VMEM((TAPS, 16, CHAN), BF16),
            pltpu.VMEM((SHARD, CHAN), F32),
            pltpu.VMEM((SENT, CHAN), F32),
            pltpu.VMEM((SENT, CHAN), BF16),
            pltpu.VMEM((KEPT, CHAN), BF16),
            pltpu.SemaphoreType.DMA((4 + ROWS,)),
        ],
        compiler_params=compiler_params(60 * 1024 * 1024),
        cost_estimate=pl.CostEstimate(flops=0, bytes_accessed=2 * 9 * SHARD * CHAN, transcendentals=0),
        name="prepare_blocks",
    )(row, features, labels, weights)


def unit(features_ref, j, parity, q):
    pair = features_ref[j, parity, q // 2 * 2 * UNIT : (q // 2 + 1) * 2 * UNIT, :]
    return pair[q % 2 * UNIT : (q % 2 + 1) * UNIT, :]


def forward_kernel(core_ref, features_ref, weights_ref, own_ref, other_ref, acc_ref, flat_ref):
    written = set()
    for j in range(GRID_J):
        for q in range(GRID_Q):
            taps = block_taps(j, q)
            kernels = jnp.concatenate(
                [weights_ref[tap * OUTS : (tap + 1) * OUTS, :] for tap, _, _ in taps], axis=0
            )
            pixels = jnp.concatenate(
                [unit(features_ref, j, 0, q), unit(features_ref, j, 1, q)], axis=0
            )
            product = lax.dot_general(
                kernels, pixels, (((1,), (1,)), ((), ())), preferred_element_type=F32
            )
            for place, (_, branch, block) in enumerate(taps):
                at = (block // 4, branch, slice(block % 4 * OUTS, (block % 4 + 1) * OUTS), slice(2 * UNIT))
                term = product[place * OUTS : (place + 1) * OUTS, :]
                acc_ref[at] = acc_ref[at] + term if (branch, block) in written else term
                written.add((branch, block))
    for group in range(UNITS // 4):
        for branch in range(3):
            turned = jnp.transpose(acc_ref[group, branch])
            for half in range(2):
                flat_ref[half, branch, group * UNIT : (group + 1) * UNIT, :] = turned[
                    half * UNIT : (half + 1) * UNIT, :
                ]
    own = core_ref[0]
    for half, out_ref in ((own, own_ref), (1 - own, other_ref)):
        for part in range(USED):
            for branch in range(3):
                out_ref[part, branch * 16 : (branch + 1) * 16, :] = flat_ref[
                    half, branch, part * 16 : (part + 1) * 16, :
                ].astype(BF16)
        out_ref[USED:] = jnp.zeros((PARTS - USED, SHARE, LANES), BF16)


def forward(core, features, weights):
    whole = pl.BlockSpec(memory_space=pltpu.VMEM)
    return pl.pallas_call(
        forward_kernel,
        in_specs=[pl.BlockSpec(memory_space=pltpu.SMEM), whole, whole],
        out_specs=[whole, whole],
        out_shape=[jax.ShapeDtypeStruct((PARTS, SHARE, LANES), BF16)] * 2,
        scratch_shapes=[
            pltpu.VMEM((UNITS // 4, 3, LANES, 2 * LANES), F32),
            pltpu.VMEM((2, 3, HALF // 4, LANES), F32),
        ],
        compiler_params=compiler_params(),
        cost_estimate=pl.CostEstimate(
            flops=4 * HALF * CHAN * TAPS * OUTS, bytes_accessed=4000000, transcendentals=0
        ),
        name="forward_taps",
    )(core, features, weights)


def sigmoid(values):
    return 1.0 / (1.0 + jnp.exp(-values))


def swish_grad(values, gate_value):
    return gate_value * (1.0 + values * (1.0 - gate_value))


def own_labels(part, marks):
    first = part * 16
    group = first // UNIT
    pixel = lax.broadcasted_iota(jnp.int32, (64, UNITS), 0)
    spot = first - group * UNIT + pixel % 16
    units = (group + jnp.where(spot >= UNIT, 1, 0)) * 4 + pixel // 16
    chosen = (units == lax.broadcasted_iota(jnp.int32, (64, UNITS), 1)).astype(BF16)
    rows = jnp.dot(chosen, marks, preferred_element_type=F32)
    pixel = lax.broadcasted_iota(jnp.int32, (64, UNIT), 0)
    spot = first - group * UNIT + pixel % 16
    spot = jnp.where(spot >= UNIT, spot - UNIT, spot)
    here = lax.broadcasted_iota(jnp.int32, (64, UNIT), 1) == spot
    return jnp.sum(jnp.where(here, rows, 0.0), axis=1, keepdims=True)


def tail_kernel(
    part_ref, parts_ref, proj_ref, classify_ref, classify_t_ref, marks_ref, out_ref, act_ref, packed_ref
):
    pieces = [(row, branch, place) for row in range(ROWS) for branch in range(3) for place in range(4)]

    def packed_at(branch, place):
        return slice(branch * 16, (branch + 1) * 16), slice(place * OUTS, (place + 1) * OUTS)

    def flat_at(row, branch, place):
        start = (row * 3 + branch) * OUTS
        return slice(place * 16, (place + 1) * 16), slice(start, start + OUTS)

    preact, gate = [], []
    for row in range(ROWS):
        total = parts_ref[row].astype(F32)
        for part in range(1, PARTS // ROWS):
            total = total + parts_ref[part * ROWS + row].astype(F32)
        preact.append(total)
        gate.append(sigmoid(total))
        packed_ref[row] = total * gate[row]
    for row, branch, place in pieces:
        at, lanes = packed_at(branch, place)
        act_ref[flat_at(row, branch, place)] = packed_ref[row, at, lanes]
    mixed_pre = jnp.dot(act_ref[...].astype(BF16), proj_ref[...], preferred_element_type=F32)
    mixed_gate = sigmoid(mixed_pre)
    hidden = (mixed_pre * mixed_gate).astype(BF16)
    logits = jnp.dot(hidden, classify_ref[...], preferred_element_type=F32)
    lane = lax.broadcasted_iota(jnp.int32, logits.shape, 1)
    exp_logits = jnp.where(lane < 3, jnp.exp(logits), 0.0)
    probabilities = exp_logits / jnp.sum(exp_logits, axis=1, keepdims=True)
    onehot = jnp.where(lane.astype(F32) == own_labels(part_ref[0], marks_ref[...]), 1.0, 0.0)
    dlogits = (probabilities - onehot).astype(BF16)
    grad_hidden = jnp.dot(dlogits, classify_t_ref[...], preferred_element_type=F32)
    grad_mixed = (grad_hidden * swish_grad(mixed_pre, mixed_gate)).astype(BF16)
    act_ref[...] = lax.dot_general(
        grad_mixed, proj_ref[...], (((1,), (1,)), ((), ())), preferred_element_type=F32
    )
    for row, branch, place in pieces:
        at, lanes = packed_at(branch, place)
        packed_ref[row, at, lanes] = act_ref[flat_at(row, branch, place)]
    for row in range(ROWS):
        block = (packed_ref[row] * swish_grad(preact[row], gate[row])).astype(BF16)
        for part in range(PARTS // ROWS):
            out_ref[part * ROWS + row] = block


def tail(part, parts, proj, classify, classify_t, marks):
    whole = pl.BlockSpec(memory_space=pltpu.VMEM)
    return pl.pallas_call(
        tail_kernel,
        in_specs=[pl.BlockSpec(memory_space=pltpu.SMEM)] + [whole] * 5,
        out_specs=whole,
        out_shape=jax.ShapeDtypeStruct((PARTS, SHARE, LANES), BF16),
        scratch_shapes=[
            pltpu.VMEM((64, ROWS * 3 * OUTS), F32),
            pltpu.VMEM((ROWS, SHARE, LANES), F32),
        ],
        compiler_params=compiler_params(),
        cost_estimate=pl.CostEstimate(
            flops=4 * 64 * 768 * CHAN, bytes_accessed=1500000, transcendentals=64 * 2000
        ),
        name="tail",
    )(part, parts, proj, classify, classify_t, marks)


def gradient_kernel(
    parity_ref, own_ref, other_ref, features_ref, out_ref, flat_ref, turned_ref, acc_ref
):
    own = parity_ref[0]
    flat_ref[:, HALF // 4 :, :] = jnp.zeros((3, LANES - UNIT, LANES), F32)
    for half, grads in enumerate((own_ref, other_ref)):
        for part in range(USED):
            for branch in range(3):
                flat_ref[branch, part * 16 : (part + 1) * 16, :] = grads[
                    part, branch * 16 : (branch + 1) * 16, :
                ].astype(F32)
        for group in range(UNITS // 4):
            for branch in range(3):
                turned = jnp.transpose(flat_ref[branch, group * UNIT : group * UNIT + LANES, :]).astype(BF16)
                for place in range(4):
                    turned_ref[
                        group * 4 + place,
                        branch * OUTS : (branch + 1) * OUTS,
                        half * LANES : (half + 1) * LANES,
                    ] = turned[place * OUTS : (place + 1) * OUTS, :]
    written = set()
    gap = jnp.zeros((LANES - UNIT, CHAN), BF16)
    for j in range(GRID_J):
        for q in range(GRID_Q):
            taps = block_taps(j, q)
            grads = jnp.concatenate(
                [turned_ref[block, branch * OUTS : (branch + 1) * OUTS, :] for _, branch, block in taps],
                axis=0,
            )
            pixels = jnp.concatenate(
                [unit(features_ref, j, own, q), gap, unit(features_ref, j, 1 - own, q), gap], axis=0
            )
            product = jnp.dot(grads, pixels, preferred_element_type=F32)
            for place, (tap, _, _) in enumerate(taps):
                at = slice(tap * OUTS, (tap + 1) * OUTS)
                term = product[place * OUTS : (place + 1) * OUTS, :]
                acc_ref[at, :] = acc_ref[at, :] + term if tap in written else term
                written.add(tap)
    out_ref[...] = acc_ref[...].astype(BF16)


def gradient(parity, own, other, features):
    whole = pl.BlockSpec(memory_space=pltpu.VMEM)
    return pl.pallas_call(
        gradient_kernel,
        in_specs=[pl.BlockSpec(memory_space=pltpu.SMEM), whole, whole, whole],
        out_specs=whole,
        out_shape=jax.ShapeDtypeStruct((TAPS * OUTS, CHAN), BF16),
        scratch_shapes=[
            pltpu.VMEM((3, HALF // 4 + LANES - UNIT, LANES), F32),
            pltpu.VMEM((UNITS, 3 * OUTS, 2 * LANES), BF16),
            pltpu.VMEM((TAPS * OUTS, CHAN), F32),
        ],
        compiler_params=compiler_params(),
        cost_estimate=pl.CostEstimate(
            flops=4 * HALF * CHAN * TAPS * OUTS, bytes_accessed=4000000, transcendentals=0
        ),
        name="gradient_taps",
    )(parity, own, other, features)


def shards(features, weights, proj, classify, labels):
    row = lax.axis_index("row")
    core = lax.axis_index("core")
    part = lax.axis_index("yhi") * ROWS + row
    swap = [(0, 1), (1, 0)]

    sent, mine = prepare(
        row.astype(jnp.int32).reshape(1),
        features.reshape(SHARD, CHAN),
        labels.transpose(1, 0, 2),
        weights.transpose(1, 2, 0, 3).reshape(TAPS, OUTS, CHAN),
    )
    gathered = lax.all_to_all(sent, "row", 0, 0).reshape(GRID_J, 2, SENT, CHAN)
    mine = mine[: 4 * TAPS].reshape(TAPS, 4, CHAN)
    theirs = lax.ppermute(mine, "zlo", swap)
    even = lax.axis_index("zlo") == 0
    pairs = jnp.stack([jnp.where(even, mine, theirs), jnp.where(even, theirs, mine)])
    kernels = lax.all_gather(pairs, "zhi").reshape(8, TAPS, 4, CHAN)
    kernels = kernels.transpose(1, 0, 2, 3).reshape(TAPS * OUTS, CHAN)

    mixing = proj.reshape(3, 8, ROWS, 4, CHAN).transpose(2, 0, 1, 3, 4).reshape(ROWS * 3 * OUTS, CHAN)
    heads = jnp.pad(classify, ((0, 0), (0, LANES - 3)))
    heads_t = jnp.pad(classify.T, ((0, LANES - 3), (0, 0)))
    marks = lax.dynamic_index_in_dim(gathered[:, :, SHARD : SHARD + GRID_Q, :UNIT], core, 1, keepdims=False)
    marks = marks.reshape(UNITS, UNIT)
    part = part.astype(jnp.int32).reshape(1)
    kernels, mixing, heads, heads_t, marks, part = lax.optimization_barrier(
        (kernels, mixing, heads, heads_t, marks, part)
    )

    parity = core.astype(jnp.int32).reshape(1)
    own, other = forward(parity, gathered, kernels)
    received = lax.ppermute(other, "core", swap)
    pair = (own.astype(F32) + received.astype(F32)).astype(BF16)

    parts = lax.all_to_all(pair, ("yhi", "row"), 0, 0)
    grads = tail(part, parts, mixing, heads, heads_t, marks)
    grads_own = lax.all_to_all(grads, ("yhi", "row"), 0, 0)
    grads_other = lax.ppermute(grads_own, "core", swap)
    partial = gradient(parity, grads_own, grads_other, gathered)
    partial = partial.reshape(TAPS, 8, 4, CHAN).transpose(1, 0, 2, 3)
    over_samples = lax.all_to_all(partial, ("zhi", "zlo"), 0, 0)
    summed = jnp.sum(over_samples.astype(F32), axis=0).astype(BF16)
    final = lax.all_to_all(jnp.broadcast_to(summed[None], (ROWS, TAPS, 4, CHAN)), "row", 0, 0)
    return final.transpose(0, 2, 1, 3).reshape(OUTS, 3, 9, CHAN)


def solution(mesh):
    split = Mesh(mesh.devices.reshape(8, 4, 2, 4, 2), ("row", "yhi", "core", "zhi", "zlo"))
    sample, channel = ("zhi", "zlo"), ("yhi", "core")
    in_specs = (
        P(sample, "row", None, channel),
        P(sample, None, None, channel),
        P(),
        P(),
        P(sample, "row", None),
    )
    out_specs = P(sample, None, None, channel)
    return jax.shard_map(shards, mesh=split, in_specs=in_specs, out_specs=out_specs, check_vma=False)
```

```python
import jax
import jax.numpy as jnp
from jax import lax
from jax.experimental import pallas as pl
from jax.experimental.pallas import tpu as pltpu
from jax.sharding import Mesh, PartitionSpec as P

BF16 = jnp.bfloat16
F32 = jnp.float32

ROWS = 8
GRID_J = 4
GRID_Q = 6
UNIT = 72
UNITS = GRID_J * GRID_Q
HALF = UNITS * UNIT
SHARD = 432
SENT = 448
PARTS = 32
USED = 27
SHARE = 48
LANES = 128
CHAN = 256
OUTS = 32
TAPS = 27
KEPT = 112
ROW_AXES = ("row",)
VMEM_LIMIT = 16 * 1024 * 1024


def block_taps(j, q):
    found = []
    for branch in range(3):
        rate = branch + 1
        for tap_row in range(3):
            out_j = j - rate * (tap_row - 1)
            if not 0 <= out_j < GRID_J:
                continue
            for tap_col in range(3):
                out_q = q - rate * (tap_col - 1)
                if not 0 <= out_q < GRID_Q:
                    continue
                found.append((9 * branch + 3 * tap_row + tap_col, branch, out_j * GRID_Q + out_q))
    return found


def compiler_params(limit=VMEM_LIMIT):
    return pltpu.CompilerParams(vmem_limit_bytes=limit)


def prepare_kernel(
    row_ref,
    features_ref,
    labels_ref,
    weights_ref,
    out_ref,
    mine_ref,
    local_ref,
    marks_ref,
    taps_ref,
    rows_ref,
    units_ref,
    block_ref,
    kept_ref,
    sems,
):
    near = weights_ref.at[:, pl.ds(row_ref[0] // 4 * 16, 16), :]
    copies = [
        pltpu.make_async_copy(source, target, sems.at[place])
        for place, (source, target) in enumerate(
            ((features_ref, local_ref), (labels_ref, marks_ref), (near, taps_ref))
        )
    ]
    for copy in (copies[2], copies[0], copies[1]):
        copy.start()
    units_ref[SHARD:, :] = jnp.zeros((SENT - SHARD, CHAN), F32)
    copies[1].wait()
    for row in range(6):
        for q in range(GRID_Q):
            units_ref[SHARD + q : SHARD + q + 1, row * 12 : row * 12 + 12] = marks_ref[
                row, :, q * 12 : q * 12 + 12
            ].astype(F32)
    copies[0].wait()
    rows_ref[...] = local_ref[...].astype(F32)
    for row in range(6):
        for q in range(GRID_Q):
            units_ref[q * UNIT + row * 12 : q * UNIT + row * 12 + 12, :] = rows_ref[
                row * 72 + q * 12 : row * 72 + q * 12 + 12, :
            ]
    block_ref[...] = units_ref[...].astype(BF16)
    sends = [
        pltpu.make_async_copy(block_ref, out_ref.at[device], sems.at[3 + device]) for device in range(ROWS)
    ]
    for send in sends:
        send.start()
    copies[2].wait()
    picked = lax.broadcasted_iota(jnp.int32, (KEPT, 16 * TAPS), 0)
    column = lax.broadcasted_iota(jnp.int32, (KEPT, 16 * TAPS), 1)
    wanted = picked // 4 * 16 + picked % 4 + row_ref[0] % 4 * 4
    picks = jnp.where(column == wanted, 1.0, 0.0).astype(BF16)
    near_rows = taps_ref[...].reshape(16 * TAPS, CHAN)
    kept_ref[...] = jnp.dot(picks, near_rows, preferred_element_type=F32).astype(BF16)
    sends.append(pltpu.make_async_copy(kept_ref, mine_ref, sems.at[3 + ROWS]))
    sends[-1].start()
    for send in sends:
        send.wait()


def prepare(row, features, labels, weights):
    hbm = pl.BlockSpec(memory_space=pl.ANY)
    return pl.pallas_call(
        prepare_kernel,
        in_specs=[pl.BlockSpec(memory_space=pltpu.SMEM), hbm, hbm, hbm],
        out_specs=[hbm, hbm],
        out_shape=[
            jax.ShapeDtypeStruct((ROWS, SENT, CHAN), BF16),
            jax.ShapeDtypeStruct((KEPT, CHAN), BF16),
        ],
        scratch_shapes=[
            pltpu.VMEM((SHARD, CHAN), BF16),
            pltpu.VMEM((6, 1, 72), jnp.int32),
            pltpu.VMEM((TAPS, 16, CHAN), BF16),
            pltpu.VMEM((SHARD, CHAN), F32),
            pltpu.VMEM((SENT, CHAN), F32),
            pltpu.VMEM((SENT, CHAN), BF16),
            pltpu.VMEM((KEPT, CHAN), BF16),
            pltpu.SemaphoreType.DMA((4 + ROWS,)),
        ],
        compiler_params=compiler_params(60 * 1024 * 1024),
        cost_estimate=pl.CostEstimate(flops=0, bytes_accessed=2 * 9 * SHARD * CHAN, transcendentals=0),
        name="prepare_blocks",
    )(row, features, labels, weights)


def unit(features_ref, j, parity, q):
    pair = features_ref[j, parity, q // 2 * 2 * UNIT : (q // 2 + 1) * 2 * UNIT, :]
    return pair[q % 2 * UNIT : (q % 2 + 1) * UNIT, :]


def forward_kernel(core_ref, features_ref, weights_ref, own_ref, other_ref, acc_ref, flat_ref):
    written = set()
    for j in range(GRID_J):
        for q in range(GRID_Q):
            taps = block_taps(j, q)
            kernels = jnp.concatenate(
                [weights_ref[tap * OUTS : (tap + 1) * OUTS, :] for tap, _, _ in taps], axis=0
            )
            pixels = jnp.concatenate(
                [unit(features_ref, j, 0, q), unit(features_ref, j, 1, q)], axis=0
            )
            product = lax.dot_general(
                kernels, pixels, (((1,), (1,)), ((), ())), preferred_element_type=F32
            )
            for place, (_, branch, block) in enumerate(taps):
                at = (block // 4, branch, slice(block % 4 * OUTS, (block % 4 + 1) * OUTS), slice(2 * UNIT))
                term = product[place * OUTS : (place + 1) * OUTS, :]
                acc_ref[at] = acc_ref[at] + term if (branch, block) in written else term
                written.add((branch, block))
    for group in range(UNITS // 4):
        for branch in range(3):
            turned = jnp.transpose(acc_ref[group, branch])
            for half in range(2):
                flat_ref[half, branch, group * UNIT : (group + 1) * UNIT, :] = turned[
                    half * UNIT : (half + 1) * UNIT, :
                ]
    own = core_ref[0]
    for half, out_ref in ((own, own_ref), (1 - own, other_ref)):
        for part in range(USED):
            for branch in range(3):
                out_ref[part, branch * 16 : (branch + 1) * 16, :] = flat_ref[
                    half, branch, part * 16 : (part + 1) * 16, :
                ].astype(BF16)
        out_ref[USED:] = jnp.zeros((PARTS - USED, SHARE, LANES), BF16)


def forward(core, features, weights):
    whole = pl.BlockSpec(memory_space=pltpu.VMEM)
    return pl.pallas_call(
        forward_kernel,
        in_specs=[pl.BlockSpec(memory_space=pltpu.SMEM), whole, whole],
        out_specs=[whole, whole],
        out_shape=[jax.ShapeDtypeStruct((PARTS, SHARE, LANES), BF16)] * 2,
        scratch_shapes=[
            pltpu.VMEM((UNITS // 4, 3, LANES, 2 * LANES), F32),
            pltpu.VMEM((2, 3, HALF // 4, LANES), F32),
        ],
        compiler_params=compiler_params(),
        cost_estimate=pl.CostEstimate(
            flops=4 * HALF * CHAN * TAPS * OUTS, bytes_accessed=4000000, transcendentals=0
        ),
        name="forward_taps",
    )(core, features, weights)


def sigmoid(values):
    return 1.0 / (1.0 + jnp.exp(-values))


def swish_grad(values, gate_value):
    return gate_value * (1.0 + values * (1.0 - gate_value))


def own_labels(part, marks):
    first = part * 16
    group = first // UNIT
    pixel = lax.broadcasted_iota(jnp.int32, (64, UNITS), 0)
    spot = first - group * UNIT + pixel % 16
    units = (group + jnp.where(spot >= UNIT, 1, 0)) * 4 + pixel // 16
    chosen = (units == lax.broadcasted_iota(jnp.int32, (64, UNITS), 1)).astype(BF16)
    rows = jnp.dot(chosen, marks, preferred_element_type=F32)
    pixel = lax.broadcasted_iota(jnp.int32, (64, UNIT), 0)
    spot = first - group * UNIT + pixel % 16
    spot = jnp.where(spot >= UNIT, spot - UNIT, spot)
    here = lax.broadcasted_iota(jnp.int32, (64, UNIT), 1) == spot
    return jnp.sum(jnp.where(here, rows, 0.0), axis=1, keepdims=True)


def tail_kernel(
    part_ref, parts_ref, proj_ref, classify_ref, classify_t_ref, marks_ref, out_ref, act_ref, packed_ref
):
    pieces = [(row, branch, place) for row in range(ROWS) for branch in range(3) for place in range(4)]

    def packed_at(branch, place):
        return slice(branch * 16, (branch + 1) * 16), slice(place * OUTS, (place + 1) * OUTS)

    def flat_at(row, branch, place):
        start = (row * 3 + branch) * OUTS
        return slice(place * 16, (place + 1) * 16), slice(start, start + OUTS)

    preact, gate = [], []
    for row in range(ROWS):
        first = row * (PARTS // ROWS)
        total = parts_ref[first].astype(F32)
        for part in range(1, PARTS // ROWS):
            total = total + parts_ref[first + part].astype(F32)
        preact.append(total)
        gate.append(sigmoid(total))
        packed_ref[row] = total * gate[row]
    for row, branch, place in pieces:
        at, lanes = packed_at(branch, place)
        act_ref[flat_at(row, branch, place)] = packed_ref[row, at, lanes]
    mixed_pre = jnp.dot(act_ref[...].astype(BF16), proj_ref[...], preferred_element_type=F32)
    mixed_gate = sigmoid(mixed_pre)
    hidden = (mixed_pre * mixed_gate).astype(BF16)
    logits = jnp.dot(hidden, classify_ref[...], preferred_element_type=F32)
    lane = lax.broadcasted_iota(jnp.int32, logits.shape, 1)
    exp_logits = jnp.where(lane < 3, jnp.exp(logits), 0.0)
    probabilities = exp_logits / jnp.sum(exp_logits, axis=1, keepdims=True)
    onehot = jnp.where(lane.astype(F32) == own_labels(part_ref[0], marks_ref[...]), 1.0, 0.0)
    dlogits = (probabilities - onehot).astype(BF16)
    grad_hidden = jnp.dot(dlogits, classify_t_ref[...], preferred_element_type=F32)
    grad_mixed = (grad_hidden * swish_grad(mixed_pre, mixed_gate)).astype(BF16)
    act_ref[...] = lax.dot_general(
        grad_mixed, proj_ref[...], (((1,), (1,)), ((), ())), preferred_element_type=F32
    )
    for row, branch, place in pieces:
        at, lanes = packed_at(branch, place)
        packed_ref[row, at, lanes] = act_ref[flat_at(row, branch, place)]
    for row in range(ROWS):
        block = (packed_ref[row] * swish_grad(preact[row], gate[row])).astype(BF16)
        for part in range(PARTS // ROWS):
            out_ref[row * (PARTS // ROWS) + part] = block


def tail(part, parts, proj, classify, classify_t, marks):
    whole = pl.BlockSpec(memory_space=pltpu.VMEM)
    return pl.pallas_call(
        tail_kernel,
        in_specs=[pl.BlockSpec(memory_space=pltpu.SMEM)] + [whole] * 5,
        out_specs=whole,
        out_shape=jax.ShapeDtypeStruct((PARTS, SHARE, LANES), BF16),
        scratch_shapes=[
            pltpu.VMEM((64, ROWS * 3 * OUTS), F32),
            pltpu.VMEM((ROWS, SHARE, LANES), F32),
        ],
        compiler_params=compiler_params(),
        cost_estimate=pl.CostEstimate(
            flops=4 * 64 * 768 * CHAN, bytes_accessed=1500000, transcendentals=64 * 2000
        ),
        name="tail",
    )(part, parts, proj, classify, classify_t, marks)


def gradient_kernel(
    parity_ref, own_ref, other_ref, features_ref, out_ref, flat_ref, turned_ref, acc_ref
):
    own = parity_ref[0]
    flat_ref[:, HALF // 4 :, :] = jnp.zeros((3, LANES - UNIT, LANES), F32)
    for half, grads in enumerate((own_ref, other_ref)):
        for part in range(USED):
            for branch in range(3):
                flat_ref[branch, part * 16 : (part + 1) * 16, :] = grads[
                    part, branch * 16 : (branch + 1) * 16, :
                ].astype(F32)
        for group in range(UNITS // 4):
            for branch in range(3):
                turned = jnp.transpose(flat_ref[branch, group * UNIT : group * UNIT + LANES, :]).astype(BF16)
                for place in range(4):
                    turned_ref[
                        group * 4 + place,
                        branch * OUTS : (branch + 1) * OUTS,
                        half * LANES : (half + 1) * LANES,
                    ] = turned[place * OUTS : (place + 1) * OUTS, :]
    written = set()
    gap = jnp.zeros((LANES - UNIT, CHAN), BF16)
    for j in range(GRID_J):
        for q in range(GRID_Q):
            taps = block_taps(j, q)
            grads = jnp.concatenate(
                [turned_ref[block, branch * OUTS : (branch + 1) * OUTS, :] for _, branch, block in taps],
                axis=0,
            )
            pixels = jnp.concatenate(
                [unit(features_ref, j, own, q), gap, unit(features_ref, j, 1 - own, q), gap], axis=0
            )
            product = jnp.dot(grads, pixels, preferred_element_type=F32)
            for place, (tap, _, _) in enumerate(taps):
                at = slice(tap * OUTS, (tap + 1) * OUTS)
                term = product[place * OUTS : (place + 1) * OUTS, :]
                acc_ref[at, :] = acc_ref[at, :] + term if tap in written else term
                written.add(tap)
    out_ref[...] = acc_ref[...].astype(BF16)


def gradient(parity, own, other, features):
    whole = pl.BlockSpec(memory_space=pltpu.VMEM)
    return pl.pallas_call(
        gradient_kernel,
        in_specs=[pl.BlockSpec(memory_space=pltpu.SMEM), whole, whole, whole],
        out_specs=whole,
        out_shape=jax.ShapeDtypeStruct((TAPS * OUTS, CHAN), BF16),
        scratch_shapes=[
            pltpu.VMEM((3, HALF // 4 + LANES - UNIT, LANES), F32),
            pltpu.VMEM((UNITS, 3 * OUTS, 2 * LANES), BF16),
            pltpu.VMEM((TAPS * OUTS, CHAN), F32),
        ],
        compiler_params=compiler_params(),
        cost_estimate=pl.CostEstimate(
            flops=4 * HALF * CHAN * TAPS * OUTS, bytes_accessed=4000000, transcendentals=0
        ),
        name="gradient_taps",
    )(parity, own, other, features)


def shards(features, weights, proj, classify, labels):
    row = lax.axis_index("row")
    core = lax.axis_index("core")
    part = row * (PARTS // ROWS) + lax.axis_index("yhi")
    swap = [(0, 1), (1, 0)]

    sent, mine = prepare(
        row.astype(jnp.int32).reshape(1),
        features.reshape(SHARD, CHAN),
        labels.transpose(1, 0, 2),
        weights.transpose(1, 2, 0, 3).reshape(TAPS, OUTS, CHAN),
    )
    gathered = lax.all_to_all(sent, "row", 0, 0).reshape(GRID_J, 2, SENT, CHAN)
    mine = mine[: 4 * TAPS].reshape(TAPS, 4, CHAN)
    theirs = lax.ppermute(mine, "zlo", swap)
    even = lax.axis_index("zlo") == 0
    pairs = jnp.stack([jnp.where(even, mine, theirs), jnp.where(even, theirs, mine)])
    kernels = lax.all_gather(pairs, "zhi").reshape(8, TAPS, 4, CHAN)
    kernels = kernels.transpose(1, 0, 2, 3).reshape(TAPS * OUTS, CHAN)

    mixing = proj.reshape(3, 8, ROWS, 4, CHAN).transpose(2, 0, 1, 3, 4).reshape(ROWS * 3 * OUTS, CHAN)
    heads = jnp.pad(classify, ((0, 0), (0, LANES - 3)))
    heads_t = jnp.pad(classify.T, ((0, LANES - 3), (0, 0)))
    marks = lax.dynamic_index_in_dim(gathered[:, :, SHARD : SHARD + GRID_Q, :UNIT], core, 1, keepdims=False)
    marks = marks.reshape(UNITS, UNIT)
    part = part.astype(jnp.int32).reshape(1)
    kernels, mixing, heads, heads_t, marks, part = lax.optimization_barrier(
        (kernels, mixing, heads, heads_t, marks, part)
    )

    parity = core.astype(jnp.int32).reshape(1)
    own, other = forward(parity, gathered, kernels)
    received = lax.ppermute(other, "core", swap)
    pair = (own.astype(F32) + received.astype(F32)).astype(BF16)

    parts = lax.all_to_all(pair, ("row", "yhi"), 0, 0)
    grads = tail(part, parts, mixing, heads, heads_t, marks)
    grads_own = lax.all_to_all(grads, ("row", "yhi"), 0, 0)
    grads_other = lax.ppermute(grads_own, "core", swap)
    partial = gradient(parity, grads_own, grads_other, gathered)
    partial = partial.reshape(TAPS, 8, 4, CHAN).transpose(1, 0, 2, 3)
    over_samples = lax.all_to_all(partial, ("zhi", "zlo"), 0, 0)
    summed = jnp.sum(over_samples.astype(F32), axis=0).astype(BF16)
    final = lax.all_to_all(jnp.broadcast_to(summed[None], (ROWS, TAPS, 4, CHAN)), "row", 0, 0)
    return final.transpose(0, 2, 1, 3).reshape(OUTS, 3, 9, CHAN)


def solution(mesh):
    split = Mesh(mesh.devices.reshape(8, 4, 2, 4, 2), ("row", "yhi", "core", "zhi", "zlo"))
    sample, channel = ("zhi", "zlo"), ("yhi", "core")
    in_specs = (
        P(sample, "row", None, channel),
        P(sample, None, None, channel),
        P(),
        P(),
        P(sample, "row", None),
    )
    out_specs = P(sample, None, None, channel)
    return jax.shard_map(shards, mesh=split, in_specs=in_specs, out_specs=out_specs, check_vma=False)
```

```python
import jax
import jax.numpy as jnp
from jax import lax
from jax.experimental import pallas as pl
from jax.experimental.pallas import tpu as pltpu
from jax.sharding import Mesh, PartitionSpec as P

BF16 = jnp.bfloat16
F32 = jnp.float32

ROWS = 8
GRID_J = 4
GRID_Q = 6
UNIT = 72
UNITS = GRID_J * GRID_Q
HALF = UNITS * UNIT
SHARD = 432
SENT = 448
PARTS = 32
USED = 27
SHARE = 48
LANES = 128
CHAN = 256
OUTS = 32
TAPS = 27
KEPT = 112
ROW_AXES = ("row",)
VMEM_LIMIT = 16 * 1024 * 1024


def block_taps(j, q):
    found = []
    for branch in range(3):
        rate = branch + 1
        for tap_row in range(3):
            out_j = j - rate * (tap_row - 1)
            if not 0 <= out_j < GRID_J:
                continue
            for tap_col in range(3):
                out_q = q - rate * (tap_col - 1)
                if not 0 <= out_q < GRID_Q:
                    continue
                found.append((9 * branch + 3 * tap_row + tap_col, branch, out_j * GRID_Q + out_q))
    return found


def compiler_params(limit=VMEM_LIMIT):
    return pltpu.CompilerParams(vmem_limit_bytes=limit)


def prepare_kernel(
    row_ref,
    features_ref,
    labels_ref,
    weights_ref,
    out_ref,
    mine_ref,
    local_ref,
    marks_ref,
    taps_ref,
    rows_ref,
    units_ref,
    block_ref,
    kept_ref,
    sems,
):
    near = weights_ref.at[:, pl.ds(row_ref[0] // 4 * 16, 16), :]
    copies = [
        pltpu.make_async_copy(source, target, sems.at[place])
        for place, (source, target) in enumerate(
            ((features_ref, local_ref), (labels_ref, marks_ref), (near, taps_ref))
        )
    ]
    for copy in (copies[2], copies[0], copies[1]):
        copy.start()
    units_ref[SHARD:, :] = jnp.zeros((SENT - SHARD, CHAN), F32)
    copies[1].wait()
    for row in range(6):
        for q in range(GRID_Q):
            units_ref[SHARD + q : SHARD + q + 1, row * 12 : row * 12 + 12] = marks_ref[
                row, :, q * 12 : q * 12 + 12
            ].astype(F32)
    copies[0].wait()
    rows_ref[...] = local_ref[...].astype(F32)
    for row in range(6):
        for q in range(GRID_Q):
            units_ref[q * UNIT + row * 12 : q * UNIT + row * 12 + 12, :] = rows_ref[
                row * 72 + q * 12 : row * 72 + q * 12 + 12, :
            ]
    block_ref[...] = units_ref[...].astype(BF16)
    sends = [
        pltpu.make_async_copy(block_ref, out_ref.at[device], sems.at[3 + device]) for device in range(ROWS)
    ]
    for send in sends:
        send.start()
    copies[2].wait()
    picked = lax.broadcasted_iota(jnp.int32, (KEPT, 16 * TAPS), 0)
    column = lax.broadcasted_iota(jnp.int32, (KEPT, 16 * TAPS), 1)
    wanted = picked // 4 * 16 + picked % 4 + row_ref[0] % 4 * 4
    picks = jnp.where(column == wanted, 1.0, 0.0).astype(BF16)
    near_rows = taps_ref[...].reshape(16 * TAPS, CHAN)
    kept_ref[...] = jnp.dot(picks, near_rows, preferred_element_type=F32).astype(BF16)
    sends.append(pltpu.make_async_copy(kept_ref, mine_ref, sems.at[3 + ROWS]))
    sends[-1].start()
    for send in sends:
        send.wait()


def prepare(row, features, labels, weights):
    hbm = pl.BlockSpec(memory_space=pl.ANY)
    return pl.pallas_call(
        prepare_kernel,
        in_specs=[pl.BlockSpec(memory_space=pltpu.SMEM), hbm, hbm, hbm],
        out_specs=[hbm, hbm],
        out_shape=[
            jax.ShapeDtypeStruct((ROWS, SENT, CHAN), BF16),
            jax.ShapeDtypeStruct((KEPT, CHAN), BF16),
        ],
        scratch_shapes=[
            pltpu.VMEM((SHARD, CHAN), BF16),
            pltpu.VMEM((6, 1, 72), jnp.int32),
            pltpu.VMEM((TAPS, 16, CHAN), BF16),
            pltpu.VMEM((SHARD, CHAN), F32),
            pltpu.VMEM((SENT, CHAN), F32),
            pltpu.VMEM((SENT, CHAN), BF16),
            pltpu.VMEM((KEPT, CHAN), BF16),
            pltpu.SemaphoreType.DMA((4 + ROWS,)),
        ],
        compiler_params=compiler_params(60 * 1024 * 1024),
        cost_estimate=pl.CostEstimate(flops=0, bytes_accessed=2 * 9 * SHARD * CHAN, transcendentals=0),
        name="prepare_blocks",
    )(row, features, labels, weights)


def unit(features_ref, j, parity, q):
    pair = features_ref[j, parity, q // 2 * 2 * UNIT : (q // 2 + 1) * 2 * UNIT, :]
    return pair[q % 2 * UNIT : (q % 2 + 1) * UNIT, :]


def forward_kernel(core_ref, features_ref, weights_ref, own_ref, other_ref, acc_ref, flat_ref):
    written = set()
    for j in range(GRID_J):
        for q in range(GRID_Q):
            taps = block_taps(j, q)
            kernels = jnp.concatenate(
                [weights_ref[tap * OUTS : (tap + 1) * OUTS, :] for tap, _, _ in taps], axis=0
            )
            pixels = jnp.concatenate(
                [unit(features_ref, j, 0, q), unit(features_ref, j, 1, q)], axis=0
            )
            product = lax.dot_general(
                kernels, pixels, (((1,), (1,)), ((), ())), preferred_element_type=F32
            )
            for place, (_, branch, block) in enumerate(taps):
                at = (block // 4, branch, slice(block % 4 * OUTS, (block % 4 + 1) * OUTS), slice(2 * UNIT))
                term = product[place * OUTS : (place + 1) * OUTS, :]
                acc_ref[at] = acc_ref[at] + term if (branch, block) in written else term
                written.add((branch, block))
    for group in range(UNITS // 4):
        for branch in range(3):
            turned = jnp.transpose(acc_ref[group, branch])
            for half in range(2):
                flat_ref[half, branch, group * UNIT : (group + 1) * UNIT, :] = turned[
                    half * UNIT : (half + 1) * UNIT, :
                ]
    own = core_ref[0]
    for half, out_ref in ((own, own_ref), (1 - own, other_ref)):
        for part in range(USED):
            for branch in range(3):
                out_ref[part, branch * 16 : (branch + 1) * 16, :] = flat_ref[
                    half, branch, part * 16 : (part + 1) * 16, :
                ].astype(BF16)
        out_ref[USED:] = jnp.zeros((PARTS - USED, SHARE, LANES), BF16)


def forward(core, features, weights):
    whole = pl.BlockSpec(memory_space=pltpu.VMEM)
    return pl.pallas_call(
        forward_kernel,
        in_specs=[pl.BlockSpec(memory_space=pltpu.SMEM), whole, whole],
        out_specs=[whole, whole],
        out_shape=[jax.ShapeDtypeStruct((PARTS, SHARE, LANES), BF16)] * 2,
        scratch_shapes=[
            pltpu.VMEM((UNITS // 4, 3, LANES, 2 * LANES), F32),
            pltpu.VMEM((2, 3, HALF // 4, LANES), F32),
        ],
        compiler_params=compiler_params(),
        cost_estimate=pl.CostEstimate(
            flops=4 * HALF * CHAN * TAPS * OUTS, bytes_accessed=4000000, transcendentals=0
        ),
        name="forward_taps",
    )(core, features, weights)


def sigmoid(values):
    return 1.0 / (1.0 + jnp.exp(-values))


def swish_grad(values, gate_value):
    return gate_value * (1.0 + values * (1.0 - gate_value))


def own_labels(part, marks):
    first = part * 16
    group = first // UNIT
    pixel = lax.broadcasted_iota(jnp.int32, (64, UNITS), 0)
    spot = first - group * UNIT + pixel % 16
    units = (group + jnp.where(spot >= UNIT, 1, 0)) * 4 + pixel // 16
    chosen = (units == lax.broadcasted_iota(jnp.int32, (64, UNITS), 1)).astype(BF16)
    rows = jnp.dot(chosen, marks, preferred_element_type=F32)
    pixel = lax.broadcasted_iota(jnp.int32, (64, UNIT), 0)
    spot = first - group * UNIT + pixel % 16
    spot = jnp.where(spot >= UNIT, spot - UNIT, spot)
    here = lax.broadcasted_iota(jnp.int32, (64, UNIT), 1) == spot
    return jnp.sum(jnp.where(here, rows, 0.0), axis=1, keepdims=True)


def tail_kernel(
    part_ref, parts_ref, proj_ref, classify_ref, classify_t_ref, marks_ref, out_ref, act_ref, packed_ref
):
    pieces = [(row, branch, place) for row in range(ROWS) for branch in range(3) for place in range(4)]

    def packed_at(branch, place):
        return slice(branch * 16, (branch + 1) * 16), slice(place * OUTS, (place + 1) * OUTS)

    def flat_at(row, branch, place):
        start = (row * 3 + branch) * OUTS
        return slice(place * 16, (place + 1) * 16), slice(start, start + OUTS)

    preact, gate = [], []
    for row in range(ROWS):
        total = parts_ref[row].astype(F32)
        for part in range(1, PARTS // ROWS):
            total = total + parts_ref[part * ROWS + row].astype(F32)
        preact.append(total)
        gate.append(sigmoid(total))
        packed_ref[row] = total * gate[row]
    for row, branch, place in pieces:
        at, lanes = packed_at(branch, place)
        act_ref[flat_at(row, branch, place)] = packed_ref[row, at, lanes]
    mixed_pre = jnp.dot(act_ref[...].astype(BF16), proj_ref[...], preferred_element_type=F32)
    mixed_gate = sigmoid(mixed_pre)
    hidden = (mixed_pre * mixed_gate).astype(BF16)
    logits = jnp.dot(hidden, classify_ref[...], preferred_element_type=F32)
    lane = lax.broadcasted_iota(jnp.int32, logits.shape, 1)
    exp_logits = jnp.where(lane < 3, jnp.exp(logits), 0.0)
    probabilities = exp_logits / jnp.sum(exp_logits, axis=1, keepdims=True)
    onehot = jnp.where(lane.astype(F32) == own_labels(part_ref[0], marks_ref[...]), 1.0, 0.0)
    dlogits = (probabilities - onehot).astype(BF16)
    grad_hidden = jnp.dot(dlogits, classify_t_ref[...], preferred_element_type=F32)
    grad_mixed = (grad_hidden * swish_grad(mixed_pre, mixed_gate)).astype(BF16)
    act_ref[...] = lax.dot_general(
        grad_mixed, proj_ref[...], (((1,), (1,)), ((), ())), preferred_element_type=F32
    )
    for row, branch, place in pieces:
        at, lanes = packed_at(branch, place)
        packed_ref[row, at, lanes] = act_ref[flat_at(row, branch, place)]
    for row in range(ROWS):
        block = (packed_ref[row] * swish_grad(preact[row], gate[row])).astype(BF16)
        for part in range(PARTS // ROWS):
            out_ref[part * ROWS + row] = block


def tail(part, parts, proj, classify, classify_t, marks):
    whole = pl.BlockSpec(memory_space=pltpu.VMEM)
    return pl.pallas_call(
        tail_kernel,
        in_specs=[pl.BlockSpec(memory_space=pltpu.SMEM)] + [whole] * 5,
        out_specs=whole,
        out_shape=jax.ShapeDtypeStruct((PARTS, SHARE, LANES), BF16),
        scratch_shapes=[
            pltpu.VMEM((64, ROWS * 3 * OUTS), F32),
            pltpu.VMEM((ROWS, SHARE, LANES), F32),
        ],
        compiler_params=compiler_params(),
        cost_estimate=pl.CostEstimate(
            flops=4 * 64 * 768 * CHAN, bytes_accessed=1500000, transcendentals=64 * 2000
        ),
        name="tail",
    )(part, parts, proj, classify, classify_t, marks)


def gradient_kernel(
    parity_ref, own_ref, other_ref, features_ref, out_ref, flat_ref, turned_ref, acc_ref
):
    own = parity_ref[0]
    flat_ref[:, HALF // 4 :, :] = jnp.zeros((3, LANES - UNIT, LANES), F32)
    for half, grads in enumerate((own_ref, other_ref)):
        for part in range(USED):
            for branch in range(3):
                flat_ref[branch, part * 16 : (part + 1) * 16, :] = grads[
                    part, branch * 16 : (branch + 1) * 16, :
                ].astype(F32)
        for group in range(UNITS // 4):
            for branch in range(3):
                turned = jnp.transpose(flat_ref[branch, group * UNIT : group * UNIT + LANES, :]).astype(BF16)
                for place in range(4):
                    turned_ref[
                        group * 4 + place,
                        branch * OUTS : (branch + 1) * OUTS,
                        half * LANES : (half + 1) * LANES,
                    ] = turned[place * OUTS : (place + 1) * OUTS, :]
    written = set()
    gap = jnp.zeros((LANES - UNIT, CHAN), BF16)
    for j in range(GRID_J):
        for q in range(GRID_Q):
            taps = block_taps(j, q)
            grads = jnp.concatenate(
                [turned_ref[block, branch * OUTS : (branch + 1) * OUTS, :] for _, branch, block in taps],
                axis=0,
            )
            pixels = jnp.concatenate(
                [unit(features_ref, j, own, q), gap, unit(features_ref, j, 1 - own, q), gap], axis=0
            )
            product = jnp.dot(grads, pixels, preferred_element_type=F32)
            for place, (tap, _, _) in enumerate(taps):
                at = slice(tap * OUTS, (tap + 1) * OUTS)
                term = product[place * OUTS : (place + 1) * OUTS, :]
                acc_ref[at, :] = acc_ref[at, :] + term if tap in written else term
                written.add(tap)
    out_ref[...] = acc_ref[...].astype(BF16)


def gradient(parity, own, other, features):
    whole = pl.BlockSpec(memory_space=pltpu.VMEM)
    return pl.pallas_call(
        gradient_kernel,
        in_specs=[pl.BlockSpec(memory_space=pltpu.SMEM), whole, whole, whole],
        out_specs=whole,
        out_shape=jax.ShapeDtypeStruct((TAPS * OUTS, CHAN), BF16),
        scratch_shapes=[
            pltpu.VMEM((3, HALF // 4 + LANES - UNIT, LANES), F32),
            pltpu.VMEM((UNITS, 3 * OUTS, 2 * LANES), BF16),
            pltpu.VMEM((TAPS * OUTS, CHAN), F32),
        ],
        compiler_params=compiler_params(),
        cost_estimate=pl.CostEstimate(
            flops=4 * HALF * CHAN * TAPS * OUTS, bytes_accessed=4000000, transcendentals=0
        ),
        name="gradient_taps",
    )(parity, own, other, features)


def shards(features, weights, proj, classify, labels):
    row = lax.axis_index("row")
    core = lax.axis_index("core")
    part = lax.axis_index("yhi") * ROWS + row
    swap = [(0, 1), (1, 0)]

    sent, mine = prepare(
        row.astype(jnp.int32).reshape(1),
        features.reshape(SHARD, CHAN),
        labels.transpose(1, 0, 2),
        weights.transpose(1, 2, 0, 3).reshape(TAPS, OUTS, CHAN),
    )
    gathered = lax.all_to_all(sent, "row", 0, 0).reshape(GRID_J, 2, SENT, CHAN)
    mine = mine[: 4 * TAPS].reshape(TAPS, 4, CHAN)
    theirs = lax.ppermute(mine, "zlo", swap)
    even = lax.axis_index("zlo") == 0
    pairs = jnp.stack([jnp.where(even, mine, theirs), jnp.where(even, theirs, mine)])
    kernels = lax.all_gather(pairs, "zhi").reshape(8, TAPS, 4, CHAN)
    kernels = kernels.transpose(1, 0, 2, 3).reshape(TAPS * OUTS, CHAN)

    mixing = proj.reshape(3, 8, ROWS, 4, CHAN).transpose(2, 0, 1, 3, 4).reshape(ROWS * 3 * OUTS, CHAN)
    heads = jnp.pad(classify, ((0, 0), (0, LANES - 3)))
    heads_t = jnp.pad(classify.T, ((0, LANES - 3), (0, 0)))
    marks = lax.dynamic_index_in_dim(gathered[:, :, SHARD : SHARD + GRID_Q, :UNIT], core, 1, keepdims=False)
    marks = marks.reshape(UNITS, UNIT)
    part = part.astype(jnp.int32).reshape(1)
    kernels, mixing, heads, heads_t, marks, part = lax.optimization_barrier(
        (kernels, mixing, heads, heads_t, marks, part)
    )

    parity = core.astype(jnp.int32).reshape(1)
    own, other = forward(parity, gathered, kernels)
    received = lax.ppermute(other, "core", swap)
    pair = (own.astype(F32) + received.astype(F32)).astype(BF16)

    parts = lax.all_to_all(pair, ("yhi", "row"), 0, 0)
    grads = tail(part, parts, mixing, heads, heads_t, marks)
    grads_own = lax.all_to_all(grads, ("yhi", "row"), 0, 0)
    grads_other = lax.ppermute(grads_own, "core", swap)
    partial = gradient(parity, grads_own, grads_other, gathered)
    partial = partial.reshape(TAPS, 4, 2, 4, CHAN).transpose(2, 1, 0, 3, 4).reshape(8, TAPS, 4, CHAN)
    over_samples = lax.all_to_all(partial, ("zlo", "zhi"), 0, 0)
    summed = jnp.sum(over_samples.astype(F32), axis=0).astype(BF16)
    final = lax.all_to_all(jnp.broadcast_to(summed[None], (ROWS, TAPS, 4, CHAN)), "row", 0, 0)
    return final.transpose(0, 2, 1, 3).reshape(OUTS, 3, 9, CHAN)


def solution(mesh):
    split = Mesh(mesh.devices.reshape(8, 4, 2, 4, 2), ("row", "yhi", "core", "zhi", "zlo"))
    sample, channel = ("zhi", "zlo"), ("yhi", "core")
    in_specs = (
        P(sample, "row", None, channel),
        P(sample, None, None, channel),
        P(),
        P(),
        P(sample, "row", None),
    )
    out_specs = P(sample, None, None, channel)
    return jax.shard_map(shards, mesh=split, in_specs=in_specs, out_specs=out_specs, check_vma=False)
```

```python
import jax
import jax.numpy as jnp
from jax import lax
from jax.experimental import pallas as pl
from jax.experimental.pallas import tpu as pltpu
from jax.sharding import Mesh, PartitionSpec as P

BF16 = jnp.bfloat16
F32 = jnp.float32

ROWS = 8
GRID_J = 4
GRID_Q = 6
UNIT = 72
UNITS = GRID_J * GRID_Q
HALF = UNITS * UNIT
SHARD = 432
SENT = 448
PARTS = 32
USED = 27
SHARE = 48
LANES = 128
CHAN = 256
OUTS = 32
TAPS = 27
KEPT = 112
ROW_AXES = ("row",)
VMEM_LIMIT = 16 * 1024 * 1024


def block_taps(j, q):
    found = []
    for branch in range(3):
        rate = branch + 1
        for tap_row in range(3):
            out_j = j - rate * (tap_row - 1)
            if not 0 <= out_j < GRID_J:
                continue
            for tap_col in range(3):
                out_q = q - rate * (tap_col - 1)
                if not 0 <= out_q < GRID_Q:
                    continue
                found.append((9 * branch + 3 * tap_row + tap_col, branch, out_j * GRID_Q + out_q))
    return found


def compiler_params(limit=VMEM_LIMIT):
    return pltpu.CompilerParams(vmem_limit_bytes=limit)


def prepare_kernel(
    row_ref,
    features_ref,
    labels_ref,
    weights_ref,
    out_ref,
    mine_ref,
    local_ref,
    marks_ref,
    taps_ref,
    rows_ref,
    units_ref,
    block_ref,
    kept_ref,
    sems,
):
    near = weights_ref.at[:, pl.ds(row_ref[0] // 4 * 16, 16), :]
    copies = [
        pltpu.make_async_copy(source, target, sems.at[place])
        for place, (source, target) in enumerate(
            ((features_ref, local_ref), (labels_ref, marks_ref), (near, taps_ref))
        )
    ]
    for copy in (copies[2], copies[0], copies[1]):
        copy.start()
    units_ref[SHARD:, :] = jnp.zeros((SENT - SHARD, CHAN), F32)
    copies[1].wait()
    for row in range(6):
        for q in range(GRID_Q):
            units_ref[SHARD + q : SHARD + q + 1, row * 12 : row * 12 + 12] = marks_ref[
                row, :, q * 12 : q * 12 + 12
            ].astype(F32)
    copies[0].wait()
    rows_ref[...] = local_ref[...].astype(F32)
    for row in range(6):
        for q in range(GRID_Q):
            units_ref[q * UNIT + row * 12 : q * UNIT + row * 12 + 12, :] = rows_ref[
                row * 72 + q * 12 : row * 72 + q * 12 + 12, :
            ]
    block_ref[...] = units_ref[...].astype(BF16)
    sends = [
        pltpu.make_async_copy(block_ref, out_ref.at[device], sems.at[3 + device]) for device in range(ROWS)
    ]
    for send in sends:
        send.start()
    copies[2].wait()
    picked = lax.broadcasted_iota(jnp.int32, (KEPT, 16 * TAPS), 0)
    column = lax.broadcasted_iota(jnp.int32, (KEPT, 16 * TAPS), 1)
    wanted = picked // 4 * 16 + picked % 4 + row_ref[0] % 4 * 4
    picks = jnp.where(column == wanted, 1.0, 0.0).astype(BF16)
    near_rows = taps_ref[...].reshape(16 * TAPS, CHAN)
    kept_ref[...] = jnp.dot(picks, near_rows, preferred_element_type=F32).astype(BF16)
    sends.append(pltpu.make_async_copy(kept_ref, mine_ref, sems.at[3 + ROWS]))
    sends[-1].start()
    for send in sends:
        send.wait()


def prepare(row, features, labels, weights):
    hbm = pl.BlockSpec(memory_space=pl.ANY)
    return pl.pallas_call(
        prepare_kernel,
        in_specs=[pl.BlockSpec(memory_space=pltpu.SMEM), hbm, hbm, hbm],
        out_specs=[hbm, hbm],
        out_shape=[
            jax.ShapeDtypeStruct((ROWS, SENT, CHAN), BF16),
            jax.ShapeDtypeStruct((KEPT, CHAN), BF16),
        ],
        scratch_shapes=[
            pltpu.VMEM((SHARD, CHAN), BF16),
            pltpu.VMEM((6, 1, 72), jnp.int32),
            pltpu.VMEM((TAPS, 16, CHAN), BF16),
            pltpu.VMEM((SHARD, CHAN), F32),
            pltpu.VMEM((SENT, CHAN), F32),
            pltpu.VMEM((SENT, CHAN), BF16),
            pltpu.VMEM((KEPT, CHAN), BF16),
            pltpu.SemaphoreType.DMA((4 + ROWS,)),
        ],
        compiler_params=compiler_params(60 * 1024 * 1024),
        cost_estimate=pl.CostEstimate(flops=0, bytes_accessed=2 * 9 * SHARD * CHAN, transcendentals=0),
        name="prepare_blocks",
    )(row, features, labels, weights)


def unit(features_ref, j, parity, q):
    pair = features_ref[j, parity, q // 2 * 2 * UNIT : (q // 2 + 1) * 2 * UNIT, :]
    return pair[q % 2 * UNIT : (q % 2 + 1) * UNIT, :]


def forward_kernel(core_ref, features_ref, weights_ref, own_ref, other_ref, acc_ref, flat_ref):
    written = set()
    for j in range(GRID_J):
        for q in range(GRID_Q):
            taps = block_taps(j, q)
            kernels = jnp.concatenate(
                [weights_ref[tap * OUTS : (tap + 1) * OUTS, :] for tap, _, _ in taps], axis=0
            )
            pixels = jnp.concatenate(
                [unit(features_ref, j, 0, q), unit(features_ref, j, 1, q)], axis=0
            )
            product = lax.dot_general(
                kernels, pixels, (((1,), (1,)), ((), ())), preferred_element_type=F32
            )
            for place, (_, branch, block) in enumerate(taps):
                at = (block // 4, branch, slice(block % 4 * OUTS, (block % 4 + 1) * OUTS), slice(2 * UNIT))
                term = product[place * OUTS : (place + 1) * OUTS, :]
                acc_ref[at] = acc_ref[at] + term if (branch, block) in written else term
                written.add((branch, block))
    for group in range(UNITS // 4):
        for branch in range(3):
            turned = jnp.transpose(acc_ref[group, branch])
            for half in range(2):
                flat_ref[half, branch, group * UNIT : (group + 1) * UNIT, :] = turned[
                    half * UNIT : (half + 1) * UNIT, :
                ]
    own = core_ref[0]
    for half, out_ref in ((own, own_ref), (1 - own, other_ref)):
        for part in range(USED):
            for branch in range(3):
                out_ref[part, branch * 16 : (branch + 1) * 16, :] = flat_ref[
                    half, branch, part * 16 : (part + 1) * 16, :
                ].astype(BF16)
        out_ref[USED:] = jnp.zeros((PARTS - USED, SHARE, LANES), BF16)


def forward(core, features, weights):
    whole = pl.BlockSpec(memory_space=pltpu.VMEM)
    return pl.pallas_call(
        forward_kernel,
        in_specs=[pl.BlockSpec(memory_space=pltpu.SMEM), whole, whole],
        out_specs=[whole, whole],
        out_shape=[jax.ShapeDtypeStruct((PARTS, SHARE, LANES), BF16)] * 2,
        scratch_shapes=[
            pltpu.VMEM((UNITS // 4, 3, LANES, 2 * LANES), F32),
            pltpu.VMEM((2, 3, HALF // 4, LANES), F32),
        ],
        compiler_params=compiler_params(),
        cost_estimate=pl.CostEstimate(
            flops=4 * HALF * CHAN * TAPS * OUTS, bytes_accessed=4000000, transcendentals=0
        ),
        name="forward_taps",
    )(core, features, weights)


def sigmoid(values):
    return 1.0 / (1.0 + jnp.exp(-values))


def swish_grad(values, gate_value):
    return gate_value * (1.0 + values * (1.0 - gate_value))


def own_labels(part, marks):
    first = part * 16
    group = first // UNIT
    pixel = lax.broadcasted_iota(jnp.int32, (64, UNITS), 0)
    spot = first - group * UNIT + pixel % 16
    units = (group + jnp.where(spot >= UNIT, 1, 0)) * 4 + pixel // 16
    chosen = (units == lax.broadcasted_iota(jnp.int32, (64, UNITS), 1)).astype(BF16)
    rows = jnp.dot(chosen, marks, preferred_element_type=F32)
    pixel = lax.broadcasted_iota(jnp.int32, (64, UNIT), 0)
    spot = first - group * UNIT + pixel % 16
    spot = jnp.where(spot >= UNIT, spot - UNIT, spot)
    here = lax.broadcasted_iota(jnp.int32, (64, UNIT), 1) == spot
    return jnp.sum(jnp.where(here, rows, 0.0), axis=1, keepdims=True)


def tail_kernel(
    part_ref, parts_ref, proj_ref, classify_ref, classify_t_ref, marks_ref, out_ref, act_ref, packed_ref
):
    pieces = [(row, branch, place) for row in range(ROWS) for branch in range(3) for place in range(4)]

    def packed_at(branch, place):
        return slice(branch * 16, (branch + 1) * 16), slice(place * OUTS, (place + 1) * OUTS)

    def flat_at(row, branch, place):
        start = (row * 3 + branch) * OUTS
        return slice(place * 16, (place + 1) * 16), slice(start, start + OUTS)

    preact, gate = [], []
    for row in range(ROWS):
        total = parts_ref[row].astype(F32)
        for part in range(1, PARTS // ROWS):
            total = total + parts_ref[part * ROWS + row].astype(F32)
        preact.append(total)
        gate.append(sigmoid(total))
        packed_ref[row] = total * gate[row]
    for row, branch, place in pieces:
        at, lanes = packed_at(branch, place)
        act_ref[flat_at(row, branch, place)] = packed_ref[row, at, lanes]
    mixed_pre = jnp.dot(act_ref[...].astype(BF16), proj_ref[...], preferred_element_type=F32)
    mixed_gate = sigmoid(mixed_pre)
    hidden = (mixed_pre * mixed_gate).astype(BF16)
    logits = jnp.dot(hidden, classify_ref[...], preferred_element_type=F32)
    lane = lax.broadcasted_iota(jnp.int32, logits.shape, 1)
    exp_logits = jnp.where(lane < 3, jnp.exp(logits), 0.0)
    probabilities = exp_logits / jnp.sum(exp_logits, axis=1, keepdims=True)
    onehot = jnp.where(lane.astype(F32) == own_labels(part_ref[0], marks_ref[...]), 1.0, 0.0)
    dlogits = (probabilities - onehot).astype(BF16)
    grad_hidden = jnp.dot(dlogits, classify_t_ref[...], preferred_element_type=F32)
    grad_mixed = (grad_hidden * swish_grad(mixed_pre, mixed_gate)).astype(BF16)
    act_ref[...] = lax.dot_general(
        grad_mixed, proj_ref[...], (((1,), (1,)), ((), ())), preferred_element_type=F32
    )
    for row, branch, place in pieces:
        at, lanes = packed_at(branch, place)
        packed_ref[row, at, lanes] = act_ref[flat_at(row, branch, place)]
    for row in range(ROWS):
        block = (packed_ref[row] * swish_grad(preact[row], gate[row])).astype(BF16)
        for part in range(PARTS // ROWS):
            out_ref[part * ROWS + row] = block


def tail(part, parts, proj, classify, classify_t, marks):
    whole = pl.BlockSpec(memory_space=pltpu.VMEM)
    return pl.pallas_call(
        tail_kernel,
        in_specs=[pl.BlockSpec(memory_space=pltpu.SMEM)] + [whole] * 5,
        out_specs=whole,
        out_shape=jax.ShapeDtypeStruct((PARTS, SHARE, LANES), BF16),
        scratch_shapes=[
            pltpu.VMEM((64, ROWS * 3 * OUTS), F32),
            pltpu.VMEM((ROWS, SHARE, LANES), F32),
        ],
        compiler_params=compiler_params(),
        cost_estimate=pl.CostEstimate(
            flops=4 * 64 * 768 * CHAN, bytes_accessed=1500000, transcendentals=64 * 2000
        ),
        name="tail",
    )(part, parts, proj, classify, classify_t, marks)


def gradient_kernel(
    parity_ref, own_ref, other_ref, features_ref, out_ref, flat_ref, turned_ref, acc_ref
):
    own = parity_ref[0]
    flat_ref[:, HALF // 4 :, :] = jnp.zeros((3, LANES - UNIT, LANES), F32)
    for half, grads in enumerate((own_ref, other_ref)):
        for part in range(USED):
            for branch in range(3):
                flat_ref[branch, part * 16 : (part + 1) * 16, :] = grads[
                    part, branch * 16 : (branch + 1) * 16, :
                ].astype(F32)
        for group in range(UNITS // 4):
            for branch in range(3):
                turned = jnp.transpose(flat_ref[branch, group * UNIT : group * UNIT + LANES, :]).astype(BF16)
                for place in range(4):
                    turned_ref[
                        group * 4 + place,
                        branch * OUTS : (branch + 1) * OUTS,
                        half * LANES : (half + 1) * LANES,
                    ] = turned[place * OUTS : (place + 1) * OUTS, :]
    written = set()
    gap = jnp.zeros((LANES - UNIT, CHAN), BF16)
    for j in range(GRID_J):
        for q in range(GRID_Q):
            taps = block_taps(j, q)
            grads = jnp.concatenate(
                [turned_ref[block, branch * OUTS : (branch + 1) * OUTS, :] for _, branch, block in taps],
                axis=0,
            )
            pixels = jnp.concatenate(
                [unit(features_ref, j, own, q), gap, unit(features_ref, j, 1 - own, q), gap], axis=0
            )
            product = jnp.dot(grads, pixels, preferred_element_type=F32)
            for place, (tap, _, _) in enumerate(taps):
                at = slice(tap * OUTS, (tap + 1) * OUTS)
                term = product[place * OUTS : (place + 1) * OUTS, :]
                acc_ref[at, :] = acc_ref[at, :] + term if tap in written else term
                written.add(tap)
    out_ref[...] = acc_ref[...].astype(BF16)


def gradient(parity, own, other, features):
    whole = pl.BlockSpec(memory_space=pltpu.VMEM)
    return pl.pallas_call(
        gradient_kernel,
        in_specs=[pl.BlockSpec(memory_space=pltpu.SMEM), whole, whole, whole],
        out_specs=whole,
        out_shape=jax.ShapeDtypeStruct((TAPS * OUTS, CHAN), BF16),
        scratch_shapes=[
            pltpu.VMEM((3, HALF // 4 + LANES - UNIT, LANES), F32),
            pltpu.VMEM((UNITS, 3 * OUTS, 2 * LANES), BF16),
            pltpu.VMEM((TAPS * OUTS, CHAN), F32),
        ],
        compiler_params=compiler_params(),
        cost_estimate=pl.CostEstimate(
            flops=4 * HALF * CHAN * TAPS * OUTS, bytes_accessed=4000000, transcendentals=0
        ),
        name="gradient_taps",
    )(parity, own, other, features)


def shards(features, weights, proj, classify, labels):
    row = lax.axis_index(("step", "parity"))
    core = lax.axis_index("core")
    part = lax.axis_index("yhi") * ROWS + row
    swap = [(0, 1), (1, 0)]

    sent, mine = prepare(
        row.astype(jnp.int32).reshape(1),
        features.reshape(SHARD, CHAN),
        labels.transpose(1, 0, 2),
        weights.transpose(1, 2, 0, 3).reshape(TAPS, OUTS, CHAN),
    )
    gathered = lax.all_to_all(sent, ("step", "parity"), 0, 0).reshape(GRID_J, 2, SENT, CHAN)
    mine = mine[: 4 * TAPS].reshape(TAPS, 4, CHAN)
    theirs = lax.ppermute(mine, "zlo", swap)
    even = lax.axis_index("zlo") == 0
    pairs = jnp.stack([jnp.where(even, mine, theirs), jnp.where(even, theirs, mine)])
    kernels = lax.all_gather(pairs, "zhi").reshape(8, TAPS, 4, CHAN)
    kernels = kernels.transpose(1, 0, 2, 3).reshape(TAPS * OUTS, CHAN)

    mixing = proj.reshape(3, 8, ROWS, 4, CHAN).transpose(2, 0, 1, 3, 4).reshape(ROWS * 3 * OUTS, CHAN)
    heads = jnp.pad(classify, ((0, 0), (0, LANES - 3)))
    heads_t = jnp.pad(classify.T, ((0, LANES - 3), (0, 0)))
    marks = lax.dynamic_index_in_dim(gathered[:, :, SHARD : SHARD + GRID_Q, :UNIT], core, 1, keepdims=False)
    marks = marks.reshape(UNITS, UNIT)
    part = part.astype(jnp.int32).reshape(1)
    kernels, mixing, heads, heads_t, marks, part = lax.optimization_barrier(
        (kernels, mixing, heads, heads_t, marks, part)
    )

    parity = core.astype(jnp.int32).reshape(1)
    own, other = forward(parity, gathered, kernels)
    received = lax.ppermute(other, "core", swap)
    pair = (own.astype(F32) + received.astype(F32)).astype(BF16)

    parts = lax.all_to_all(pair, ("yhi", "step", "parity"), 0, 0)
    grads = tail(part, parts, mixing, heads, heads_t, marks)
    grads_own = lax.all_to_all(grads, ("yhi", "step", "parity"), 0, 0)
    grads_other = lax.ppermute(grads_own, "core", swap)
    partial = gradient(parity, grads_own, grads_other, gathered)
    partial = partial.reshape(TAPS, 4, 2, 4, CHAN).transpose(2, 1, 0, 3, 4).reshape(8, TAPS, 4, CHAN)
    over_samples = lax.all_to_all(partial, ("zlo", "zhi"), 0, 0)
    summed = jnp.sum(over_samples.astype(F32), axis=0).astype(BF16)
    final = lax.all_to_all(jnp.broadcast_to(summed[None], (ROWS, TAPS, 4, CHAN)), ("parity", "step"), 0, 0)
    final = final.reshape(2, GRID_J, TAPS, 4, CHAN).transpose(1, 0, 3, 2, 4)
    return final.reshape(OUTS, 3, 9, CHAN)


def solution(mesh):
    split = Mesh(mesh.devices.reshape(4, 2, 4, 2, 4, 2), ("step", "parity", "yhi", "core", "zhi", "zlo"))
    sample, channel = ("zhi", "zlo"), ("yhi", "core")
    in_specs = (
        P(sample, ("step", "parity"), None, channel),
        P(sample, None, None, channel),
        P(),
        P(),
        P(sample, ("step", "parity"), None),
    )
    out_specs = P(sample, None, None, channel)
    return jax.shard_map(shards, mesh=split, in_specs=in_specs, out_specs=out_specs, check_vma=False)
```
